32 devices in a mesh: seq: 4 (over y, core), head: 8 (over z, x).
Axes of the slice: x: 2, y: 2, z: 4, core: 2. Of those that a mesh axis runs over, the one named last changes fastest.
Arguments:
- tokens: bfloat16 [8192, 1024], P(('seq', 'head')), may hold values from -6 to 6
- leading_layer_value: bfloat16 [8192, 1024], P(('seq', 'head')), may hold values from -6 to 6
- output_gradient: bfloat16 [8192, 1024], P(('seq', 'head')), may hold values from -6 to 6
- lengths: int32 [4, 4], P('seq'), may hold values from 1 to 1024, 2048 in all within a row
- sequence_block_of: int32 [4, 16], P('seq'), may hold values from 0 to 15, as said below
- stored_block_of: int32 [4, 16], P('seq'), may hold values from 0 to 15, as said below
- channel_settings: bfloat16 [1024, 19], P(('seq', 'head')), may hold values from -6 to 2, as said below
- receptance_matrix: bfloat16 [1024, 1024], P(('seq', 'head')), may hold values from -0.1875 to 0.1875
- key_matrix: bfloat16 [1024, 1024], P(('seq', 'head')), may hold values from -0.1875 to 0.1875
- value_matrix: bfloat16 [1024, 1024], P(('seq', 'head')), may hold values from -0.1875 to 0.1875
- output_matrix: bfloat16 [1024, 1024], P(('seq', 'head')), may hold values from -0.1875 to 0.1875
- branch_down_weight: bfloat16 [1024, 288], P(('seq', 'head')), may hold values from -0.1875 to 0.1875
- branch_up_weight: bfloat16 [1024, 288], P(('seq', 'head')), may hold values from -0.75 to 0.75
- channel_key_weight: bfloat16 [1024, 4096], P(('seq', 'head')), may hold values from -0.1875 to 0.1875
- channel_value_weight: bfloat16 [1024, 4096], P(('seq', 'head')), may hold values from -0.09375 to 0.09375
Outputs:
- layer_out: bfloat16 [8192, 1024], P(('seq', 'head'))
- tokens_grad: float32 [8192, 1024], P(('seq', 'head'))
- first_value_grad: float32 [8192, 1024], P(('seq', 'head'))
- channel_grad: float32 [1024, 19], P(('seq', 'head'))
- recept_grad: float32 [1024, 1024], P('head', 'seq')
- key_grad: float32 [1024, 1024], P('head', 'seq')
- value_grad: float32 [1024, 1024], P('head', 'seq')
- output_grad: float32 [1024, 1024], P('head', 'seq')
- lora_down_grad: float32 [1024, 288], P('head', 'seq')
- lora_up_grad: float32 [1024, 288], P('head', 'seq')
- ffn_key_grad: float32 [1024, 4096], P('head', 'seq')
- ffn_value_grad: float32 [1024, 4096], P('head', 'seq')
The draws below stay inside these ranges and needn't reach their ends.
Inputs may be any that keep to these rules, and one draw needn't show every extreme that they name: Row s lists the lengths of group s's 4 sequences in order; they sum to 2048 and the longest is exactly 1024. `sequence_block_of`: each row is a permutation of 0 to 15. stored_block_of[s, sequence_block_of[s, j]] = j for every s and j. `channel_settings`: Columns: 0, 1 first norm's gain and bias; 2 to 7 token-shift mixes of receptance, decay, key, value, rate, gate; 8 decay base; 9 rate base; 10 value-residual base; 11 key scale; 12 key rate; 13 bonus scale; 14, 15 group norm's gain and bias; 16, 17 second norm's gain and bias; 18 channel-mix token-shift mix.
All inputs are finite; a program needn't handle non-finite values.
Results may differ from the reference program's by a relative error of at most 0.013.
The reference program's roundings to bfloat16 on the way count: a program that leaves them out, or rounds other values in their place, can miss the bound.
Values may be sent and summed in bfloat16 or wider, within the bound.
No kernel may reach another device: no remote copies, remote signals or barrier semaphores. Data moves between devices by JAX's collectives and lax.ppermute only.
A program may use at most 320 MiB of HBM per device.

```python
import math
import jax
import jax.numpy as jnp
import numpy as np
from jax import lax

MODEL_WIDTH = 1024
ATTENTION_SPAN = 64
FF = 4096
DECAY_RANK = 64
DA = 64
DV = 32
NVEC = 19
BLOCK = 128
SEQS = 4
LOW_RANK_TOTAL = 288
GROUPS = 4
GROUP_TOK = 2048
NBG = 16
TOKENS = 8192


def deal_table(key):
    keys = jax.random.split(key, GROUPS)
    return jax.vmap(lambda single: jax.random.permutation(single, NBG))(keys).astype(jnp.int32)


def draw_sequence_block_of(key, part):
    return deal_table(key)


def draw_stored_block_of(key, part):
    table = deal_table(key)
    return jnp.argsort(table, axis=1, stable=True).astype(jnp.int32)


def draw_channel_settings(key, part):
    key = jax.random.fold_in(key, 7)
    lows = jnp.array([0.5, -0.5, 0.0, 0.0, 0.0, 0.0, 0.0, 0.0, -6.0, -1.0, -1.0, 0.5, 0.0, -1.0, 0.5, -0.3, 0.5, -0.3, 0.0], jnp.float32)
    highs = jnp.array([1.5, 0.5, 1.0, 1.0, 1.0, 1.0, 1.0, 1.0, 2.0, 1.0, 1.0, 1.5, 1.0, 1.0, 1.5, 0.3, 1.5, 0.3, 1.0], jnp.float32)
    unit = jax.random.uniform(key, (MODEL_WIDTH, NVEC), jnp.float32)
    return (lows + (highs - lows) * unit).astype(jnp.bfloat16)


def block_levels(rng, extent, pieces, least, high):
    def one(dim, parts):
        steps = jax.random.uniform(jax.random.fold_in(jax.random.fold_in(rng, 6), dim), (parts,), jnp.float32, least / len(pieces), high / len(pieces))
        return jnp.repeat(jnp.exp(steps), extent[dim] // parts).reshape((-1,) + (1,) * (len(extent) - dim - 1))

    factor_of = one(*pieces[0])
    for cut in pieces[1:]:
        factor_of = factor_of * one(*cut)
    return factor_of


def length_profile(count, total, reach, skew):
    loads = [(1 << 20) // math.isqrt(rank ** skew) + 1 for rank in range(2, count + 1)]
    rest, counts = total - reach - (count - 1), [1] * (count - 1)
    while rest > 0:
        candidates = [i for i in range(count - 1) if counts[i] < reach]
        pool, budget = sum([loads[i] for i in candidates]), rest
        for i in candidates:
            addition = min(reach - counts[i], max(1, budget * loads[i] // pool), rest)
            counts[i] = counts[i] + addition
            rest = rest - addition
    return np.array([reach] + counts)


def ragged_sizes(own_key, number_of, total, limit, skew):
    if number_of == 2:
        one = jax.random.randint(own_key, (), max(1, total - limit), min(limit, total - 1) + 1)
        return jnp.stack([one, total - one])
    sizes = jnp.asarray(length_profile(number_of, total, limit, skew), jnp.int32)
    couples = (number_of - 1) // 2
    giver, taker = sizes[1:1 + 2 * couples:2], sizes[2:2 + 2 * couples:2]
    room = jnp.minimum(giver - 1, limit - taker)
    moved = jax.random.randint(jax.random.fold_in(own_key, 1), (couples,), 0, 1 << 20) % (room + 1)
    sizes = sizes.at[1:1 + 2 * couples:2].set(giver - moved).at[2:2 + 2 * couples:2].set(taker + moved)
    return sizes[jax.random.permutation(jax.random.fold_in(own_key, 2), number_of)]


def noise(key, extent, width, limit, shards=(), dtype=jnp.bfloat16):
    values = jax.random.normal(key, extent, jnp.float32) * width
    if len(shards) > 0:
        values = block_levels(key, extent, shards, -0.22, 0.18) * values
    return jnp.clip(values, min=-limit, max=limit).astype(dtype)


def setup_inputs(seed: int = 0) -> dict:
    streams_of = jax.random.split(jax.random.key(seed), 16)
    return {
        "tokens": noise(streams_of[0], (TOKENS, MODEL_WIDTH), 1.0, 6.0, ((0, 32),)),
        "leading_layer_value": noise(streams_of[1], (TOKENS, MODEL_WIDTH), 1.0, 6.0, ((0, 32),)),
        "output_gradient": noise(streams_of[2], (TOKENS, MODEL_WIDTH), 1.0, 6.0, ((0, 32),)),
        "lengths": jax.vmap(lambda own: ragged_sizes(own, SEQS, GROUP_TOK, GROUP_TOK // 2, 2))(jax.random.split(streams_of[3], GROUPS)).reshape((GROUPS, SEQS)).astype(jnp.int32),
        "sequence_block_of": draw_sequence_block_of(jax.random.fold_in(streams_of[15], 71), 0),
        "stored_block_of": draw_stored_block_of(jax.random.fold_in(streams_of[15], 71), 0),
        "channel_settings": draw_channel_settings(jax.random.fold_in(streams_of[15], 71), 0),
        "receptance_matrix": noise(streams_of[7], (MODEL_WIDTH, MODEL_WIDTH), MODEL_WIDTH ** -0.5, 0.1875, ((0, 32),)),
        "key_matrix": noise(streams_of[8], (MODEL_WIDTH, MODEL_WIDTH), MODEL_WIDTH ** -0.5, 0.1875, ((0, 32),)),
        "value_matrix": noise(streams_of[9], (MODEL_WIDTH, MODEL_WIDTH), MODEL_WIDTH ** -0.5, 0.1875, ((0, 32),)),
        "output_matrix": noise(streams_of[10], (MODEL_WIDTH, MODEL_WIDTH), MODEL_WIDTH ** -0.5, 0.1875, ((0, 32),)),
        "branch_down_weight": noise(streams_of[11], (MODEL_WIDTH, LOW_RANK_TOTAL), MODEL_WIDTH ** -0.5, 0.1875, ((0, 32),)),
        "branch_up_weight": noise(streams_of[12], (MODEL_WIDTH, LOW_RANK_TOTAL), DECAY_RANK ** -0.5, 0.75, ((0, 32),)),
        "channel_key_weight": noise(streams_of[13], (MODEL_WIDTH, FF), MODEL_WIDTH ** -0.5, 0.1875, ((0, 32),)),
        "channel_value_weight": noise(streams_of[14], (MODEL_WIDTH, FF), FF ** -0.5, 0.09375, ((0, 32),)),
    }


@jax.custom_vjp
def reduced_rows(v):
    return lax.optimization_barrier(v.astype(jnp.bfloat16)).astype(jnp.float32)

@jax.custom_vjp
def reduced_gradient(v):
    return v

def low_keep(v):
    return (reduced_rows(v), None)

def low_pass(kept, grad):
    return (grad,)

def back_keep(v):
    return (v, None)

def back_low(kept, grad):
    return (reduced_rows(grad),)
reduced_rows.defvjp(low_keep, low_pass)
reduced_gradient.defvjp(back_keep, back_low)
HIGHEST = lax.Precision.HIGHEST

def matrix_product(left, right):
    return jnp.dot(left, right, precision=HIGHEST, preferred_element_type=jnp.float32)

def transposed_product(left, right):
    return lax.dot_general(left, right, (((1,), (1,)), ((), ())), precision=HIGHEST, preferred_element_type=jnp.float32)

def layer_norm(inputs, gain, bias):
    center = inputs - lax.optimization_barrier(jnp.mean(inputs, -1, keepdims=True))
    spread = lax.optimization_barrier(jnp.mean(center * center, -1, keepdims=True))
    return center * lax.rsqrt(spread + 1e-05) * gain + bias

def shifted(inputs, starts):
    moved = jnp.concatenate([jnp.zeros_like(inputs[:1]), inputs[:-1]], 0)
    return moved * (1.0 - starts)[:, None]

def head_inputs(recept_pre, key_pre, value_pre, decay_raised, rate_raised, value_raised, first_vals, column_list):
    log_decay = -jnp.exp(-jax.nn.softplus(-(column_list[:, 8] + decay_raised)) - 0.5)
    learn_rate = jax.nn.sigmoid(column_list[:, 9] + rate_raised)
    element_tally = key_pre.shape[0]
    scaled = (key_pre * column_list[:, 11]).reshape(element_tally, -1, ATTENTION_SPAN)
    key_norm = (scaled * lax.rsqrt(lax.optimization_barrier(jnp.sum(scaled * scaled, -1, keepdims=True)) + 1e-06)).reshape(key_pre.shape)
    main_lookup_vector = key_pre * (1.0 + (learn_rate - 1.0) * column_list[:, 12])
    payload_entries = value_pre + (first_vals - value_pre) * jax.nn.sigmoid(column_list[:, 10] + value_raised)
    return (recept_pre, log_decay, main_lookup_vector, key_norm, learn_rate, payload_entries)

def attention_answer(prefix_recurrence_answer, acceptance_entries, main_lookup_vector, payload_entries, extra_multiplier, cluster_multiplier, cluster_offset_term):
    element_tally = prefix_recurrence_answer.shape[0]
    per_head = prefix_recurrence_answer.reshape(element_tally, -1, ATTENTION_SPAN)
    center = per_head - lax.optimization_barrier(jnp.mean(per_head, -1, keepdims=True))
    spread = lax.optimization_barrier(jnp.mean(center * center, -1, keepdims=True))
    standardized_entries = (center * lax.rsqrt(spread + 0.00064)).reshape(prefix_recurrence_answer.shape) * cluster_multiplier + cluster_offset_term
    extra_shift_term = lax.optimization_barrier(jnp.sum((acceptance_entries * main_lookup_vector * extra_multiplier).reshape(element_tally, -1, ATTENTION_SPAN), -1, keepdims=True))
    return standardized_entries + (extra_shift_term * payload_entries.reshape(element_tally, -1, ATTENTION_SPAN)).reshape(prefix_recurrence_answer.shape)

def token_step(memory, inputs):
    acceptance_entries, log_decay, main_lookup_vector, key_norm, learn_rate, payload_entries, is_start = inputs
    memory = memory * (1.0 - is_start)
    pulled = jnp.einsum('hvk,hk->hv', memory, -key_norm, precision=HIGHEST)
    memory = memory * jnp.exp(log_decay)[:, None, :] + pulled[:, :, None] * (key_norm * learn_rate)[:, None, :] + payload_entries[:, :, None] * main_lookup_vector[:, None, :]
    return (memory, jnp.einsum('hvk,hk->hv', memory, acceptance_entries, precision=HIGHEST))

def block_steps(memory, block):
    return lax.scan(token_step, memory, block)

def delta_scan(acceptance_entries, log_decay, main_lookup_vector, key_norm, learn_rate, payload_entries, starts):
    element_tally = acceptance_entries.shape[0]

    def to_blocks(array):
        return array.reshape(element_tally // BLOCK, BLOCK, -1, ATTENTION_SPAN)
    blocks = tuple((to_blocks(array) for array in (acceptance_entries, log_decay, main_lookup_vector, key_norm, learn_rate, payload_entries)))
    blocks = blocks + (starts.reshape(element_tally // BLOCK, BLOCK),)
    memory = jnp.zeros((acceptance_entries.shape[1] // ATTENTION_SPAN, ATTENTION_SPAN, ATTENTION_SPAN), jnp.float32)
    _, outputs = lax.scan(jax.checkpoint(block_steps), memory, blocks)
    return outputs.reshape(acceptance_entries.shape)

def layer_group(settings, inputs, first_vals, starts):
    column_list, receptance_weight, key_weight_local, value_weight_local, output_weight_local, branch_down_weight, branch_up_weight, channel_key, channel_value = settings
    sliced_decay = DECAY_RANK
    sliced_rate = DECAY_RANK + DA
    sliced_value = DECAY_RANK + DA + DV
    standardized_entries = layer_norm(inputs, column_list[:, 0], column_list[:, 1])
    shift_diff = shifted(standardized_entries, starts) - standardized_entries
    in_recept, decay_input, in_key, value_input, rate_input, gate_input = [reduced_rows(standardized_entries + shift_diff * column_list[:, slot]) for slot in range(2, 8)]
    recept_pre = reduced_gradient(matrix_product(in_recept, receptance_weight))
    key_pre = reduced_gradient(matrix_product(in_key, key_weight_local))
    value_pre = reduced_gradient(matrix_product(value_input, value_weight_local))
    decay_between = reduced_rows(jnp.tanh(reduced_gradient(matrix_product(decay_input, branch_down_weight[:, :sliced_decay]))))
    decay_raised = reduced_gradient(transposed_product(decay_between, branch_up_weight[:, :sliced_decay]))
    rate_between = reduced_rows(reduced_gradient(matrix_product(rate_input, branch_down_weight[:, sliced_decay:sliced_rate])))
    rate_raised = reduced_gradient(transposed_product(rate_between, branch_up_weight[:, sliced_decay:sliced_rate]))
    value_between = reduced_rows(reduced_gradient(matrix_product(value_input, branch_down_weight[:, sliced_rate:sliced_value])))
    value_raised = reduced_gradient(transposed_product(value_between, branch_up_weight[:, sliced_rate:sliced_value]))
    gate_between = reduced_rows(jax.nn.sigmoid(reduced_gradient(matrix_product(gate_input, branch_down_weight[:, sliced_value:]))))
    gate_result = reduced_gradient(transposed_product(gate_between, branch_up_weight[:, sliced_value:]))
    scan_in = head_inputs(recept_pre, key_pre, value_pre, decay_raised, rate_raised, value_raised, first_vals, column_list)
    acceptance_entries, log_decay, main_lookup_vector, key_norm, learn_rate, payload_entries = [reduced_rows(reduced_gradient(array)) for array in scan_in]
    prefix_recurrence_answer = delta_scan(acceptance_entries, log_decay, main_lookup_vector, key_norm, learn_rate, payload_entries, starts)
    joined = reduced_rows(reduced_gradient(attention_answer(prefix_recurrence_answer, acceptance_entries, main_lookup_vector, payload_entries, column_list[:, 13], column_list[:, 14], column_list[:, 15])))
    out_in = reduced_rows(joined * gate_result)
    middle = inputs + reduced_gradient(matrix_product(out_in, output_weight_local))
    mid_normed = layer_norm(middle, column_list[:, 16], column_list[:, 17])
    ffn_in = reduced_rows(mid_normed + (shifted(mid_normed, starts) - mid_normed) * column_list[:, 18])
    ffn_pre = reduced_gradient(matrix_product(ffn_in, channel_key))
    hidden = reduced_rows(jnp.square(jax.nn.relu(ffn_pre)))
    return middle + reduced_gradient(transposed_product(hidden, channel_value))

def reorder(array, table):
    blocks = array.reshape(array.shape[0], table.shape[1], -1, array.shape[-1])
    picked = jnp.take_along_axis(blocks, table.astype(jnp.int32)[:, :, None, None], axis=1)
    return picked.reshape(array.shape)

def reference(tokens, leading_layer_value, output_gradient, lengths, sequence_block_of, stored_block_of, channel_settings, receptance_matrix, key_matrix, value_matrix, output_matrix, branch_down_weight, branch_up_weight, channel_key_weight, channel_value_weight):
    settings = tuple((weight_matrix.astype(jnp.float32) for weight_matrix in (channel_settings, receptance_matrix, key_matrix, value_matrix, output_matrix, branch_down_weight, branch_up_weight, channel_key_weight, channel_value_weight)))
    position = jnp.arange(GROUP_TOK).astype(jnp.int32)
    begins = (jnp.cumsum(lengths, axis=1) - lengths).astype(jnp.int32)
    starts = jnp.any(position[None, :, None] == begins[:, None, :], -1).astype(jnp.float32)
    group_fn = jax.checkpoint(layer_group)

    def forward(weights, inputs, first_vals):
        seq_in = reorder(inputs.reshape(GROUPS, GROUP_TOK, MODEL_WIDTH), stored_block_of)
        seq_first = reorder(first_vals.reshape(GROUPS, GROUP_TOK, MODEL_WIDTH), stored_block_of)

        def step(carry, item):
            return (carry, group_fn(weights, item[0], item[1], item[2]))
        _, outputs = lax.scan(step, None, (seq_in, seq_first, starts))
        return reorder(outputs, sequence_block_of).reshape(inputs.shape)
    result, pullback = jax.vjp(forward, settings, tokens.astype(jnp.float32), leading_layer_value.astype(jnp.float32))
    grad_params, grad_tokens, grad_first = pullback(output_gradient.astype(jnp.float32))
    return (result.astype(jnp.bfloat16), grad_tokens, grad_first, grad_params[0], grad_params[1], grad_params[2], grad_params[3], grad_params[4], grad_params[5], grad_params[6], grad_params[7], grad_params[8])
```

```python
import functools
import jax
import jax.numpy as jnp
from jax import lax
from jax.experimental import pallas as pl
from jax.experimental.pallas import tpu as pltpu
from jax.sharding import Mesh
from jax.sharding import PartitionSpec as P

DECAY_RANK = 64
DA = 64
DV = 32
BLOCK = 128
SPAN = 64
HEAD = 64
FORWARD_CHUNKS = 8
BACKWARD_CHUNKS = 4
LOW = jnp.bfloat16
F32 = jnp.float32
NN = (((1,), (0,)), ((), ()))
NT = (((1,), (1,)), ((), ()))
TN = (((0,), (0,)), ((), ()))
PASSES = {"pair": 3, "inv": 3, "val": 3, "chain": 3, "bpair": 3}


def work(micros):
    return pl.CostEstimate(flops=0, bytes_accessed=int(micros * 3_000), transcendentals=0)


def dot(a, b, dims):
    return lax.dot_general(a, b, dims, preferred_element_type=F32)


def halves(x):
    high = x.astype(LOW)
    return high, (x - high.astype(F32)).astype(LOW)


def product(a, b, dims, passes):
    if passes == 1:
        return dot(a.astype(LOW), b.astype(LOW), dims)
    la, lb = dims[0][0][0], dims[0][1][0]
    a_high, a_low = halves(a)
    if passes == 2:
        b = b.astype(LOW)
        return dot(jnp.concatenate([a_high, a_low], la), jnp.concatenate([b, b], lb), dims)
    b_high, b_low = halves(b)
    first = dot(jnp.concatenate([a_high, a_low], la), jnp.concatenate([b_high, b_high], lb), dims)
    return first + dot(a_high, b_low, dims)


def head_masks(heads):
    lane = lax.broadcasted_iota(jnp.int32, (1, heads * HEAD), 1) // HEAD
    return [(lane == h).astype(F32) for h in range(heads)]


def stacked(x, masks):
    if len(masks) == 1:
        return x
    return jnp.concatenate([x * m for m in masks], 0)


def unstacked(x, heads):
    rows = x.shape[0] // heads
    out = x[:rows]
    for h in range(1, heads):
        out = out + x[h * rows : (h + 1) * rows]
    return out


def head_ones(width):
    row = lax.broadcasted_iota(jnp.int32, (width, width), 0) // HEAD
    col = lax.broadcasted_iota(jnp.int32, (width, width), 1) // HEAD
    return (row == col).astype(LOW)


def head_sum(x, ones):
    high, low = halves(x)
    return dot(jnp.concatenate([high, low], 1), jnp.concatenate([ones, ones], 0), NN)


class Chunk:
    def __init__(self, r, lw, k, kn, a, begins, start, heads):
        self.heads = heads
        masks = head_masks(heads)
        rows = heads * SPAN
        local = [jnp.where(b >= start, b - start, SPAN) for b in begins]
        row_t = lax.broadcasted_iota(jnp.int32, (rows, 1), 0) % SPAN
        col_t = lax.broadcasted_iota(jnp.int32, (1, rows), 1) % SPAN
        row_seg = sum((row_t >= b).astype(jnp.int32) for b in local)
        col_seg = sum((col_t >= b).astype(jnp.int32) for b in local)
        last = sum((b < SPAN).astype(jnp.int32) for b in local)
        same = row_seg == col_seg
        self.strict = same & (row_t > col_t)
        self.upto = same & (row_t >= col_t)
        self.carried = (row_seg == 0).astype(F32)
        self.final = (row_seg == last).astype(F32)
        self.whole = (last == 0).astype(F32)
        tri_r = lax.broadcasted_iota(jnp.int32, (SPAN, SPAN), 0)
        tri_c = lax.broadcasted_iota(jnp.int32, (SPAN, SPAN), 1)
        running = dot((tri_r >= tri_c).astype(LOW), lw, NN)
        lw = lw.astype(F32)
        decay = jnp.exp(running)
        before = jnp.exp(running - lw)
        inverse = jnp.exp(-running)
        end = running[SPAN - 1 : SPAN]
        to_end = jnp.exp(end - running)
        self.end = jnp.exp(end)
        kn = kn.astype(F32)
        beta = kn * a.astype(F32)
        k = k.astype(F32)
        self.decay, self.before, self.inverse, self.to_end = decay, before, inverse, to_end
        self.a_hat = stacked(-kn * before, masks)
        self.r_hat = stacked(r.astype(F32) * decay, masks)
        self.b_hat = stacked(beta * inverse, masks)
        self.k_hat = stacked(k * inverse, masks)
        self.b_end = stacked(beta * to_end, masks) * self.final
        self.k_end = stacked(k * to_end, masks) * self.final


def block_inverses(all_pairs, passes):
    rows = all_pairs[0].shape[0]
    row = lax.broadcasted_iota(jnp.int32, (rows, rows), 0)
    col = lax.broadcasted_iota(jnp.int32, (rows, rows), 1)
    eye = (row == col).astype(F32)

    def products(left, right):
        return [product(a, b, NN, passes) for a, b in zip(left, right)]

    within = row // 8 == col // 8
    small = [jnp.where(within, pairs, 0.0) for pairs in all_pairs]
    square = products(small, small)
    fourth = products(square, square)
    first = [eye + x for x in small]
    inverse = [a + b for a, b in zip(first, products(first, square))]
    inverse = [a + b for a, b in zip(inverse, products(inverse, fourth))]
    size = 8
    while size < SPAN:
        within = (row // (2 * size) == col // (2 * size)) & (row // size != col // size)
        cross = [jnp.where(within, pairs, 0.0) for pairs in all_pairs]
        step = products(products(inverse, cross), inverse)
        inverse = [a + b for a, b in zip(inverse, step)]
        size *= 2
    return inverse


def group_norm_parts(scanned, ones):
    center = scanned - head_sum(scanned, ones) * (1.0 / HEAD)
    spread = head_sum(center * center, ones) * (1.0 / HEAD)
    scale = lax.rsqrt(spread + 0.00064)
    return center * scale, scale


def scan_forward_kernel(
    heads, p, begins_ref, parts_ref, gate_ref, cols_ref,
    out_ref, joined_ref, scanned_ref, state_ref, mats_ref, state,
):
    step = pl.program_id(0)
    width = heads * HEAD

    @pl.when(step == 0)
    def _():
        state[...] = jnp.zeros_like(state)

    begins = [begins_ref[i] for i in range(begins_ref.shape[0])]
    masks = head_masks(heads)
    n = heads * SPAN
    eye = (
        lax.broadcasted_iota(jnp.int32, (width, width), 0)
        == lax.broadcasted_iota(jnp.int32, (width, width), 1)
    ).astype(F32)
    held = []
    for c in range(FORWARD_CHUNKS):
        rows = pl.ds(c * SPAN, SPAN)
        r, lw, k, kn, a, v = [parts_ref[i, rows] for i in range(6)]
        q = Chunk(r, lw, k, kn, a, begins, (step * FORWARD_CHUNKS + c) * SPAN, heads)
        v_st = stacked(v.astype(F32), masks).astype(LOW)
        held.append((q, r, k, v, v_st))
    all_pairs = [
        product(
            jnp.concatenate([q.a_hat, q.r_hat], 0), jnp.concatenate([q.b_hat, q.k_hat], 0), NT, p["pair"]
        )
        for q, *_ in held
    ]
    l_ab = [jnp.where(h[0].strict, x[:n, :n], 0.0) for h, x in zip(held, all_pairs)]
    l_ak = [jnp.where(h[0].strict, x[:n, n:], 0.0) for h, x in zip(held, all_pairs)]
    l_rb = [jnp.where(h[0].upto, x[n:, :n], 0.0) for h, x in zip(held, all_pairs)]
    l_rk = [jnp.where(h[0].upto, x[n:, n:], 0.0) for h, x in zip(held, all_pairs)]
    both_v = [
        product(jnp.concatenate([ak, rk], 0), h[4], NN, 2 if p["val"] == 3 else 1)
        for ak, rk, h in zip(l_ak, l_rk, held)
    ]
    inverses = block_inverses(l_ab, p["inv"])
    solved = [
        product(t, jnp.concatenate([h[0].a_hat * h[0].carried, b[:n]], 1), NN, p["val"])
        for t, h, b in zip(inverses, held, both_v)
    ]
    ends = [product(x, h[0].b_end, TN, p["val"]) for x, h in zip(solved, held)]
    grown = []
    for q, _, _, _, v_st in held:
        if p["val"] == 3:
            k_high, k_low = halves(q.k_end)
            grown.append(dot(jnp.concatenate([v_st, v_st], 0), jnp.concatenate([k_high, k_low], 0), TN))
        else:
            grown.append(dot(v_st, q.k_end.astype(LOW), TN))
    ready = []
    for c in range(FORWARD_CHUNKS):
        q, r, k, v, _ = held[c]
        through = product(l_rb[c], solved[c], NN, p["val"])
        r_thru = q.r_hat * q.carried + through[:, :width]
        o_val = both_v[c][n:] + through[:, width:]
        move = eye * (q.end * q.whole) + ends[c][:width]
        gain = ends[c][width:] + grown[c]
        mats = [
            inverses[c], l_ak[c], l_rb[c], l_rk[c], solved[c][:, :width], solved[c][:, width:], move, r_thru,
        ]
        for i, m in enumerate(mats):
            mats_ref[c, i] = m
        ready.append((move, gain, r_thru, o_val, r, k, v))
    ones = head_ones(width)
    now = state[...]
    begun = []
    for c in range(FORWARD_CHUNKS):
        begun.append(now)
        state_ref[c] = now
        now = product(now, ready[c][0], NN, p["chain"]) + ready[c][1]
    state[...] = now
    for c in range(FORWARD_CHUNKS):
        rows = pl.ds(c * SPAN, SPAN)
        _, _, r_thru, o_val, r, k, v = ready[c]
        scanned = unstacked(o_val + product(r_thru, begun[c], NT, p["val"]), heads)
        scanned_ref[rows] = scanned
        unit, _ = group_norm_parts(scanned, ones)
        bonus = head_sum(r.astype(F32) * k.astype(F32) * cols_ref[0:1], ones)
        joined = unit * cols_ref[1:2] + cols_ref[2:3] + bonus * v.astype(F32)
        joined = joined.astype(LOW)
        joined_ref[rows] = joined
        out_ref[rows] = (joined.astype(F32) * gate_ref[rows]).astype(LOW)


def scan_forward(parts, gate, cols, begins, p):
    _, total, width = parts.shape
    heads = width // HEAD
    rows = FORWARD_CHUNKS * SPAN
    n = heads * SPAN
    spans = total // SPAN
    assert n == width
    row_spec = pl.BlockSpec((rows, width), lambda i, b: (i, 0))
    return pl.pallas_call(
        functools.partial(scan_forward_kernel, heads, p),
        grid_spec=pltpu.PrefetchScalarGridSpec(
            num_scalar_prefetch=1,
            grid=(total // rows,),
            in_specs=[
                pl.BlockSpec((6, rows, width), lambda i, b: (0, i, 0)),
                row_spec,
                pl.BlockSpec(cols.shape, lambda i, b: (0, 0)),
            ],
            out_specs=[
                row_spec,
                row_spec,
                row_spec,
                pl.BlockSpec((FORWARD_CHUNKS, width, width), lambda i, b: (i, 0, 0)),
                pl.BlockSpec((FORWARD_CHUNKS, 8, n, width), lambda i, b: (i, 0, 0, 0)),
            ],
            scratch_shapes=[pltpu.VMEM((width, width), F32)],
        ),
        out_shape=[
            jax.ShapeDtypeStruct((total, width), LOW),
            jax.ShapeDtypeStruct((total, width), LOW),
            jax.ShapeDtypeStruct((total, width), F32),
            jax.ShapeDtypeStruct((spans, width, width), F32),
            jax.ShapeDtypeStruct((spans, 8, n, width), F32),
        ],
        compiler_params=pltpu.CompilerParams(vmem_limit_bytes=48 * 1024 * 1024),
        cost_estimate=work(80),
    )(begins, parts, gate, cols)


def scan_backward_kernel(
    heads, p, home_ref, begins_ref, parts_ref, joined_ref, scanned_ref, gate_ref, grad_a_ref, grad_b_ref,
    pre_ref, first_ref, cols_ref, state_ref, mats_ref, *rest,
):
    steps = pl.num_programs(0)
    step = steps - 1 - pl.program_id(0)
    grads_ref, first_grad_ref, col_grad_ref, state = rest
    width = heads * HEAD
    n = heads * SPAN

    @pl.when(pl.program_id(0) == 0)
    def _():
        state[...] = jnp.zeros_like(state)
        col_grad_ref[...] = jnp.zeros_like(col_grad_ref)

    begins = [begins_ref[i] for i in range(begins_ref.shape[0])]
    masks = head_masks(heads)
    ones = head_ones(width)
    tri_r = lax.broadcasted_iota(jnp.int32, (SPAN, SPAN), 0)
    tri_c = lax.broadcasted_iota(jnp.int32, (SPAN, SPAN), 1)
    later = (tri_c >= tri_r).astype(LOW)
    after = (tri_c > tri_r).astype(LOW)
    sums = [jnp.zeros((1, width), F32) for _ in range(8)]

    def add(slot, value):
        sums[slot] = sums[slot] + jnp.sum(value, 0, keepdims=True)

    c13, c14 = cols_ref[0:1], cols_ref[1:2]
    grads = jnp.concatenate([grad_a_ref[0], grad_b_ref[0]], 0).astype(F32)
    ready = []
    for c in range(BACKWARD_CHUNKS):
        rows = pl.ds(c * SPAN, SPAN)
        r, lw, k, kn, a, v = [parts_ref[i, rows] for i in range(6)]
        q = Chunk(r, lw, k, kn, a, begins, (step * BACKWARD_CHUNKS + c) * SPAN, heads)
        r, k, v = r.astype(F32), k.astype(F32), v.astype(F32)
        unit, scale = group_norm_parts(scanned_ref[rows], ones)
        grad_out = grads[c * SPAN : (c + 1) * SPAN]
        grad_joined = (grad_out * gate_ref[rows]).astype(LOW).astype(F32)
        grad_gate = (grad_out * joined_ref[rows].astype(F32)).astype(LOW)
        add(6, grad_joined * unit)
        add(7, grad_joined)
        grad_unit = grad_joined * c14
        grad_scan = scale * (
            grad_unit
            - head_sum(grad_unit, ones) * (1.0 / HEAD)
            - unit * (head_sum(grad_unit * unit, ones) * (1.0 / HEAD))
        )
        bonus = head_sum(r * k * c13, ones)
        grad_bonus = head_sum(grad_joined * v, ones)
        add(5, grad_bonus * r * k)
        own_r = grad_bonus * k * c13
        own_k = grad_bonus * r * c13
        own_v = grad_joined * bonus
        d_out = stacked(grad_scan, masks)
        flow = product(d_out, mats_ref[c, 7], TN, p["val"])
        ready.append((q, d_out, flow, own_r, own_k, own_v, grad_gate))
    now = state[...]
    ended = [None] * BACKWARD_CHUNKS
    for c in reversed(range(BACKWARD_CHUNKS)):
        ended[c] = now
        now = product(now, mats_ref[c, 6], NT, p["chain"]) + ready[c][2]
    state[...] = now
    span = range(BACKWARD_CHUNKS)
    mats = [[mats_ref[c, i] for i in range(6)] for c in span]
    begin = [state_ref[c] for c in span]
    chunks = [ready[c][0] for c in span]
    d_outs = [ready[c][1] for c in span]
    v_st = [stacked(parts_ref[5, pl.ds(c * SPAN, SPAN)].astype(F32), masks) for c in span]
    update = [mats[c][5] + product(mats[c][4], begin[c], NT, p["val"]) for c in span]
    through = [product(mats[c][2], d_outs[c], TN, p["val"]) for c in span]
    through = [
        through[c] + product(chunks[c].b_end, ended[c], NT, p["val"]) for c in span
    ]
    back = [product(mats[c][0], through[c], TN, p["val"]) for c in span]
    left = [jnp.concatenate([back[c], d_outs[c]], 0) for c in span]
    right = [jnp.concatenate([update[c], v_st[c]], 0) for c in span]
    d_hats = [product(left[c], begin[c], NN, p["val"]) for c in span]
    pair_grads = [product(left[c], right[c], NT, p["bpair"]) for c in span]
    for c in span:
        strict, upto = chunks[c].strict.astype(F32), chunks[c].upto.astype(F32)
        mask = jnp.concatenate(
            [jnp.concatenate([strict, strict], 1), jnp.concatenate([upto, upto], 1)], 0
        )
        pair_grads[c] = pair_grads[c] * mask
    all_asks = []
    for c in span:
        q = chunks[c]
        keys = jnp.concatenate([q.b_hat, q.k_hat], 0)
        carried = jnp.concatenate([q.carried, q.carried], 0)
        all_asks.append(d_hats[c] * carried + product(pair_grads[c], keys, NN, p["bpair"]))
    all_keys = [
        product(
            pair_grads[c], jnp.concatenate([chunks[c].a_hat, chunks[c].r_hat], 0), TN, p["bpair"]
        )
        for c in span
    ]
    all_ends = [product(right[c], ended[c], NN, p["val"]) for c in span]
    all_vals = [
        product(jnp.concatenate([mats[c][1], mats[c][3]], 0), left[c], TN, p["val"]) for c in span
    ]
    all_vals = [
        all_vals[c] + product(chunks[c].k_end, ended[c], NT, p["val"]) for c in span
    ]
    for c in span:
        rows = pl.ds(c * SPAN, SPAN)
        q, _, _, own_r, own_k, own_v, grad_gate = ready[c]
        end_grad, begin_now = ended[c], begin[c]
        r, lw, k, kn, a, v = [parts_ref[i, rows].astype(F32) for i in range(6)]
        d_asks, d_keys, d_val = all_asks[c], all_keys[c], all_vals[c]
        d_ends = all_ends[c] * jnp.concatenate([q.final, q.final], 0)
        d_a, d_r = unstacked(d_asks[:n], heads) * q.before, unstacked(d_asks[n:], heads) * q.decay
        d_b = unstacked(d_keys[:n], heads) * q.inverse
        d_k = unstacked(d_keys[n:], heads) * q.inverse
        e_b = unstacked(d_ends[:n], heads) * q.to_end
        e_k = unstacked(d_ends[n:], heads) * q.to_end
        d_v = unstacked(d_val, heads) + own_v
        beta = kn * a
        end_part = e_b * beta + e_k * k
        here = d_r * r - d_b * beta - d_k * k - end_part
        ahead = -d_a * kn
        at_end = jnp.sum(end_part, 0, keepdims=True) + q.whole * q.end * jnp.sum(
            begin_now * end_grad, 0, keepdims=True
        )
        high, low = halves(here)
        high2, low2 = halves(ahead)
        d_lw = at_end + dot(
            jnp.concatenate([later, later, after, after], 1),
            jnp.concatenate([high, low, high2, low2], 0),
            NN,
        )
        d_b = d_b + e_b
        d_k = d_k + e_k + own_k
        d_r = d_r + own_r
        d_kn = d_b * a - d_a
        d_rate = d_b * kn
        g_r, g_lw, g_k, g_kn, g_a, g_v = [
            x.astype(LOW).astype(F32) for x in (d_r, d_lw, d_k, d_kn, d_rate, d_v)
        ]
        key_pre, value_pre, decay_up, rate_up, value_up = [pre_ref[i, rows] for i in range(5)]
        first = first_ref[rows].astype(F32)
        c8, c9, c10, c11, c12 = [cols_ref[i : i + 1] for i in range(3, 8)]
        sig = jax.nn.sigmoid(c8 + decay_up)
        log_decay = -0.6065306597126334 * sig
        g_decay = g_lw * log_decay * (1.0 - sig)
        add(0, g_decay)
        rate = jax.nn.sigmoid(c9 + rate_up)
        g_rate = (g_a + g_k * key_pre * c12) * rate * (1.0 - rate)
        add(1, g_rate)
        g_key = g_k * (1.0 + (rate - 1.0) * c12)
        add(4, g_k * key_pre * (rate - 1.0))
        scaled = key_pre * c11
        norm = lax.rsqrt(head_sum(scaled * scaled, ones) + 1e-06)
        unit = scaled * norm
        g_scaled = norm * (g_kn - unit * head_sum(g_kn * unit, ones))
        g_key = g_key + g_scaled * c11
        add(3, g_scaled * key_pre)
        mix = jax.nn.sigmoid(c10 + value_up)
        g_value = g_v * (1.0 - mix)
        first_grad_ref[rows] = (g_v * mix).astype(first_grad_ref.dtype)
        g_vup = g_v * (first - value_pre) * mix * (1.0 - mix)
        add(2, g_vup)
        for i, x in enumerate((g_r, g_key, g_value, g_decay, g_rate, g_vup)):
            grads_ref[i, rows] = x.astype(LOW)
        grads_ref[6, rows] = grad_gate
    col_grad_ref[...] += jnp.concatenate(sums, 0)


def scan_backward(parts, joined, scanned, gate, grad, pre, first, cols, states, mats, home, begins, p):
    _, total, width = parts.shape
    heads = width // HEAD
    rows = BACKWARD_CHUNKS * SPAN
    n = heads * SPAN
    steps = total // rows
    row_spec = pl.BlockSpec((rows, width), lambda i, *_: (steps - 1 - i, 0))
    assert rows == 2 * BLOCK

    def stored(which):
        return pl.BlockSpec(
            (1, BLOCK, width), lambda i, home, b: (home[2 * (steps - 1 - i) + which], 0, 0)
        )

    return pl.pallas_call(
        functools.partial(scan_backward_kernel, heads, p),
        grid_spec=pltpu.PrefetchScalarGridSpec(
            num_scalar_prefetch=2,
            grid=(steps,),
            in_specs=[
                pl.BlockSpec((6, rows, width), lambda i, *_: (0, steps - 1 - i, 0)),
                row_spec,
                row_spec,
                row_spec,
                stored(0),
                stored(1),
                pl.BlockSpec((5, rows, width), lambda i, *_: (0, steps - 1 - i, 0)),
                row_spec,
                pl.BlockSpec(cols.shape, lambda i, *_: (0, 0)),
                pl.BlockSpec((BACKWARD_CHUNKS, width, width), lambda i, *_: (steps - 1 - i, 0, 0)),
                pl.BlockSpec((BACKWARD_CHUNKS, 8, n, width), lambda i, *_: (steps - 1 - i, 0, 0, 0)),
            ],
            out_specs=[
                pl.BlockSpec((7, rows, width), lambda i, *_: (0, steps - 1 - i, 0)),
                row_spec,
                pl.BlockSpec((8, width), lambda i, *_: (0, 0)),
            ],
            scratch_shapes=[pltpu.VMEM((width, width), F32)],
        ),
        out_shape=[
            jax.ShapeDtypeStruct((7, total, width), LOW),
            jax.ShapeDtypeStruct((total, width), LOW),
            jax.ShapeDtypeStruct((8, width), F32),
        ],
        compiler_params=pltpu.CompilerParams(vmem_limit_bytes=56 * 1024 * 1024),
        cost_estimate=work(60),
    )(home, begins, parts, joined, scanned, gate, grad, grad, pre, first, cols, states, mats)


def norm_rows(x):
    center = x - jnp.mean(x, -1, keepdims=True)
    scale = lax.rsqrt(jnp.mean(center * center, -1, keepdims=True) + 1e-05)
    return center * scale, scale


def keep_rows(rows, first, begins):
    position = first + lax.broadcasted_iota(jnp.int32, (rows, 1), 0)
    hit = position == begins[0]
    for b in begins[1:]:
        hit = hit | (position == b)
    return 1.0 - hit.astype(F32)


def rows_down(x, edge):
    row = lax.broadcasted_iota(jnp.int32, (x.shape[0], 1), 0)
    return jnp.where(row == 0, edge, pltpu.roll(x, 1, 0))


def rows_up(x, edge):
    row = lax.broadcasted_iota(jnp.int32, (x.shape[0], 1), 0)
    return jnp.where(row == x.shape[0] - 1, edge, pltpu.roll(x, x.shape[0] - 1, 0))


def lane_below(limit):
    return lax.broadcasted_iota(jnp.int32, (1, 128), 1) < limit


def kept(x, mask):
    return jnp.where(mask, x, jnp.zeros_like(x))


class SmallWeights:
    def __init__(self, small, up):
        self.pair, self.gate, self.value = small[:, :128], small[:, 128:256], small[:, 256:384]
        self.up_pair, self.up_gate = up[:, 384:512], up[:, 512:640]
        self.up_value = jnp.concatenate([up[:, 320:352], jnp.zeros((up.shape[0], 96), LOW)], 1)


def project_kernel(
    place_ref, home_ref, begins_ref, xa_ref, xb_ref, fa_ref, fb_ref, cols_ref, own_ref, columns_ref,
    small_ref, up_ref, parts_ref, gate_ref, pre_ref, first_ref, pair_ref, vm_ref, gs_ref, edge,
):
    step = pl.program_id(0)

    @pl.when(step == 0)
    def _():
        edge[...] = jnp.zeros_like(edge)

    begins = [begins_ref[i] for i in range(begins_ref.shape[0])]
    x = jnp.concatenate([xa_ref[0], xb_ref[0]], 0).astype(F32)
    rows = x.shape[0]
    unit, _ = norm_rows(x)
    normed = unit * cols_ref[0:1] + cols_ref[1:2]
    moved = rows_down(normed, edge[0:1]) * keep_rows(rows, step * rows, begins)
    edge[0:1] = normed[rows - 1 : rows]
    diff = moved - normed
    mixed = [(normed + diff * cols_ref[i : i + 1]).astype(LOW) for i in range(2, 8)]
    in_r, in_d, in_k, in_v, in_a, in_g = mixed
    low = SmallWeights(small_ref[...], up_ref[...])
    width = own_ref.shape[1]
    recept = dot(in_r, columns_ref[:, :width], NN)
    key_pre = dot(in_k, columns_ref[:, width : 2 * width], NN)
    values = dot(in_v, jnp.concatenate([columns_ref[:, 2 * width :], low.value], 1), NN)
    value_pre = values[:, :width]
    value_mid = kept(values[:, width:], lane_below(DV)).astype(LOW)
    decay, rate = dot(in_d, low.pair, NN), dot(in_a, low.pair, NN)
    pair = jnp.where(lane_below(DECAY_RANK), jnp.tanh(decay), rate)
    pair_low = pair.astype(LOW)
    gate_sig = jax.nn.sigmoid(dot(in_g, low.gate, NN))
    decay_up = dot(kept(pair_low, lane_below(DECAY_RANK)), low.up_pair, NT)
    rate_up = dot(kept(pair_low, ~lane_below(DECAY_RANK)), low.up_pair, NT)
    value_up = dot(value_mid, low.up_value, NT)
    gate_ref[...] = dot(gate_sig.astype(LOW), low.up_gate, NT)
    pair_ref[...] = pair
    vm_ref[...] = value_mid
    gs_ref[...] = gate_sig
    first_low = jnp.concatenate([fa_ref[0], fb_ref[0]], 0)
    first_ref[...] = first_low
    first = first_low.astype(F32)
    for i, value in enumerate((key_pre, value_pre, decay_up, rate_up, value_up)):
        pre_ref[i] = value
    c8, c9, c10, c11, c12 = [own_ref[i : i + 1] for i in range(3, 8)]
    ones = head_ones(recept.shape[1])
    log_decay = -jnp.exp(-jax.nn.softplus(-(c8 + decay_up)) - 0.5)
    rate = jax.nn.sigmoid(c9 + rate_up)
    scaled = key_pre * c11
    key_norm = scaled * lax.rsqrt(head_sum(scaled * scaled, ones) + 1e-06)
    key_main = key_pre * (1.0 + (rate - 1.0) * c12)
    values = value_pre + (first - value_pre) * jax.nn.sigmoid(c10 + value_up)
    for i, value in enumerate((recept, log_decay, key_main, key_norm, rate, values)):
        parts_ref[i] = value.astype(LOW)


def block_spec(per, which, rows, width, blocks, back, table=0):
    def index(i, *tables):
        step = blocks // 2 - 1 - i if back else i
        stored = tables[table][jnp.maximum(2 * step + which, 0)]
        return (stored // per, (stored % per) * (BLOCK // rows) + BLOCK // rows - 1, 0)

    return pl.BlockSpec((1, rows, width), index)


def whole_spec(array):
    return pl.BlockSpec(array.shape, lambda i, *_: (0,) * array.ndim)


def project(x, first, cols, own, weights, place, home, begins, per):
    blocks = home.shape[0]
    total = blocks * BLOCK
    rows = 2 * BLOCK
    width = own.shape[1]
    span = lambda w: pl.BlockSpec((rows, w), lambda i, *_: (i, 0))
    deep = lambda n: pl.BlockSpec((n, rows, width), lambda i, *_: (0, i, 0))
    shape = jax.ShapeDtypeStruct
    return pl.pallas_call(
        project_kernel,
        grid_spec=pltpu.PrefetchScalarGridSpec(
            num_scalar_prefetch=3,
            grid=(blocks // 2,),
            in_specs=[
                block_spec(per, 0, BLOCK, x.shape[2], blocks, False),
                block_spec(per, 1, BLOCK, x.shape[2], blocks, False),
                block_spec(per, 0, BLOCK, width, blocks, False, 1),
                block_spec(per, 1, BLOCK, width, blocks, False, 1),
                whole_spec(cols),
                whole_spec(own),
            ]
            + [whole_spec(w) for w in weights],
            out_specs=[deep(6), span(width), deep(5), span(width), span(128), span(128), span(128)],
            scratch_shapes=[pltpu.VMEM((8, x.shape[2]), F32)],
        ),
        out_shape=[
            shape((6, total, width), LOW),
            shape((total, width), F32),
            shape((5, total, width), F32),
            shape((total, width), LOW),
            shape((total, 128), F32),
            shape((total, 128), LOW),
            shape((total, 128), F32),
        ],
        compiler_params=pltpu.CompilerParams(vmem_limit_bytes=56 * 1024 * 1024),
        cost_estimate=work(20),
    )(place, home, begins, x, x, first, first, cols, own, *weights)


def project_back_kernel(
    place_ref, begins_ref, xa_ref, xb_ref, xp_ref, grads_ref, pair_ref, vm_ref, gs_ref, cols_ref,
    columns_ref, small_ref, up_ref, back_ref, sum_ref, up_sum_ref, edge,
):
    step = pl.num_programs(0) - 1 - pl.program_id(0)

    @pl.when(pl.program_id(0) == 0)
    def _():
        for ref in (edge, sum_ref, up_sum_ref):
            ref[...] = jnp.zeros_like(ref)

    begins = [begins_ref[i] for i in range(begins_ref.shape[0])]
    x = jnp.concatenate([xa_ref[0], xb_ref[0]], 0).astype(F32)
    rows = x.shape[0]
    unit, _ = norm_rows(x)
    normed = unit * cols_ref[0:1] + cols_ref[1:2]
    prior_unit, _ = norm_rows(xp_ref[0].astype(F32))
    prior = prior_unit * cols_ref[0:1] + cols_ref[1:2]
    keep = keep_rows(rows, step * rows, begins)
    diff = rows_down(normed, prior[prior.shape[0] - 1 :]) * keep - normed
    low = SmallWeights(small_ref[...], up_ref[...])
    width = grads_ref.shape[2]
    g_r, g_k, g_v, g_decay, g_rate, g_vup, g_gate = [grads_ref[i] for i in range(7)]
    pair, sig = pair_ref[...], gs_ref[...]
    pair_low = pair.astype(LOW)
    is_decay = lane_below(DECAY_RANK)
    m_pair = jnp.where(
        is_decay, dot(g_decay, low.up_pair, NN) * (1.0 - pair * pair), dot(g_rate, low.up_pair, NN)
    ).astype(LOW)
    m_v = kept(dot(g_vup, low.up_value, NN), lane_below(DV)).astype(LOW)
    m_g = (dot(g_gate, low.up_gate, NN) * sig * (1.0 - sig)).astype(LOW)
    near = jnp.zeros_like(x)
    far = jnp.zeros_like(x)
    value_weights = jnp.concatenate([columns_ref[:, 2 * width :], low.value], 1)
    cut = DECAY_RANK + DA + 3 * width
    grads = (
        (2, g_r, columns_ref[:, :width], ((0, g_r),)),
        (3, kept(m_pair, is_decay), low.pair, ((3 * width, m_pair[:, :DECAY_RANK]),)),
        (4, g_k, columns_ref[:, width : 2 * width], ((width, g_k),)),
        (5, jnp.concatenate([g_v, m_v], 1), value_weights, ((2 * width, g_v), (cut, m_v[:, :DV]))),
        (6, kept(m_pair, ~is_decay), low.pair, ((3 * width + DECAY_RANK, m_pair[:, DECAY_RANK:]),)),
        (7, m_g, low.gate, ((cut + DV, m_g),)),
    )
    col_sums = []
    for slot, grad, weight, parts in grads:
        mix = cols_ref[slot : slot + 1]
        mixed = (normed + diff * mix).astype(LOW)
        total = dot(grad, weight, NT)
        for start, part in parts:
            sum_ref[start : start + part.shape[1]] += dot(part, mixed, TN)
        near = near + total
        far = far + total * mix
        col_sums.append(jnp.sum(total * diff, 0, keepdims=True))
    start = 0
    for mid, grad in (
        (pair_low[:, :DECAY_RANK], g_decay),
        (pair_low[:, DECAY_RANK:], g_rate),
        (vm_ref[:, :DV], g_vup),
        (sig.astype(LOW), g_gate),
    ):
        up_sum_ref[start : start + mid.shape[1]] += dot(mid, grad, TN)
        start += mid.shape[1]
    moved = far * keep
    back = near - far + rows_up(moved, edge[0:1])
    edge[0:1] = moved[0:1]
    back_ref[...] = back.astype(LOW)
    first = [jnp.sum(back * unit, 0, keepdims=True), jnp.sum(back, 0, keepdims=True)]
    sum_ref[sum_ref.shape[0] - 8 :] += jnp.concatenate(first + col_sums, 0)


def project_back(x, grads, mids, cols, weights, place, begins, per):
    blocks = place.shape[0]
    total = blocks * BLOCK
    rows = 2 * BLOCK
    steps = blocks // 2
    wide = x.shape[2]
    width = grads.shape[2]
    low_rank = DECAY_RANK + DA + DV + 128
    span = lambda w: pl.BlockSpec((rows, w), lambda i, *_: (steps - 1 - i, 0))
    shape = jax.ShapeDtypeStruct
    sums = [shape((3 * width + low_rank + 8, wide), F32), shape((low_rank, width), F32)]
    return pl.pallas_call(
        project_back_kernel,
        grid_spec=pltpu.PrefetchScalarGridSpec(
            num_scalar_prefetch=2,
            grid=(steps,),
            in_specs=[
                block_spec(per, 0, BLOCK, wide, blocks, True),
                block_spec(per, 1, BLOCK, wide, blocks, True),
                block_spec(per, -1, 16, wide, blocks, True),
                pl.BlockSpec((7, rows, width), lambda i, *_: (0, steps - 1 - i, 0)),
            ]
            + [span(m.shape[1]) for m in mids]
            + [whole_spec(cols)]
            + [whole_spec(w) for w in weights],
            out_specs=[span(wide)] + [whole_spec(s) for s in sums],
            scratch_shapes=[pltpu.VMEM((8, wide), F32)],
        ),
        out_shape=[shape((total, wide), LOW)] + sums,
        compiler_params=pltpu.CompilerParams(vmem_limit_bytes=56 * 1024 * 1024),
        cost_estimate=work(34),
    )(place, begins, x, x, x, grads, *mids, cols, *weights)


TALL = BLOCK + 16


def block_keeps(local_ref, begins_ref, j):
    begins = [begins_ref[i] for i in range(begins_ref.shape[0])]
    first = local_ref[j] * BLOCK
    after = jnp.float32(1.0)
    for b in begins:
        after = jnp.where(first + BLOCK == b, 0.0, after)
    return keep_rows(BLOCK, first, begins), after


def middle_kernel(
    per, local_ref, begins_ref, out_ref, tokens_ref, weight_ref, cols_ref, middle_ref, ffn_ref, rows_ref
):
    heads = out_ref.shape[0]
    rows = [jnp.concatenate([out_ref[h, j] for h in range(heads)], 1) for j in range(per)]
    rows = jnp.concatenate(rows, 0)
    rows_ref[...] = rows
    middle = tokens_ref[...].astype(F32) + dot(rows, weight_ref[...], NN)
    middle_ref[...] = middle
    unit, _ = norm_rows(middle)
    normed = unit * cols_ref[16:17] + cols_ref[17:18]
    c18 = cols_ref[18:19]
    extra_row = lax.broadcasted_iota(jnp.int32, (TALL - BLOCK, 1), 0)
    for j in range(per):
        main = normed[j * TALL : j * TALL + BLOCK]
        extra = normed[j * TALL + BLOCK : (j + 1) * TALL]
        keep, keep_after = block_keeps(local_ref, begins_ref, j)
        moved = rows_down(main, extra[0:1]) * keep
        ffn_ref[j * TALL : j * TALL + BLOCK] = (main + (moved - main) * c18).astype(LOW)
        after = extra + (main[BLOCK - 1 :] * keep_after - extra) * c18
        ffn_ref[j * TALL + BLOCK : (j + 1) * TALL] = jnp.where(extra_row == 1, after, 0.0).astype(LOW)


def middle_rows(out, tokens_ext, weight, cols, local, begins):
    _, per, _, _ = out.shape
    wide = weight.shape[0]
    shape = jax.ShapeDtypeStruct
    return pl.pallas_call(
        functools.partial(middle_kernel, per),
        grid_spec=pltpu.PrefetchScalarGridSpec(
            num_scalar_prefetch=2,
            grid=(1,),
            in_specs=[whole_spec(x) for x in (out, tokens_ext, weight, cols)],
            out_specs=[whole_spec(tokens_ext)] * 3,
        ),
        out_shape=[
            shape((per * TALL, wide), F32),
            shape((per * TALL, wide), LOW),
            shape((per * TALL, wide), LOW),
        ],
        compiler_params=pltpu.CompilerParams(vmem_limit_bytes=48 * 1024 * 1024),
        cost_estimate=work(6),
    )(local, begins, out, tokens_ext, weight, cols)


def with_extra(main, extra):
    per = main.shape[0] // BLOCK
    pieces = []
    for j in range(per):
        pieces += [main[j * BLOCK : (j + 1) * BLOCK], extra[j * 16 : (j + 1) * 16]]
    return pieces


def channel_kernel(
    xa_ref, xb_ref, ga_ref, gb_ref, ea_ref, eb_ref, key_ref, value_ref, hidden_ref, pre_ref, a_ref, b_ref
):
    rows = xa_ref.shape[0]
    x = jnp.concatenate([xa_ref[...], xb_ref[...]], 0)
    g = jnp.concatenate(with_extra(ga_ref, ea_ref) + with_extra(gb_ref, eb_ref), 0)
    key, value = key_ref[...], value_ref[...]
    active = jnp.maximum(dot(x, key, NN), 0.0)
    hidden_ref[...] = (active * active).astype(LOW)
    grad = (dot(g, value, NN) * 2.0 * active).astype(LOW)
    pre_ref[...] = grad
    back = dot(grad, key, NT)

    @pl.when(pl.program_id(0) == 0)
    def _():
        a_ref[...] = back[:rows]
        b_ref[...] = back[rows:]

    @pl.when(pl.program_id(0) > 0)
    def _():
        a_ref[...] += back[:rows]
        b_ref[...] += back[rows:]


def channel_mix(x, g, extra, key, value):
    rows, wide = x[0].shape
    columns = key.shape[1]
    part = columns // 4
    piece = pl.BlockSpec((2 * rows, part), lambda i: (0, i))
    shape = jax.ShapeDtypeStruct
    return pl.pallas_call(
        channel_kernel,
        grid=(4,),
        in_specs=[whole_spec(a) for a in (*x, *g, *extra)]
        + [pl.BlockSpec((wide, part), lambda i: (0, i))] * 2,
        out_specs=[piece, piece, whole_spec(x[0]), whole_spec(x[0])],
        out_shape=[
            shape((2 * rows, columns), LOW),
            shape((2 * rows, columns), LOW),
            shape((rows, wide), F32),
            shape((rows, wide), F32),
        ],
        compiler_params=pltpu.CompilerParams(vmem_limit_bytes=48 * 1024 * 1024),
        cost_estimate=work(8),
    )(*x, *g, *extra, key, value)


def main_rows(refs):
    pieces = []
    for ref in refs:
        for start in range(0, ref.shape[0], TALL):
            pieces.append(ref[start : start + BLOCK])
    return jnp.concatenate(pieces, 0)


def channel_grad_kernel(count, *refs):
    og, x = jnp.concatenate([r[...] for r in refs[:count]], 0), main_rows(refs[count : 2 * count])
    hidden, pre = main_rows(refs[2 * count : 2 * count + 2]), main_rows(refs[2 * count + 2 : 2 * count + 4])
    out = refs[2 * count + 4]
    columns = hidden.shape[1]
    out[:, :columns] = dot(og, hidden, TN).astype(LOW)
    out[:, columns : 2 * columns] = dot(x, pre, TN).astype(LOW)


def channel_grads(og, x, hidden, pre, extra):
    wide = og[0].shape[1]
    part = 256
    columns = hidden[0].shape[1]
    return pl.pallas_call(
        functools.partial(channel_grad_kernel, len(og)),
        grid=(wide // part,),
        in_specs=[pl.BlockSpec((a.shape[0], part), lambda i: (0, i)) for a in (*og, *x)]
        + [whole_spec(h) for h in (*hidden, *pre)],
        out_specs=pl.BlockSpec((part, 2 * columns + extra), lambda i: (i, 0)),
        out_shape=jax.ShapeDtypeStruct((wide, 2 * columns + extra), LOW),
        compiler_params=pltpu.CompilerParams(vmem_limit_bytes=48 * 1024 * 1024),
        cost_estimate=work(9),
    )(*og, *x, *hidden, *pre)


def output_grad_kernel(count, which_ref, *refs):
    rows, grads, out = refs[:count], refs[count : 2 * count], refs[-1]
    left = jnp.concatenate([r[...] for r in rows], 0)
    right = jnp.concatenate([r[...] for r in grads], 0)
    out[...] = dot(left, right, TN).astype(LOW)


def output_grads(rows, grads, which, room):
    tall, wide = rows[0].shape
    part = 256
    last = room.shape[1] // part - 1
    return pl.pallas_call(
        functools.partial(output_grad_kernel, len(rows)),
        grid_spec=pltpu.PrefetchScalarGridSpec(
            num_scalar_prefetch=1,
            grid=(wide // part,),
            in_specs=[pl.BlockSpec((tall, part), lambda i, w: (0, i))] * len(rows)
            + [pl.BlockSpec((tall, part), lambda i, w: (0, w[0]))] * len(grads)
            + [pl.BlockSpec(memory_space=pl.ANY)],
            out_specs=pl.BlockSpec((part, part), lambda i, w: (i, last)),
        ),
        out_shape=jax.ShapeDtypeStruct(room.shape, LOW),
        input_output_aliases={2 * len(rows) + 1: 0},
        compiler_params=pltpu.CompilerParams(vmem_limit_bytes=48 * 1024 * 1024),
        cost_estimate=work(2),
    )(which, *rows, *grads, room)


def middle_back_kernel(
    per, local_ref, begins_ref, near_ref, core_ref, far_ref, middle_ref, og_ref, weight_ref, cols_ref,
    grad_ref, low_ref, heads_ref, sums_ref,
):
    c16, c17, c18 = [cols_ref[i : i + 1] for i in (16, 17, 18)]
    grad_in = near_ref[...] + core_ref[...] + far_ref[...].astype(F32)
    sums = [jnp.zeros((1, c16.shape[1]), F32) for _ in range(3)]
    lows = []
    for j in range(per):
        start = j * TALL
        grad, after = grad_in[start : start + BLOCK], grad_in[start + BLOCK + 1 : start + BLOCK + 2]
        keep, keep_after = block_keeps(local_ref, begins_ref, j)
        ahead = rows_up(grad * keep, after * keep_after)
        grad_normed = grad + (ahead - grad) * c18
        unit, scale = norm_rows(middle_ref[start : start + BLOCK])
        prior, _ = norm_rows(middle_ref[start + BLOCK : start + TALL])
        normed = unit * c16 + c17
        diff = rows_down(normed, prior[0:1] * c16 + c17) * keep - normed
        for i, value in enumerate((grad_normed * unit, grad_normed, grad * diff)):
            sums[i] = sums[i] + jnp.sum(value, 0, keepdims=True)
        og = og_ref[j * BLOCK : (j + 1) * BLOCK].astype(F32)
        total = og + norm_back(grad_normed, unit, scale, c16)
        grad_ref[j * BLOCK : (j + 1) * BLOCK] = total
        lows.append(total.astype(LOW))
        low_ref[start : start + BLOCK] = lows[-1]
        low_ref[start + BLOCK : start + TALL] = jnp.zeros((TALL - BLOCK, c16.shape[1]), LOW)
    sums_ref[...] = jnp.concatenate(sums + [jnp.zeros((5, c16.shape[1]), F32)], 0)
    out = dot(jnp.concatenate(lows, 0), weight_ref[...], NT).astype(LOW)
    width = heads_ref.shape[2]
    for h in range(heads_ref.shape[0]):
        heads_ref[h] = out[:, h * width : (h + 1) * width]


def norm_back(grad, unit, scale, gain):
    grad = grad * gain
    return scale * (
        grad - jnp.mean(grad, -1, keepdims=True) - unit * jnp.mean(grad * unit, -1, keepdims=True)
    )


def middle_back(near, core, far, middle, og, weight, cols, local, begins, heads):
    tall, wide = near.shape
    per = tall // TALL
    shape = jax.ShapeDtypeStruct
    outs = [
        shape((per * BLOCK, wide), F32),
        shape((tall, wide), LOW),
        shape((heads, per * BLOCK, wide // heads), LOW),
        shape((8, wide), F32),
    ]
    operands = (near, core, far, middle, og, weight, cols)
    return pl.pallas_call(
        functools.partial(middle_back_kernel, per),
        grid_spec=pltpu.PrefetchScalarGridSpec(
            num_scalar_prefetch=2,
            grid=(1,),
            in_specs=[whole_spec(x) for x in operands],
            out_specs=[whole_spec(x) for x in outs],
        ),
        out_shape=outs,
        compiler_params=pltpu.CompilerParams(vmem_limit_bytes=48 * 1024 * 1024),
        cost_estimate=work(8),
    )(local, begins, *operands)


HEAD_AXES = ("hz", "hx")


def all_gather(x, axes):
    return lax.all_gather(x, axes, axis=0, tiled=True)


def steps_along(x, axis):
    size = lax.axis_size(axis)
    return [lax.ppermute(x, axis, [(i, i ^ k) for i in range(size)]) for k in range(1, size)]


def grown(x, axis):
    return jnp.concatenate([x] + steps_along(x, axis), 0)


def in_order(x, axes):
    strides, stride = {}, 1
    for axis in axes:
        strides[axis] = stride
        stride *= lax.axis_size(axis)
    index = jnp.arange(stride, dtype=jnp.int32)
    place, below = jnp.zeros((), jnp.int32), stride
    for axis in ("ys", "core") + HEAD_AXES:
        if axis in axes:
            below //= lax.axis_size(axis)
            there = (index // below) % lax.axis_size(axis)
            place = place + (there ^ lax.axis_index(axis)) * strides[axis]
    x = taken_blocks(x, place)
    return x.reshape((x.shape[0] * x.shape[1],) + x.shape[2:])


def swap(x, axis):
    return lax.ppermute(x, axis, [(0, 1), (1, 0)])


def seq_gather(x):
    if lax.axis_size("ys") != 2:
        return list(lax.all_gather(x, ("ys", "core"), axis=0))
    far = swap(x, "ys")
    return [x, swap(x, "core"), far, swap(far, "core")]


def seq_return(near, core, far, diagonal):
    return swap(core, "core"), swap((far + swap(diagonal, "core")).astype(LOW), "ys")


def seq_step(x, axis):
    if lax.axis_size("ys") != 2:
        if axis == "ys":
            return x
        return lax.psum_scatter(x, ("ys", "core"), scatter_dimension=0, tiled=True)[0].astype(F32)
    if axis == "ys":
        x = x.reshape((2, 2) + x.shape[1:])
    index = lax.axis_index(axis)
    sent = swap(lax.dynamic_index_in_dim(x, 1 - index, 0, keepdims=False).astype(LOW), axis)
    return lax.dynamic_index_in_dim(x, index, 0, keepdims=False).astype(F32) + sent.astype(F32)


def taken_blocks(x, table):
    return x.at[table].get(mode="promise_in_bounds")


def start_flags(positions, begins):
    return jnp.any(positions[..., None] == begins, -1).astype(F32)


def body(
    tokens,
    leading_layer_value,
    output_gradient,
    lengths,
    sequence_block_of,
    stored_block_of,
    channel_settings,
    receptance_matrix,
    key_matrix,
    value_matrix,
    output_matrix,
    branch_down_weight,
    branch_up_weight,
    channel_key_weight,
    channel_value_weight,
):
    rows_here, wide = tokens.shape
    per = rows_here // BLOCK
    ys, heads_axis = lax.axis_size("ys"), lax.axis_size("hz") * lax.axis_size("hx")
    seqs = 2 * ys
    head = lax.axis_index(HEAD_AXES)
    core = lax.axis_index("core")
    width = wide // heads_axis
    weight_rows = receptance_matrix.shape[0]
    low_rank = branch_down_weight.shape[1]
    order, home = sequence_block_of[0], stored_block_of[0]
    blocks = order.shape[0]
    begins = (jnp.cumsum(lengths[0]) - lengths[0]).astype(jnp.int32)
    splits = (DECAY_RANK, DECAY_RANK + DA, DECAY_RANK + DA + DV)

    og_first = output_gradient.reshape(per, BLOCK, wide)[:, 0]
    pad = jnp.zeros((16 - per, wide), LOW)
    place = home
    local = lax.dynamic_slice_in_dim(order, head * per, per)
    before_place = taken_blocks(place, jnp.maximum(local - 1, 0))
    after_place = taken_blocks(place, jnp.minimum(local + 1, blocks - 1))
    group = all_gather(jnp.concatenate([tokens, og_first, pad], 0)[None], HEAD_AXES)
    og_parts = seq_gather(output_gradient)

    quarter = channel_key_weight.shape[1] // seqs
    pair = jnp.stack([channel_key_weight, channel_value_weight], 0).reshape(2, weight_rows, seqs, quarter)
    pair = lax.all_to_all(
        pair.transpose(2, 0, 1, 3), ("ys", "core"), split_axis=0, concat_axis=0, tiled=True
    )
    to_heads = jnp.concatenate(
        [
            leading_layer_value.reshape(rows_here, heads_axis, width).transpose(1, 0, 2),
            jnp.stack([receptance_matrix, key_matrix, value_matrix], 1)
            .reshape(weight_rows * 3, heads_axis, width)
            .transpose(1, 0, 2),
        ],
        1,
    )
    def rank_columns(weight):
        return jnp.split(weight, (DECAY_RANK + DA, DECAY_RANK + DA + DV), 1)

    (down_pair, down_value, down_gate), (up_pair, up_value, up_gate) = [
        rank_columns(w) for w in (branch_down_weight, branch_up_weight)
    ]
    count = channel_settings.shape[1]
    blank = [jnp.zeros((weight_rows, n), LOW) for n in (32 - count, 32)]
    small = jnp.concatenate(
        [
            down_pair, down_gate, down_value, channel_settings, blank[0], up_value, blank[1],
            up_pair, up_gate,
        ],
        1,
    )[None]
    to_heads = lax.all_to_all(to_heads, HEAD_AXES, split_axis=0, concat_axis=0, tiled=True)
    for axis in HEAD_AXES + ("ys", "core"):
        small = grown(small, axis)
    small = in_order(small, HEAD_AXES + ("ys", "core"))
    first_group = to_heads[:, :rows_here]
    columns = to_heads[:, rows_here:].reshape(1, heads_axis * weight_rows, 3 * width)
    columns = in_order(grown(grown(columns, "ys"), "core"), ("ys", "core"))
    out_shards = grown(grown(output_matrix[None], "hz"), "hx")
    settings = small[:, 256 + DV : 256 + DV + count].astype(F32).T
    up = lax.dynamic_slice_in_dim(small, head * width, width, 0)
    own = lax.dynamic_slice_in_dim(settings, head * width, width, 1)
    own = jnp.concatenate([own[13:16], own[8:13]], 0)
    group, columns, small, settings, up, own, og_parts, out_shards, pair = lax.optimization_barrier(
        (group, columns, small, settings, up, own, og_parts, out_shards, pair)
    )
    out_shards = grown(out_shards, "ys")
    weights = [columns, small, up]

    def gathered(half):
        return all_gather(half[None], HEAD_AXES).transpose(1, 0, 2, 3)

    whole_quarter = quarter == wide
    if whole_quarter:
        every = all_gather(pair.transpose(1, 0, 2, 3).reshape(1, -1, weight_rows, wide), HEAD_AXES)
    else:
        every = (gathered(pair[:, 0]), gathered(pair[:, 1]))

    parts, gate, pre, first, *mids = project(
        group, first_group, settings, own, weights, place, home, begins, per
    )
    after_seq = local + 1
    after_live = (after_seq < blocks).astype(LOW)[:, None]
    stored = group[:, :rows_here].reshape(-1, BLOCK, wide)
    row_before = taken_blocks(stored[:, BLOCK - 1], before_place)
    row_after = taken_blocks(stored[:, 0], after_place)
    og_rows = group[:, rows_here : rows_here + per].reshape(-1, wide)
    og_after = taken_blocks(og_rows, after_place) * after_live
    none = jnp.zeros((per, 14, wide), LOW)
    og_extra = jnp.concatenate([none[:, :1], og_after[:, None], none], 1).reshape(-1, wide)
    extra_parts = seq_gather(og_extra)
    parts, og_parts, extra_parts, out_shards = lax.optimization_barrier(
        (parts, og_parts, extra_parts, out_shards)
    )
    out_shards = grown(out_shards, "core")
    out_in, joined, scanned, states, mats = scan_forward(parts, gate, own, begins, PASSES)

    before, follow = jnp.maximum(order - 1, 0), jnp.minimum(order + 1, blocks - 1)
    in_blocks = out_in.reshape(blocks, BLOCK, width)
    extended = jnp.concatenate(
        [
            taken_blocks(in_blocks, order),
            taken_blocks(in_blocks[:, BLOCK - 1], before)[:, None],
            taken_blocks(in_blocks[:, 0], follow)[:, None],
            jnp.zeros((blocks, 14, width), LOW),
        ],
        1,
    )
    extended, every = lax.optimization_barrier((extended, every))
    out_ext = lax.all_to_all(
        extended.reshape(heads_axis, per, TALL, width), HEAD_AXES, split_axis=0, concat_axis=0, tiled=True
    )
    if whole_quarter:
        key_part, value_part = [
            x.reshape(wide, quarter)
            for x in jnp.moveaxis(every.reshape(heads_axis, 2, seqs, weight_rows, wide), 0, 2)
        ]
    else:
        key_part, value_part = [x.reshape(wide, quarter) for x in every]
    out_weight = in_order(out_shards, HEAD_AXES + ("ys", "core"))
    out_ext, key_part, value_part, out_weight = lax.optimization_barrier(
        (out_ext, key_part, value_part, out_weight)
    )
    tokens_b = tokens.reshape(per, BLOCK, wide)
    tokens_ext = jnp.concatenate([tokens_b, row_before[:, None], row_after[:, None], none], 1)
    middle, ffn_in, out_rows = middle_rows(
        out_ext, tokens_ext.reshape(-1, wide), out_weight, settings, local, begins
    )
    ffn_parts = seq_gather(ffn_in)
    if whole_quarter:
        *near, own_part, core_part = channel_mix(
            ffn_parts[:2], og_parts[:2], extra_parts[:2], key_part, value_part
        )
        ffn_parts[2:], near, own_part, core_part, out_rows = lax.optimization_barrier(
            (ffn_parts[2:], near, own_part, core_part, out_rows)
        )
        *far, far_part, diagonal = channel_mix(
            ffn_parts[2:], og_parts[2:], extra_parts[2:], key_part, value_part
        )
        came_core, came_far = seq_return(own_part, core_part, far_part, diagonal)
        grads_here = channel_grads(
            og_parts, ffn_parts, (near[0], far[0]), (near[1], far[1]), wide // seqs
        )
        came_far, grads_here = lax.optimization_barrier((came_far, grads_here))
        hidden = [near[0], far[0]]
    else:
        rows = jnp.concatenate(ffn_parts, 0)
        og_rows = jnp.concatenate(
            [
                jnp.concatenate([g.reshape(per, BLOCK, wide), x.reshape(per, 16, wide)], 1).reshape(-1, wide)
                for g, x in zip(og_parts, extra_parts)
            ],
            0,
        )
        active = jax.nn.relu(dot(rows, key_part, NN))
        hidden = [(active * active).astype(LOW)]
        grad_pre = (dot(og_rows, value_part, NN) * 2.0 * active).astype(LOW)
        own_part = dot(grad_pre, key_part, NT).reshape(seqs, per * TALL, wide)
        own_part = lax.psum_scatter(own_part, ("ys", "core"), scatter_dimension=0, tiled=True)[0]
        came_core, came_far = jnp.zeros_like(own_part), jnp.zeros_like(ffn_in)
        is_main = (jnp.arange(rows.shape[0]) % TALL < BLOCK).astype(LOW)[:, None]
        grads_here = [dot(og_rows * is_main, hidden[0], TN), dot(rows * is_main, grad_pre, TN)]
    grad_middle, middle_low, grad_out, cols_ffn = middle_back(
        own_part, came_core, came_far, middle, output_gradient, out_weight, settings, local, begins, heads_axis
    )
    cols_ffn = cols_ffn[:3]
    grad_heads = lax.all_to_all(grad_out, HEAD_AXES, split_axis=0, concat_axis=0, tiled=True)
    out_parts, low_parts = seq_gather(out_rows), seq_gather(middle_low)
    which = lax.axis_index(("ys", "core"))
    if whole_quarter:
        grads_here = output_grads(out_parts, low_parts, which[None], grads_here)
    else:
        right = jnp.concatenate(low_parts, 0).reshape(seqs * per * TALL, seqs, -1)
        right = lax.dynamic_index_in_dim(right, which, 1, keepdims=False)
        grads_here.append(dot(jnp.concatenate(out_parts, 0), right, TN))
        grads_here = jnp.concatenate(grads_here, 1).astype(LOW)
    grad_heads, grads_here = lax.optimization_barrier((grad_heads, grads_here))
    grads_here = lax.psum_scatter(grads_here, HEAD_AXES, scatter_dimension=0, tiled=True)

    scan_grads, first_grad, cols_scan = scan_backward(
        parts, joined, scanned, gate, grad_heads.reshape(blocks, BLOCK, width), pre, first, own, states,
        mats, home, begins, PASSES,
    )
    first_grad = taken_blocks(first_grad.reshape(blocks, BLOCK, width), order)
    first_value_grad = lax.all_to_all(
        first_grad.reshape(heads_axis, rows_here, width), HEAD_AXES, split_axis=0, concat_axis=2, tiled=True
    ).reshape(rows_here, wide).astype(F32)

    back, down_sums, up_sums = project_back(
        group, scan_grads, mids, settings, weights, place, begins, per
    )
    back = taken_blocks(back.reshape(blocks, BLOCK, wide), order).reshape(-1, wide)
    back, grads_here, first_value_grad = lax.optimization_barrier((back, grads_here, first_value_grad))
    back = lax.psum_scatter(back, HEAD_AXES, scatter_dimension=0, tiled=True).astype(F32)
    value_sum, key_sum, out_sum = jnp.split(grads_here.astype(F32), (quarter, 2 * quarter), 1)

    share = wide // seqs
    thin = low_rank // seqs
    fold = heads_axis // seqs

    def over_ys(sums):
        down_sums, up_sums, own_cols = sums
        own_cols = lax.dynamic_update_slice(jnp.zeros((8, wide), F32), own_cols, (0, head * width))
        rows_out = jnp.concatenate([down_sums, own_cols, cols_ffn], 0)
        rows_out = jnp.pad(rows_out, ((0, -rows_out.shape[0] % 16), (0, 0)))
        rows_out = rows_out.astype(LOW).reshape(-1, seqs, share).transpose(1, 0, 2)
        both = jnp.concatenate(
            [rows_out, up_sums.astype(LOW).reshape(seqs, thin * width // share, share)], 1
        )
        return seq_step(both, "ys")

    def over_core(x):
        return seq_step(x, "core")

    def to_owners(x):
        rows_out_count = x.shape[0] - thin * width // share
        rows_out, up_sums = x[:rows_out_count], x[rows_out_count:].reshape(thin, width)
        rows_low = rows_out.astype(LOW)
        squares = rows_low[: 3 * width].reshape(3 * width, fold, width)
        mixed = rows_low[3 * width : 3 * width + low_rank].reshape(seqs, thin, fold, width)
        mixed = mixed.transpose(0, 2, 1, 3).reshape(heads_axis, thin, width)
        cols_part = rows_low[3 * width + low_rank :][:count].reshape(count, heads_axis, -1)
        cols_part = jnp.pad(
            cols_part.transpose(1, 0, 2), ((0, 0), (0, -count % 8), (0, width - cols_part.shape[2]))
        )
        mixed = lax.all_to_all(
            jnp.concatenate([mixed, cols_part], 1), HEAD_AXES, split_axis=0, concat_axis=0, tiled=True
        )
        came = []
        for k in range(fold):
            sent = lax.dynamic_index_in_dim(squares, (head + k) % fold, 1, keepdims=False)
            came.append(
                lax.ppermute(
                    sent, every_axis, [(q * heads_axis + h, owner(q, h, (h + k) % fold)) for q, h in pairs]
                )
            )
        return up_sums, mixed, came

    every_axis = ("ys", "core") + HEAD_AXES
    pairs = [(q, h) for q in range(seqs) for h in range(heads_axis)]

    def owner(q, h, j):
        return (h // fold) * heads_axis + q * fold + j

    up_sums, mixed, came = to_owners(over_core(over_ys((down_sums, up_sums, cols_scan))))
    unit, scale = norm_rows(tokens.astype(F32))
    tokens_grad = grad_middle + norm_back(back, unit, scale, settings[0])
    mixed = jnp.sum(mixed.astype(F32), 0)
    channel_grad = mixed[thin : thin + count, :weight_rows].T
    down_grad = lax.ppermute(
        mixed[:thin].astype(LOW), every_axis, [(q * heads_axis + h, owner(q, h, h % fold)) for q, h in pairs]
    ).T.astype(F32)
    outs = [dot(h, value_part, NT) for h in hidden]
    main_middle = middle.reshape(per, TALL, wide)[:, :BLOCK].reshape(rows_here, wide)

    def main_of(x):
        return x.reshape(-1, per, TALL, wide)[:, :, :BLOCK].reshape(-1, rows_here, wide)

    if whole_quarter:
        near, far = [main_of(x) for x in outs]
        came_core, came_far = seq_return(near[0], near[1], far[0], far[1])
        layer_out = main_middle + near[0] + came_core + came_far.astype(F32)
    else:
        layer_out = main_middle + lax.psum_scatter(
            main_of(outs[0]), ("ys", "core"), scatter_dimension=0, tiled=True
        )[0]
    came = jnp.stack(came, 0)
    came = taken_blocks(came, (head - jnp.arange(fold, dtype=jnp.int32)) % fold)
    came = came.reshape(fold, 3, width, width).transpose(1, 3, 0, 2).reshape(3, width, share)
    recept_grad, key_grad, value_grad = [came[i].astype(F32) for i in range(3)]
    up_grad = up_sums.T
    return (
        layer_out.astype(LOW),
        tokens_grad,
        first_value_grad,
        channel_grad,
        recept_grad,
        key_grad,
        value_grad,
        out_sum,
        down_grad,
        up_grad,
        key_sum,
        value_sum,
    )


def solution(mesh):
    seqs, heads = mesh.devices.shape
    split = Mesh(mesh.devices.reshape(seqs // 2, 2, 4, heads // 4), ("ys", "core") + HEAD_AXES)
    rows = P(("ys", "core") + HEAD_AXES, None)
    table = P(("ys", "core"), None)
    square = P(HEAD_AXES, ("ys", "core"))
    return jax.shard_map(
        body,
        mesh=split,
        in_specs=(rows,) * 3 + (table,) * 3 + (rows,) * 9,
        out_specs=(rows,) * 4 + (square,) * 8,
        check_vma=False,
    )
```

```python
import functools
import jax
import jax.numpy as jnp
from jax import lax
from jax.experimental import pallas as pl
from jax.experimental.pallas import tpu as pltpu
from jax.sharding import Mesh
from jax.sharding import PartitionSpec as P

DECAY_RANK = 64
DA = 64
DV = 32
BLOCK = 128
SPAN = 64
HEAD = 64
FORWARD_CHUNKS = 8
BACKWARD_CHUNKS = 4
LOW = jnp.bfloat16
F32 = jnp.float32
NN = (((1,), (0,)), ((), ()))
NT = (((1,), (1,)), ((), ()))
TN = (((0,), (0,)), ((), ()))
PASSES = {"pair": 3, "inv": 3, "val": 3, "chain": 3, "bpair": 3}


def work(micros):
    return pl.CostEstimate(flops=0, bytes_accessed=int(micros * 3_000), transcendentals=0)


def dot(a, b, dims):
    return lax.dot_general(a, b, dims, preferred_element_type=F32)


def halves(x):
    high = x.astype(LOW)
    return high, (x - high.astype(F32)).astype(LOW)


def product(a, b, dims, passes):
    if passes == 1:
        return dot(a.astype(LOW), b.astype(LOW), dims)
    la, lb = dims[0][0][0], dims[0][1][0]
    a_high, a_low = halves(a)
    if passes == 2:
        b = b.astype(LOW)
        return dot(jnp.concatenate([a_high, a_low], la), jnp.concatenate([b, b], lb), dims)
    b_high, b_low = halves(b)
    first = dot(jnp.concatenate([a_high, a_low], la), jnp.concatenate([b_high, b_high], lb), dims)
    return first + dot(a_high, b_low, dims)


def head_masks(heads):
    lane = lax.broadcasted_iota(jnp.int32, (1, heads * HEAD), 1) // HEAD
    return [(lane == h).astype(F32) for h in range(heads)]


def stacked(x, masks):
    if len(masks) == 1:
        return x
    return jnp.concatenate([x * m for m in masks], 0)


def unstacked(x, heads):
    rows = x.shape[0] // heads
    out = x[:rows]
    for h in range(1, heads):
        out = out + x[h * rows : (h + 1) * rows]
    return out


def head_ones(width):
    row = lax.broadcasted_iota(jnp.int32, (width, width), 0) // HEAD
    col = lax.broadcasted_iota(jnp.int32, (width, width), 1) // HEAD
    return (row == col).astype(LOW)


def head_sum(x, ones):
    high, low = halves(x)
    return dot(jnp.concatenate([high, low], 1), jnp.concatenate([ones, ones], 0), NN)


class Chunk:
    def __init__(self, r, lw, k, kn, a, begins, start, heads):
        self.heads = heads
        masks = head_masks(heads)
        rows = heads * SPAN
        local = [jnp.where(b >= start, b - start, SPAN) for b in begins]
        row_t = lax.broadcasted_iota(jnp.int32, (rows, 1), 0) % SPAN
        col_t = lax.broadcasted_iota(jnp.int32, (1, rows), 1) % SPAN
        row_seg = sum((row_t >= b).astype(jnp.int32) for b in local)
        col_seg = sum((col_t >= b).astype(jnp.int32) for b in local)
        last = sum((b < SPAN).astype(jnp.int32) for b in local)
        same = row_seg == col_seg
        self.strict = same & (row_t > col_t)
        self.upto = same & (row_t >= col_t)
        self.carried = (row_seg == 0).astype(F32)
        self.final = (row_seg == last).astype(F32)
        self.whole = (last == 0).astype(F32)
        tri_r = lax.broadcasted_iota(jnp.int32, (SPAN, SPAN), 0)
        tri_c = lax.broadcasted_iota(jnp.int32, (SPAN, SPAN), 1)
        running = dot((tri_r >= tri_c).astype(LOW), lw, NN)
        lw = lw.astype(F32)
        decay = jnp.exp(running)
        before = jnp.exp(running - lw)
        inverse = jnp.exp(-running)
        end = running[SPAN - 1 : SPAN]
        to_end = jnp.exp(end - running)
        self.end = jnp.exp(end)
        kn = kn.astype(F32)
        beta = kn * a.astype(F32)
        k = k.astype(F32)
        self.decay, self.before, self.inverse, self.to_end = decay, before, inverse, to_end
        self.a_hat = stacked(-kn * before, masks)
        self.r_hat = stacked(r.astype(F32) * decay, masks)
        self.b_hat = stacked(beta * inverse, masks)
        self.k_hat = stacked(k * inverse, masks)
        self.b_end = stacked(beta * to_end, masks) * self.final
        self.k_end = stacked(k * to_end, masks) * self.final


def block_inverses(all_pairs, passes):
    rows = all_pairs[0].shape[0]
    row = lax.broadcasted_iota(jnp.int32, (rows, rows), 0)
    col = lax.broadcasted_iota(jnp.int32, (rows, rows), 1)
    eye = (row == col).astype(F32)

    def products(left, right):
        return [product(a, b, NN, passes) for a, b in zip(left, right)]

    within = row // 8 == col // 8
    small = [jnp.where(within, pairs, 0.0) for pairs in all_pairs]
    square = products(small, small)
    fourth = products(square, square)
    first = [eye + x for x in small]
    inverse = [a + b for a, b in zip(first, products(first, square))]
    inverse = [a + b for a, b in zip(inverse, products(inverse, fourth))]
    size = 8
    while size < SPAN:
        within = (row // (2 * size) == col // (2 * size)) & (row // size != col // size)
        cross = [jnp.where(within, pairs, 0.0) for pairs in all_pairs]
        step = products(products(inverse, cross), inverse)
        inverse = [a + b for a, b in zip(inverse, step)]
        size *= 2
    return inverse


def group_norm_parts(scanned, ones):
    center = scanned - head_sum(scanned, ones) * (1.0 / HEAD)
    spread = head_sum(center * center, ones) * (1.0 / HEAD)
    scale = lax.rsqrt(spread + 0.00064)
    return center * scale, scale


def scan_forward_kernel(
    heads, p, home_ref, begins_ref, parts_ref, pre_ref, gate_ref, cols_ref, *rest,
):
    first_refs, rest = rest[: FORWARD_CHUNKS * SPAN // BLOCK], rest[FORWARD_CHUNKS * SPAN // BLOCK :]
    values_ref, out_ref, joined_ref, scanned_ref, state_ref, mats_ref, state = rest
    step = pl.program_id(0)
    width = heads * HEAD

    @pl.when(step == 0)
    def _():
        state[...] = jnp.zeros_like(state)

    begins = [begins_ref[i] for i in range(begins_ref.shape[0])]
    masks = head_masks(heads)
    n = heads * SPAN
    eye = (
        lax.broadcasted_iota(jnp.int32, (width, width), 0)
        == lax.broadcasted_iota(jnp.int32, (width, width), 1)
    ).astype(F32)
    first = jnp.concatenate([ref[0] for ref in first_refs], 0).astype(F32)
    mix = jax.nn.sigmoid(cols_ref[5:6] + pre_ref[4])
    values = (pre_ref[1] + (first - pre_ref[1]) * mix).astype(LOW)
    values_ref[...] = values
    held = []
    for c in range(FORWARD_CHUNKS):
        rows = pl.ds(c * SPAN, SPAN)
        r, lw, k, kn, a = [parts_ref[i, rows] for i in range(5)]
        v = values[c * SPAN : (c + 1) * SPAN]
        q = Chunk(r, lw, k, kn, a, begins, (step * FORWARD_CHUNKS + c) * SPAN, heads)
        v_st = stacked(v.astype(F32), masks).astype(LOW)
        held.append((q, r, k, v, v_st))
    all_pairs = [
        product(
            jnp.concatenate([q.a_hat, q.r_hat], 0), jnp.concatenate([q.b_hat, q.k_hat], 0), NT, p["pair"]
        )
        for q, *_ in held
    ]
    l_ab = [jnp.where(h[0].strict, x[:n, :n], 0.0) for h, x in zip(held, all_pairs)]
    l_ak = [jnp.where(h[0].strict, x[:n, n:], 0.0) for h, x in zip(held, all_pairs)]
    l_rb = [jnp.where(h[0].upto, x[n:, :n], 0.0) for h, x in zip(held, all_pairs)]
    l_rk = [jnp.where(h[0].upto, x[n:, n:], 0.0) for h, x in zip(held, all_pairs)]
    both_v = [
        product(jnp.concatenate([ak, rk], 0), h[4], NN, 2 if p["val"] == 3 else 1)
        for ak, rk, h in zip(l_ak, l_rk, held)
    ]
    inverses = block_inverses(l_ab, p["inv"])
    solved = [
        product(t, jnp.concatenate([h[0].a_hat * h[0].carried, b[:n]], 1), NN, p["val"])
        for t, h, b in zip(inverses, held, both_v)
    ]
    ends = [product(x, h[0].b_end, TN, p["val"]) for x, h in zip(solved, held)]
    grown = []
    for q, _, _, _, v_st in held:
        if p["val"] == 3:
            k_high, k_low = halves(q.k_end)
            grown.append(dot(jnp.concatenate([v_st, v_st], 0), jnp.concatenate([k_high, k_low], 0), TN))
        else:
            grown.append(dot(v_st, q.k_end.astype(LOW), TN))
    ready = []
    for c in range(FORWARD_CHUNKS):
        q, r, k, v, _ = held[c]
        through = product(l_rb[c], solved[c], NN, p["val"])
        r_thru = q.r_hat * q.carried + through[:, :width]
        o_val = both_v[c][n:] + through[:, width:]
        move = eye * (q.end * q.whole) + ends[c][:width]
        gain = ends[c][width:] + grown[c]
        mats = [
            inverses[c], l_ak[c], l_rb[c], l_rk[c], solved[c][:, :width], solved[c][:, width:], move, r_thru,
        ]
        for i, m in enumerate(mats):
            mats_ref[c, i] = m
        ready.append((move, gain, r_thru, o_val, r, k, v))
    ones = head_ones(width)
    now = state[...]
    begun = []
    for c in range(FORWARD_CHUNKS):
        begun.append(now)
        state_ref[c] = now
        now = product(now, ready[c][0], NN, p["chain"]) + ready[c][1]
    state[...] = now
    for c in range(FORWARD_CHUNKS):
        rows = pl.ds(c * SPAN, SPAN)
        _, _, r_thru, o_val, r, k, v = ready[c]
        scanned = unstacked(o_val + product(r_thru, begun[c], NT, p["val"]), heads)
        scanned_ref[rows] = scanned
        unit, _ = group_norm_parts(scanned, ones)
        bonus = head_sum(r.astype(F32) * k.astype(F32) * cols_ref[0:1], ones)
        joined = unit * cols_ref[1:2] + cols_ref[2:3] + bonus * v.astype(F32)
        joined = joined.astype(LOW)
        joined_ref[rows] = joined
        out_ref[rows] = (joined.astype(F32) * gate_ref[rows]).astype(LOW)


def scan_forward(parts, pre, first, gate, cols, home, begins, p):
    _, total, width = parts.shape
    heads = width // HEAD
    rows = FORWARD_CHUNKS * SPAN
    n = heads * SPAN
    spans = total // SPAN
    assert n == width
    row_spec = pl.BlockSpec((rows, width), lambda i, *_: (i, 0))
    per_step = rows // BLOCK

    def stored(which):
        return pl.BlockSpec((1, BLOCK, width), lambda i, home, b: (home[per_step * i + which], 0, 0))

    return pl.pallas_call(
        functools.partial(scan_forward_kernel, heads, p),
        grid_spec=pltpu.PrefetchScalarGridSpec(
            num_scalar_prefetch=2,
            grid=(total // rows,),
            in_specs=[
                pl.BlockSpec((5, rows, width), lambda i, *_: (0, i, 0)),
                pl.BlockSpec((5, rows, width), lambda i, *_: (0, i, 0)),
                row_spec,
                pl.BlockSpec(cols.shape, lambda i, *_: (0, 0)),
            ]
            + [stored(w) for w in range(per_step)],
            out_specs=[
                row_spec,
                row_spec,
                row_spec,
                row_spec,
                pl.BlockSpec((FORWARD_CHUNKS, width, width), lambda i, *_: (i, 0, 0)),
                pl.BlockSpec((FORWARD_CHUNKS, 8, n, width), lambda i, *_: (i, 0, 0, 0)),
            ],
            scratch_shapes=[pltpu.VMEM((width, width), F32)],
        ),
        out_shape=[
            jax.ShapeDtypeStruct((total, width), LOW),
            jax.ShapeDtypeStruct((total, width), LOW),
            jax.ShapeDtypeStruct((total, width), LOW),
            jax.ShapeDtypeStruct((total, width), F32),
            jax.ShapeDtypeStruct((spans, width, width), F32),
            jax.ShapeDtypeStruct((spans, 8, n, width), F32),
        ],
        compiler_params=pltpu.CompilerParams(vmem_limit_bytes=48 * 1024 * 1024),
        cost_estimate=work(80),
    )(home, begins, parts, pre, gate, cols, *[first] * per_step)


def scan_backward_kernel(
    heads, p, home_ref, begins_ref, parts_ref, values_ref, joined_ref, scanned_ref, gate_ref, grad_a_ref,
    grad_b_ref, pre_ref, first_a_ref, first_b_ref, cols_ref, state_ref, mats_ref, *rest,
):
    steps = pl.num_programs(0)
    step = steps - 1 - pl.program_id(0)
    grads_ref, first_grad_ref, col_grad_ref, state = rest
    width = heads * HEAD
    n = heads * SPAN

    @pl.when(pl.program_id(0) == 0)
    def _():
        state[...] = jnp.zeros_like(state)
        col_grad_ref[...] = jnp.zeros_like(col_grad_ref)

    begins = [begins_ref[i] for i in range(begins_ref.shape[0])]
    masks = head_masks(heads)
    ones = head_ones(width)
    tri_r = lax.broadcasted_iota(jnp.int32, (SPAN, SPAN), 0)
    tri_c = lax.broadcasted_iota(jnp.int32, (SPAN, SPAN), 1)
    later = (tri_c >= tri_r).astype(LOW)
    after = (tri_c > tri_r).astype(LOW)
    sums = [jnp.zeros((1, width), F32) for _ in range(8)]

    def add(slot, value):
        sums[slot] = sums[slot] + jnp.sum(value, 0, keepdims=True)

    c13, c14 = cols_ref[0:1], cols_ref[1:2]
    grads = jnp.concatenate([grad_a_ref[0], grad_b_ref[0]], 0).astype(F32)
    firsts = jnp.concatenate([first_a_ref[0], first_b_ref[0]], 0).astype(F32)
    ready = []
    for c in range(BACKWARD_CHUNKS):
        rows = pl.ds(c * SPAN, SPAN)
        r, lw, k, kn, a = [parts_ref[i, rows] for i in range(5)]
        v = values_ref[rows]
        q = Chunk(r, lw, k, kn, a, begins, (step * BACKWARD_CHUNKS + c) * SPAN, heads)
        r, k, v = r.astype(F32), k.astype(F32), v.astype(F32)
        unit, scale = group_norm_parts(scanned_ref[rows], ones)
        grad_out = grads[c * SPAN : (c + 1) * SPAN]
        grad_joined = (grad_out * gate_ref[rows]).astype(LOW).astype(F32)
        grad_gate = (grad_out * joined_ref[rows].astype(F32)).astype(LOW)
        add(6, grad_joined * unit)
        add(7, grad_joined)
        grad_unit = grad_joined * c14
        grad_scan = scale * (
            grad_unit
            - head_sum(grad_unit, ones) * (1.0 / HEAD)
            - unit * (head_sum(grad_unit * unit, ones) * (1.0 / HEAD))
        )
        bonus = head_sum(r * k * c13, ones)
        grad_bonus = head_sum(grad_joined * v, ones)
        add(5, grad_bonus * r * k)
        own_r = grad_bonus * k * c13
        own_k = grad_bonus * r * c13
        own_v = grad_joined * bonus
        d_out = stacked(grad_scan, masks)
        flow = product(d_out, mats_ref[c, 7], TN, p["val"])
        ready.append((q, d_out, flow, own_r, own_k, own_v, grad_gate))
    now = state[...]
    ended = [None] * BACKWARD_CHUNKS
    for c in reversed(range(BACKWARD_CHUNKS)):
        ended[c] = now
        now = product(now, mats_ref[c, 6], NT, p["chain"]) + ready[c][2]
    state[...] = now
    span = range(BACKWARD_CHUNKS)
    mats = [[mats_ref[c, i] for i in range(6)] for c in span]
    begin = [state_ref[c] for c in span]
    chunks = [ready[c][0] for c in span]
    d_outs = [ready[c][1] for c in span]
    v_st = [stacked(values_ref[pl.ds(c * SPAN, SPAN)].astype(F32), masks) for c in span]
    update = [mats[c][5] + product(mats[c][4], begin[c], NT, p["val"]) for c in span]
    through = [product(mats[c][2], d_outs[c], TN, p["val"]) for c in span]
    through = [
        through[c] + product(chunks[c].b_end, ended[c], NT, p["val"]) for c in span
    ]
    back = [product(mats[c][0], through[c], TN, p["val"]) for c in span]
    left = [jnp.concatenate([back[c], d_outs[c]], 0) for c in span]
    right = [jnp.concatenate([update[c], v_st[c]], 0) for c in span]
    d_hats = [product(left[c], begin[c], NN, p["val"]) for c in span]
    pair_grads = [product(left[c], right[c], NT, p["bpair"]) for c in span]
    for c in span:
        strict, upto = chunks[c].strict.astype(F32), chunks[c].upto.astype(F32)
        mask = jnp.concatenate(
            [jnp.concatenate([strict, strict], 1), jnp.concatenate([upto, upto], 1)], 0
        )
        pair_grads[c] = pair_grads[c] * mask
    all_asks = []
    for c in span:
        q = chunks[c]
        keys = jnp.concatenate([q.b_hat, q.k_hat], 0)
        carried = jnp.concatenate([q.carried, q.carried], 0)
        all_asks.append(d_hats[c] * carried + product(pair_grads[c], keys, NN, p["bpair"]))
    all_keys = [
        product(
            pair_grads[c], jnp.concatenate([chunks[c].a_hat, chunks[c].r_hat], 0), TN, p["bpair"]
        )
        for c in span
    ]
    all_ends = [product(right[c], ended[c], NN, p["val"]) for c in span]
    all_vals = [
        product(jnp.concatenate([mats[c][1], mats[c][3]], 0), left[c], TN, p["val"]) for c in span
    ]
    all_vals = [
        all_vals[c] + product(chunks[c].k_end, ended[c], NT, p["val"]) for c in span
    ]
    for c in span:
        rows = pl.ds(c * SPAN, SPAN)
        q, _, _, own_r, own_k, own_v, grad_gate = ready[c]
        end_grad, begin_now = ended[c], begin[c]
        r, lw, k, kn, a = [parts_ref[i, rows].astype(F32) for i in range(5)]
        v = values_ref[rows].astype(F32)
        d_asks, d_keys, d_val = all_asks[c], all_keys[c], all_vals[c]
        d_ends = all_ends[c] * jnp.concatenate([q.final, q.final], 0)
        d_a, d_r = unstacked(d_asks[:n], heads) * q.before, unstacked(d_asks[n:], heads) * q.decay
        d_b = unstacked(d_keys[:n], heads) * q.inverse
        d_k = unstacked(d_keys[n:], heads) * q.inverse
        e_b = unstacked(d_ends[:n], heads) * q.to_end
        e_k = unstacked(d_ends[n:], heads) * q.to_end
        d_v = unstacked(d_val, heads) + own_v
        beta = kn * a
        end_part = e_b * beta + e_k * k
        here = d_r * r - d_b * beta - d_k * k - end_part
        ahead = -d_a * kn
        at_end = jnp.sum(end_part, 0, keepdims=True) + q.whole * q.end * jnp.sum(
            begin_now * end_grad, 0, keepdims=True
        )
        high, low = halves(here)
        high2, low2 = halves(ahead)
        d_lw = at_end + dot(
            jnp.concatenate([later, later, after, after], 1),
            jnp.concatenate([high, low, high2, low2], 0),
            NN,
        )
        d_b = d_b + e_b
        d_k = d_k + e_k + own_k
        d_r = d_r + own_r
        d_kn = d_b * a - d_a
        d_rate = d_b * kn
        g_r, g_lw, g_k, g_kn, g_a, g_v = [
            x.astype(LOW).astype(F32) for x in (d_r, d_lw, d_k, d_kn, d_rate, d_v)
        ]
        key_pre, value_pre, decay_up, rate_up, value_up = [pre_ref[i, rows] for i in range(5)]
        first = firsts[c * SPAN : (c + 1) * SPAN]
        c8, c9, c10, c11, c12 = [cols_ref[i : i + 1] for i in range(3, 8)]
        sig = jax.nn.sigmoid(c8 + decay_up)
        log_decay = -0.6065306597126334 * sig
        g_decay = g_lw * log_decay * (1.0 - sig)
        add(0, g_decay)
        rate = jax.nn.sigmoid(c9 + rate_up)
        g_rate = (g_a + g_k * key_pre * c12) * rate * (1.0 - rate)
        add(1, g_rate)
        g_key = g_k * (1.0 + (rate - 1.0) * c12)
        add(4, g_k * key_pre * (rate - 1.0))
        scaled = key_pre * c11
        norm = lax.rsqrt(head_sum(scaled * scaled, ones) + 1e-06)
        unit = scaled * norm
        g_scaled = norm * (g_kn - unit * head_sum(g_kn * unit, ones))
        g_key = g_key + g_scaled * c11
        add(3, g_scaled * key_pre)
        mix = jax.nn.sigmoid(c10 + value_up)
        g_value = g_v * (1.0 - mix)
        first_grad_ref[rows] = (g_v * mix).astype(first_grad_ref.dtype)
        g_vup = g_v * (first - value_pre) * mix * (1.0 - mix)
        add(2, g_vup)
        for i, x in enumerate((g_r, g_key, g_value, g_decay, g_rate, g_vup)):
            grads_ref[i, rows] = x.astype(LOW)
        grads_ref[6, rows] = grad_gate
    col_grad_ref[...] += jnp.concatenate(sums, 0)


def scan_backward(parts, values, joined, scanned, gate, grad, pre, first, cols, states, mats, home, begins, p):
    _, total, width = parts.shape
    heads = width // HEAD
    rows = BACKWARD_CHUNKS * SPAN
    n = heads * SPAN
    steps = total // rows
    row_spec = pl.BlockSpec((rows, width), lambda i, *_: (steps - 1 - i, 0))
    assert rows == 2 * BLOCK

    def stored(which):
        return pl.BlockSpec(
            (1, BLOCK, width), lambda i, home, b: (home[2 * (steps - 1 - i) + which], 0, 0)
        )

    return pl.pallas_call(
        functools.partial(scan_backward_kernel, heads, p),
        grid_spec=pltpu.PrefetchScalarGridSpec(
            num_scalar_prefetch=2,
            grid=(steps,),
            in_specs=[
                pl.BlockSpec((5, rows, width), lambda i, *_: (0, steps - 1 - i, 0)),
                row_spec,
                row_spec,
                row_spec,
                row_spec,
                stored(0),
                stored(1),
                pl.BlockSpec((5, rows, width), lambda i, *_: (0, steps - 1 - i, 0)),
                stored(0),
                stored(1),
                pl.BlockSpec(cols.shape, lambda i, *_: (0, 0)),
                pl.BlockSpec((BACKWARD_CHUNKS, width, width), lambda i, *_: (steps - 1 - i, 0, 0)),
                pl.BlockSpec((BACKWARD_CHUNKS, 8, n, width), lambda i, *_: (steps - 1 - i, 0, 0, 0)),
            ],
            out_specs=[
                pl.BlockSpec((7, rows, width), lambda i, *_: (0, steps - 1 - i, 0)),
                row_spec,
                pl.BlockSpec((8, width), lambda i, *_: (0, 0)),
            ],
            scratch_shapes=[pltpu.VMEM((width, width), F32)],
        ),
        out_shape=[
            jax.ShapeDtypeStruct((7, total, width), LOW),
            jax.ShapeDtypeStruct((total, width), LOW),
            jax.ShapeDtypeStruct((8, width), F32),
        ],
        compiler_params=pltpu.CompilerParams(vmem_limit_bytes=56 * 1024 * 1024),
        cost_estimate=work(60),
    )(home, begins, parts, values, joined, scanned, gate, grad, grad, pre, first, first, cols, states, mats)


def norm_rows(x):
    center = x - jnp.mean(x, -1, keepdims=True)
    scale = lax.rsqrt(jnp.mean(center * center, -1, keepdims=True) + 1e-05)
    return center * scale, scale


def keep_rows(rows, first, begins):
    position = first + lax.broadcasted_iota(jnp.int32, (rows, 1), 0)
    hit = position == begins[0]
    for b in begins[1:]:
        hit = hit | (position == b)
    return 1.0 - hit.astype(F32)


def rows_down(x, edge):
    row = lax.broadcasted_iota(jnp.int32, (x.shape[0], 1), 0)
    return jnp.where(row == 0, edge, pltpu.roll(x, 1, 0))


def rows_up(x, edge):
    row = lax.broadcasted_iota(jnp.int32, (x.shape[0], 1), 0)
    return jnp.where(row == x.shape[0] - 1, edge, pltpu.roll(x, x.shape[0] - 1, 0))


def lane_below(limit):
    return lax.broadcasted_iota(jnp.int32, (1, 128), 1) < limit


def kept(x, mask):
    return jnp.where(mask, x, jnp.zeros_like(x))


class SmallWeights:
    def __init__(self, small, up):
        self.pair, self.gate, self.value = small[:, :128], small[:, 128:256], small[:, 256:384]
        self.up_pair, self.up_gate = up[:, 384:512], up[:, 512:640]
        self.up_value = jnp.concatenate([up[:, 320:352], jnp.zeros((up.shape[0], 96), LOW)], 1)


def project_kernel(
    place_ref, begins_ref, xa_ref, xb_ref, cols_ref, own_ref, columns_ref,
    small_ref, up_ref, ends_ref, parts_ref, gate_ref, pre_ref, pair_ref, vm_ref, gs_ref, edge,
):
    step = pl.program_id(0)

    @pl.when(step == 0)
    def _():
        edge[...] = jnp.zeros_like(edge)

    begins = [begins_ref[i] for i in range(begins_ref.shape[0])]
    for i, ref in enumerate((xa_ref, xb_ref)):
        ends_ref[i] = jnp.concatenate([ref[0, :16], ref[0, BLOCK - 16 :]], 0)
    x = jnp.concatenate([xa_ref[0], xb_ref[0]], 0).astype(F32)
    rows = x.shape[0]
    unit, _ = norm_rows(x)
    normed = unit * cols_ref[0:1] + cols_ref[1:2]
    moved = rows_down(normed, edge[0:1]) * keep_rows(rows, step * rows, begins)
    edge[0:1] = normed[rows - 1 : rows]
    diff = moved - normed
    mixed = [(normed + diff * cols_ref[i : i + 1]).astype(LOW) for i in range(2, 8)]
    in_r, in_d, in_k, in_v, in_a, in_g = mixed
    low = SmallWeights(small_ref[...], up_ref[...])
    width = own_ref.shape[1]
    recept = dot(in_r, columns_ref[:, :width], NN)
    key_pre = dot(in_k, columns_ref[:, width : 2 * width], NN)
    values = dot(in_v, jnp.concatenate([columns_ref[:, 2 * width :], low.value], 1), NN)
    value_pre = values[:, :width]
    value_mid = kept(values[:, width:], lane_below(DV)).astype(LOW)
    decay, rate = dot(in_d, low.pair, NN), dot(in_a, low.pair, NN)
    pair = jnp.where(lane_below(DECAY_RANK), jnp.tanh(decay), rate)
    pair_low = pair.astype(LOW)
    gate_sig = jax.nn.sigmoid(dot(in_g, low.gate, NN))
    decay_up = dot(kept(pair_low, lane_below(DECAY_RANK)), low.up_pair, NT)
    rate_up = dot(kept(pair_low, ~lane_below(DECAY_RANK)), low.up_pair, NT)
    value_up = dot(value_mid, low.up_value, NT)
    gate_ref[...] = dot(gate_sig.astype(LOW), low.up_gate, NT)
    pair_ref[...] = pair
    vm_ref[...] = value_mid
    gs_ref[...] = gate_sig
    for i, value in enumerate((key_pre, value_pre, decay_up, rate_up, value_up)):
        pre_ref[i] = value
    c8, c9, _, c11, c12 = [own_ref[i : i + 1] for i in range(3, 8)]
    ones = head_ones(recept.shape[1])
    log_decay = -jnp.exp(-jax.nn.softplus(-(c8 + decay_up)) - 0.5)
    rate = jax.nn.sigmoid(c9 + rate_up)
    scaled = key_pre * c11
    key_norm = scaled * lax.rsqrt(head_sum(scaled * scaled, ones) + 1e-06)
    key_main = key_pre * (1.0 + (rate - 1.0) * c12)
    for i, value in enumerate((recept, log_decay, key_main, key_norm, rate)):
        parts_ref[i] = value.astype(LOW)


def block_spec(per, which, rows, width, blocks, back, table=0):
    def index(i, *tables):
        step = blocks // 2 - 1 - i if back else i
        stored = tables[table][jnp.maximum(2 * step + which, 0)]
        return (stored // per, (stored % per) * (BLOCK // rows) + BLOCK // rows - 1, 0)

    return pl.BlockSpec((1, rows, width), index)


def whole_spec(array):
    return pl.BlockSpec(array.shape, lambda i, *_: (0,) * array.ndim)


def project(x, cols, own, weights, place, begins, per):
    blocks = place.shape[0]
    total = blocks * BLOCK
    rows = 2 * BLOCK
    width = own.shape[1]
    span = lambda w: pl.BlockSpec((rows, w), lambda i, *_: (i, 0))
    deep = lambda n: pl.BlockSpec((n, rows, width), lambda i, *_: (0, i, 0))
    shape = jax.ShapeDtypeStruct
    return pl.pallas_call(
        project_kernel,
        grid_spec=pltpu.PrefetchScalarGridSpec(
            num_scalar_prefetch=2,
            grid=(blocks // 2,),
            in_specs=[
                block_spec(per, 0, BLOCK, x.shape[2], blocks, False),
                block_spec(per, 1, BLOCK, x.shape[2], blocks, False),
                whole_spec(cols),
                whole_spec(own),
            ]
            + [whole_spec(w) for w in weights],
            out_specs=[
                pl.BlockSpec((2, 32, x.shape[2]), lambda i, *_: (i, 0, 0)),
                deep(5), span(width), deep(5), span(128), span(128), span(128),
            ],
            scratch_shapes=[pltpu.VMEM((8, x.shape[2]), F32)],
        ),
        out_shape=[
            shape((blocks, 32, x.shape[2]), LOW),
            shape((5, total, width), LOW),
            shape((total, width), F32),
            shape((5, total, width), F32),
            shape((total, 128), F32),
            shape((total, 128), LOW),
            shape((total, 128), F32),
        ],
        compiler_params=pltpu.CompilerParams(vmem_limit_bytes=56 * 1024 * 1024),
        cost_estimate=work(20),
    )(place, begins, x, x, cols, own, *weights)


def project_back_kernel(
    part, parts, place_ref, turn_ref, row_ref, begins_ref, head_ref, xa_ref, xb_ref, xp_ref, grads_ref,
    pair_ref, vm_ref, gs_ref, scan_ref, ffn_ref, cols_ref, columns_ref, small_ref, up_ref, *rest,
):
    sizes_x = len(rest) - 4 - (2 if part == 0 else 1)
    back_refs, rest = rest[:sizes_x], rest[sizes_x:]
    if part == 0:
        low_sum_ref, up_sum_ref, edge, sum_ref, buffer, sems = rest
    else:
        low_sum_ref, edge, sum_ref, buffer, sems = rest
    turn = pl.program_id(0)
    step = pl.num_programs(0) - 1 - turn
    wide = columns_ref.shape[0]
    lanes = slice(part * wide, (part + 1) * wide)

    @pl.when(turn == 0)
    def _():
        for ref in (edge, sum_ref) + ((up_sum_ref,) if part == 0 else ()):
            ref[...] = jnp.zeros_like(ref)

    begins = [begins_ref[i] for i in range(begins_ref.shape[0])]

    def normal(x):
        x = x.astype(F32)
        mean = jnp.mean(x, -1, keepdims=True)
        spread = jnp.mean((x - mean) * (x - mean), -1, keepdims=True)
        return (x[:, lanes] - mean) * lax.rsqrt(spread + 1e-05)

    unit = normal(jnp.concatenate([xa_ref[0], xb_ref[0]], 0))
    rows = unit.shape[0]
    normed = unit * cols_ref[0:1] + cols_ref[1:2]
    prior = normal(xp_ref[0]) * cols_ref[0:1] + cols_ref[1:2]
    keep = keep_rows(rows, step * rows, begins)
    diff = rows_down(normed, prior[prior.shape[0] - 1 :]) * keep - normed
    low = SmallWeights(small_ref[...], up_ref[...])
    width = grads_ref.shape[2]
    g_r, g_k, g_v, g_decay, g_rate, g_vup, g_gate = [grads_ref[i] for i in range(7)]
    pair, sig = pair_ref[...], gs_ref[...]
    is_decay = lane_below(DECAY_RANK)
    m_pair = jnp.where(
        is_decay, dot(g_decay, low.up_pair, NN) * (1.0 - pair * pair), dot(g_rate, low.up_pair, NN)
    ).astype(LOW)
    m_v = kept(dot(g_vup, low.up_value, NN), lane_below(DV)).astype(LOW)
    m_g = (dot(g_gate, low.up_gate, NN) * sig * (1.0 - sig)).astype(LOW)
    near = jnp.zeros_like(unit)
    far = jnp.zeros_like(unit)
    value_weights = jnp.concatenate([columns_ref[:, 2 * width :], low.value], 1)
    cut = DECAY_RANK + DA + 3 * width
    grads = (
        (2, g_r, columns_ref[:, :width], ((0, g_r),)),
        (3, kept(m_pair, is_decay), low.pair, ((3 * width, m_pair[:, :DECAY_RANK]),)),
        (4, g_k, columns_ref[:, width : 2 * width], ((width, g_k),)),
        (5, jnp.concatenate([g_v, m_v], 1), value_weights, ((2 * width, g_v), (cut, m_v[:, :DV]))),
        (6, kept(m_pair, ~is_decay), low.pair, ((3 * width + DECAY_RANK, m_pair[:, DECAY_RANK:]),)),
        (7, m_g, low.gate, ((cut + DV, m_g),)),
    )
    col_sums = []
    for slot, grad, weight, pieces in grads:
        mix = cols_ref[slot : slot + 1]
        mixed = (normed + diff * mix).astype(LOW)
        total = dot(grad, weight, NT)
        for start, piece in pieces:
            sum_ref[start : start + piece.shape[1]] += dot(piece, mixed, TN)
        near = near + total
        far = far + total * mix
        col_sums.append(jnp.sum(total * diff, 0, keepdims=True))
    if part == 0:
        start = 0
        pair_low = pair.astype(LOW)
        for mid, grad in (
            (pair_low[:, :DECAY_RANK], g_decay),
            (pair_low[:, DECAY_RANK:], g_rate),
            (vm_ref[:, :DV], g_vup),
            (sig.astype(LOW), g_gate),
        ):
            up_sum_ref[start : start + mid.shape[1]] += dot(mid, grad, TN)
            start += mid.shape[1]
    moved = far * keep
    back = near - far + rows_up(moved, edge[0:1])
    edge[0:1] = moved[0:1]
    first = [jnp.sum(back * unit, 0, keepdims=True), jnp.sum(back, 0, keepdims=True)]
    sum_ref[sum_ref.shape[0] - 8 :] += jnp.concatenate(first + col_sums, 0)

    slot = turn % 2

    def leave(where):
        for which in range(2):
            pltpu.make_async_copy(
                buffer.at[where, which], back_refs[0].at[0], sems.at[where, which]
            ).wait()

    @pl.when(turn >= 2)
    def _():
        leave(slot)

    buffer[slot] = back.astype(LOW).reshape(2, BLOCK, wide)
    for which in range(2):
        block = 2 * step + which
        for x, ref in enumerate(back_refs):

            @pl.when(turn_ref[block] == x)
            def _():
                pltpu.make_async_copy(
                    buffer.at[slot, which], ref.at[row_ref[block]], sems.at[slot, which]
                ).start()

    @pl.when(step == 0)
    def _():
        held = sum_ref.shape[0]
        low_sum_ref[:held] = sum_ref[...].astype(LOW)
        lane = lax.broadcasted_iota(jnp.int32, (1, wide), 1) + part * wide
        spread = jnp.concatenate([scan_ref[...]] * (wide // width), 1)
        spread = jnp.where(lane // width == head_ref[0], spread, 0.0)
        low_sum_ref[held : held + 16] = jnp.concatenate([spread, ffn_ref[...]], 0).astype(LOW)
        low_sum_ref[held + 16 :] = jnp.zeros_like(low_sum_ref[held + 16 :])
        leave(1 - slot)
        leave(slot)


def project_back(
    part, parts, x, grads, mids, extra_cols, cols, weights, place, turn, row, begins, head, per, sizes
):
    blocks = place.shape[0]
    rows = 2 * BLOCK
    steps = blocks // 2
    wide = x.shape[2] // parts
    width = grads.shape[2]
    size_z, size_x = sizes
    low_rank = DECAY_RANK + DA + DV + 128
    span = lambda w: pl.BlockSpec((rows, w), lambda i, *_: (steps - 1 - i, 0))
    shape = jax.ShapeDtypeStruct
    held = 3 * width + low_rank + 8
    sums = [shape((held + 16 + -(held + 16) % 16, wide), LOW)]
    if part == 0:
        sums.append(shape((low_rank, width), F32))
    columns, small, up = weights
    assert steps > 1
    return pl.pallas_call(
        functools.partial(project_back_kernel, part, parts),
        grid_spec=pltpu.PrefetchScalarGridSpec(
            num_scalar_prefetch=5,
            grid=(steps,),
            in_specs=[
                block_spec(per, 0, BLOCK, x.shape[2], blocks, True),
                block_spec(per, 1, BLOCK, x.shape[2], blocks, True),
                block_spec(per, -1, 16, x.shape[2], blocks, True),
                pl.BlockSpec((7, rows, width), lambda i, *_: (0, steps - 1 - i, 0)),
            ]
            + [span(m.shape[1]) for m in mids]
            + [
                whole_spec(extra_cols[0]),
                pl.BlockSpec((8, wide), lambda i, *_: (0, part)),
                pl.BlockSpec((cols.shape[0], wide), lambda i, *_: (0, part)),
                pl.BlockSpec((wide, columns.shape[1]), lambda i, *_: (part, 0)),
                pl.BlockSpec((wide, small.shape[1]), lambda i, *_: (part, 0)),
                whole_spec(up),
            ],
            out_specs=[pl.BlockSpec(memory_space=pl.ANY)] * size_x + [whole_spec(s) for s in sums],
            scratch_shapes=[
                pltpu.VMEM((8, wide), F32),
                pltpu.VMEM((held, wide), F32),
                pltpu.VMEM((2, 2, BLOCK, wide), LOW),
                pltpu.SemaphoreType.DMA((2, 2)),
            ],
        ),
        out_shape=[shape((size_z * per, BLOCK, wide), LOW)] * size_x + sums,
        compiler_params=pltpu.CompilerParams(vmem_limit_bytes=56 * 1024 * 1024),
        cost_estimate=work(17000),
    )(
        place, turn, row, begins, head, x, x, x, grads, *mids, *extra_cols, cols, columns, small, up
    )


TALL = BLOCK + 16


def block_keeps(local_ref, begins_ref, j):
    begins = [begins_ref[i] for i in range(begins_ref.shape[0])]
    first = local_ref[j] * BLOCK
    after = jnp.float32(1.0)
    for b in begins:
        after = jnp.where(first + BLOCK == b, 0.0, after)
    return keep_rows(BLOCK, first, begins), after


def middle_kernel(
    per, local_ref, begins_ref, out_ref, tokens_ref, weight_ref, cols_ref, middle_ref, ffn_ref, rows_ref
):
    heads = out_ref.shape[0]
    rows = [jnp.concatenate([out_ref[h, j] for h in range(heads)], 1) for j in range(per)]
    rows = jnp.concatenate(rows, 0)
    rows_ref[...] = rows
    middle = tokens_ref[...].astype(F32) + dot(rows, weight_ref[...], NN)
    middle_ref[...] = middle
    unit, _ = norm_rows(middle)
    normed = unit * cols_ref[16:17] + cols_ref[17:18]
    c18 = cols_ref[18:19]
    extra_row = lax.broadcasted_iota(jnp.int32, (TALL - BLOCK, 1), 0)
    for j in range(per):
        main = normed[j * TALL : j * TALL + BLOCK]
        extra = normed[j * TALL + BLOCK : (j + 1) * TALL]
        keep, keep_after = block_keeps(local_ref, begins_ref, j)
        moved = rows_down(main, extra[0:1]) * keep
        ffn_ref[j * TALL : j * TALL + BLOCK] = (main + (moved - main) * c18).astype(LOW)
        after = extra + (main[BLOCK - 1 :] * keep_after - extra) * c18
        ffn_ref[j * TALL + BLOCK : (j + 1) * TALL] = jnp.where(extra_row == 1, after, 0.0).astype(LOW)


def middle_rows(out, tokens_ext, weight, cols, local, begins):
    _, per, _, _ = out.shape
    wide = weight.shape[0]
    shape = jax.ShapeDtypeStruct
    return pl.pallas_call(
        functools.partial(middle_kernel, per),
        grid_spec=pltpu.PrefetchScalarGridSpec(
            num_scalar_prefetch=2,
            grid=(1,),
            in_specs=[whole_spec(x) for x in (out, tokens_ext, weight, cols)],
            out_specs=[whole_spec(tokens_ext)] * 3,
        ),
        out_shape=[
            shape((per * TALL, wide), F32),
            shape((per * TALL, wide), LOW),
            shape((per * TALL, wide), LOW),
        ],
        compiler_params=pltpu.CompilerParams(vmem_limit_bytes=48 * 1024 * 1024),
        cost_estimate=work(6),
    )(local, begins, out, tokens_ext, weight, cols)


def with_extra(main, extra):
    per = main.shape[0] // BLOCK
    pieces = []
    for j in range(per):
        pieces += [main[j * BLOCK : (j + 1) * BLOCK], extra[j * 16 : (j + 1) * 16]]
    return pieces


def weight_rows_of(ref):
    heads, _, seqs, _, _ = ref.shape
    return jnp.concatenate([ref[h, 0, s] for s in range(seqs) for h in range(heads)], 0)


def channel_kernel(
    xa_ref, xb_ref, ga_ref, gb_ref, ea_ref, eb_ref, key_ref, value_ref, hidden_ref, pre_ref, a_ref, b_ref
):
    rows = xa_ref.shape[0]
    x = jnp.concatenate([xa_ref[...], xb_ref[...]], 0)
    g = jnp.concatenate(with_extra(ga_ref, ea_ref) + with_extra(gb_ref, eb_ref), 0)
    key, value = weight_rows_of(key_ref), weight_rows_of(value_ref)
    active = jnp.maximum(dot(x, key, NN), 0.0)
    hidden_ref[...] = (active * active).astype(LOW)
    grad = (dot(g, value, NN) * 2.0 * active).astype(LOW)
    pre_ref[...] = grad
    back = dot(grad, key, NT)

    @pl.when(pl.program_id(0) == 0)
    def _():
        a_ref[...] = back[:rows]
        b_ref[...] = back[rows:]

    @pl.when(pl.program_id(0) > 0)
    def _():
        a_ref[...] += back[:rows]
        b_ref[...] += back[rows:]


def channel_mix(x, g, extra, weights):
    rows, wide = x[0].shape
    heads, _, seqs, weight_rows, columns = weights.shape
    part = columns // 4

    def weight(which):
        return pl.BlockSpec(
            (heads, 1, seqs, weight_rows, part), lambda i: (0, which, 0, 0, i)
        )

    piece = pl.BlockSpec((2 * rows, part), lambda i: (0, i))
    shape = jax.ShapeDtypeStruct
    return pl.pallas_call(
        channel_kernel,
        grid=(4,),
        in_specs=[whole_spec(a) for a in (*x, *g, *extra)]
        + [weight(0), weight(1)],
        out_specs=[piece, piece, whole_spec(x[0]), whole_spec(x[0])],
        out_shape=[
            shape((2 * rows, columns), LOW),
            shape((2 * rows, columns), LOW),
            shape((rows, wide), F32),
            shape((rows, wide), F32),
        ],
        compiler_params=pltpu.CompilerParams(vmem_limit_bytes=48 * 1024 * 1024),
        cost_estimate=work(8),
    )(*x, *g, *extra, weights, weights)


def main_rows(refs):
    pieces = []
    for ref in refs:
        for start in range(0, ref.shape[0], TALL):
            pieces.append(ref[start : start + BLOCK])
    return jnp.concatenate(pieces, 0)


def channel_grad_kernel(count, *refs):
    og, x = jnp.concatenate([r[...] for r in refs[:count]], 0), main_rows(refs[count : 2 * count])
    hidden, pre = main_rows(refs[2 * count : 2 * count + 2]), main_rows(refs[2 * count + 2 : 2 * count + 4])
    out = refs[2 * count + 4]
    columns = hidden.shape[1]
    out[:, :columns] = dot(og, hidden, TN).astype(LOW)
    out[:, columns : 2 * columns] = dot(x, pre, TN).astype(LOW)


def channel_grads(og, x, hidden, pre, extra):
    wide = og[0].shape[1]
    part = 256
    columns = hidden[0].shape[1]
    return pl.pallas_call(
        functools.partial(channel_grad_kernel, len(og)),
        grid=(wide // part,),
        in_specs=[pl.BlockSpec((a.shape[0], part), lambda i: (0, i)) for a in (*og, *x)]
        + [whole_spec(h) for h in (*hidden, *pre)],
        out_specs=pl.BlockSpec((part, 2 * columns + extra), lambda i: (i, 0)),
        out_shape=jax.ShapeDtypeStruct((wide, 2 * columns + extra), LOW),
        compiler_params=pltpu.CompilerParams(vmem_limit_bytes=48 * 1024 * 1024),
        cost_estimate=work(9),
    )(*og, *x, *hidden, *pre)


def output_grad_kernel(count, which_ref, *refs):
    rows, grads, out = refs[:count], refs[count : 2 * count], refs[-1]
    left = jnp.concatenate([r[...] for r in rows], 0)
    right = jnp.concatenate([r[...] for r in grads], 0)
    out[...] = dot(left, right, TN).astype(LOW)


def output_grads(rows, grads, which, room):
    tall, wide = rows[0].shape
    part = 256
    last = room.shape[1] // part - 1
    return pl.pallas_call(
        functools.partial(output_grad_kernel, len(rows)),
        grid_spec=pltpu.PrefetchScalarGridSpec(
            num_scalar_prefetch=1,
            grid=(wide // part,),
            in_specs=[pl.BlockSpec((tall, part), lambda i, w: (0, i))] * len(rows)
            + [pl.BlockSpec((tall, part), lambda i, w: (0, w[0]))] * len(grads)
            + [pl.BlockSpec(memory_space=pl.ANY)],
            out_specs=pl.BlockSpec((part, part), lambda i, w: (i, last)),
        ),
        out_shape=jax.ShapeDtypeStruct(room.shape, LOW),
        input_output_aliases={2 * len(rows) + 1: 0},
        compiler_params=pltpu.CompilerParams(vmem_limit_bytes=48 * 1024 * 1024),
        cost_estimate=work(2),
    )(which, *rows, *grads, room)


def middle_back_kernel(
    per, local_ref, begins_ref, near_ref, core_ref, far_ref, middle_ref, og_ref, weight_ref, cols_ref,
    grad_ref, low_ref, heads_ref, sums_ref,
):
    c16, c17, c18 = [cols_ref[i : i + 1] for i in (16, 17, 18)]
    grad_in = near_ref[...] + core_ref[...] + far_ref[...].astype(F32)
    sums = [jnp.zeros((1, c16.shape[1]), F32) for _ in range(3)]
    lows = []
    for j in range(per):
        start = j * TALL
        grad, after = grad_in[start : start + BLOCK], grad_in[start + BLOCK + 1 : start + BLOCK + 2]
        keep, keep_after = block_keeps(local_ref, begins_ref, j)
        ahead = rows_up(grad * keep, after * keep_after)
        grad_normed = grad + (ahead - grad) * c18
        unit, scale = norm_rows(middle_ref[start : start + BLOCK])
        prior, _ = norm_rows(middle_ref[start + BLOCK : start + TALL])
        normed = unit * c16 + c17
        diff = rows_down(normed, prior[0:1] * c16 + c17) * keep - normed
        for i, value in enumerate((grad_normed * unit, grad_normed, grad * diff)):
            sums[i] = sums[i] + jnp.sum(value, 0, keepdims=True)
        og = og_ref[j * BLOCK : (j + 1) * BLOCK].astype(F32)
        total = og + norm_back(grad_normed, unit, scale, c16)
        grad_ref[j * BLOCK : (j + 1) * BLOCK] = total
        lows.append(total.astype(LOW))
        low_ref[start : start + BLOCK] = lows[-1]
        low_ref[start + BLOCK : start + TALL] = jnp.zeros((TALL - BLOCK, c16.shape[1]), LOW)
    sums_ref[...] = jnp.concatenate(sums + [jnp.zeros((5, c16.shape[1]), F32)], 0)
    out = dot(jnp.concatenate(lows, 0), weight_ref[...], NT).astype(LOW)
    width = heads_ref.shape[2]
    for h in range(heads_ref.shape[0]):
        heads_ref[h] = out[:, h * width : (h + 1) * width]


def norm_back(grad, unit, scale, gain):
    grad = grad * gain
    return scale * (
        grad - jnp.mean(grad, -1, keepdims=True) - unit * jnp.mean(grad * unit, -1, keepdims=True)
    )


def middle_back(near, core, far, middle, og, weight, cols, local, begins, heads):
    tall, wide = near.shape
    per = tall // TALL
    shape = jax.ShapeDtypeStruct
    outs = [
        shape((per * BLOCK, wide), F32),
        shape((tall, wide), LOW),
        shape((heads, per * BLOCK, wide // heads), LOW),
        shape((8, wide), F32),
    ]
    operands = (near, core, far, middle, og, weight, cols)
    return pl.pallas_call(
        functools.partial(middle_back_kernel, per),
        grid_spec=pltpu.PrefetchScalarGridSpec(
            num_scalar_prefetch=2,
            grid=(1,),
            in_specs=[whole_spec(x) for x in operands],
            out_specs=[whole_spec(x) for x in outs],
        ),
        out_shape=outs,
        compiler_params=pltpu.CompilerParams(vmem_limit_bytes=48 * 1024 * 1024),
        cost_estimate=work(8),
    )(local, begins, *operands)


HEAD_AXES = ("hz", "hx")


def all_gather(x, axes):
    return lax.all_gather(x, axes, axis=0, tiled=True)


def steps_along(x, axis):
    size = lax.axis_size(axis)
    return [lax.ppermute(x, axis, [(i, i ^ k) for i in range(size)]) for k in range(1, size)]


def grown(x, axis):
    return jnp.concatenate([x] + steps_along(x, axis), 0)


def in_order(x, axes):
    strides, stride = {}, 1
    for axis in axes:
        strides[axis] = stride
        stride *= lax.axis_size(axis)
    index = jnp.arange(stride, dtype=jnp.int32)
    place, below = jnp.zeros((), jnp.int32), stride
    for axis in ("ys", "core") + HEAD_AXES:
        if axis in axes:
            below //= lax.axis_size(axis)
            there = (index // below) % lax.axis_size(axis)
            place = place + (there ^ lax.axis_index(axis)) * strides[axis]
    x = taken_blocks(x, place)
    return x.reshape((x.shape[0] * x.shape[1],) + x.shape[2:])


def swap(x, axis):
    return lax.ppermute(x, axis, [(0, 1), (1, 0)])


def seq_gather(x):
    if lax.axis_size("ys") != 2:
        return list(lax.all_gather(x, ("ys", "core"), axis=0))
    far = swap(x, "ys")
    return [x, swap(x, "core"), far, swap(far, "core")]


def seq_return(near, core, far, diagonal):
    return swap(core, "core"), swap((far + swap(diagonal, "core")).astype(LOW), "ys")


def seq_step(x, axis):
    if lax.axis_size("ys") != 2:
        if axis == "ys":
            return x
        return lax.psum_scatter(x, ("ys", "core"), scatter_dimension=0, tiled=True)[0].astype(F32)
    if axis == "ys":
        x = x.reshape((2, 2) + x.shape[1:])
    index = lax.axis_index(axis)
    sent = swap(lax.dynamic_index_in_dim(x, 1 - index, 0, keepdims=False).astype(LOW), axis)
    return lax.dynamic_index_in_dim(x, index, 0, keepdims=False).astype(F32) + sent.astype(F32)


def taken_blocks(x, table):
    return x.at[table].get(mode="promise_in_bounds")


def start_flags(positions, begins):
    return jnp.any(positions[..., None] == begins, -1).astype(F32)


def body(
    tokens,
    leading_layer_value,
    output_gradient,
    lengths,
    sequence_block_of,
    stored_block_of,
    channel_settings,
    receptance_matrix,
    key_matrix,
    value_matrix,
    output_matrix,
    branch_down_weight,
    branch_up_weight,
    channel_key_weight,
    channel_value_weight,
):
    rows_here, wide = tokens.shape
    per = rows_here // BLOCK
    ys, heads_axis = lax.axis_size("ys"), lax.axis_size("hz") * lax.axis_size("hx")
    seqs = 2 * ys
    head = lax.axis_index(HEAD_AXES)
    core = lax.axis_index("core")
    width = wide // heads_axis
    weight_rows = receptance_matrix.shape[0]
    low_rank = branch_down_weight.shape[1]
    order, home = sequence_block_of[0], stored_block_of[0]
    blocks = order.shape[0]
    begins = (jnp.cumsum(lengths[0]) - lengths[0]).astype(jnp.int32)
    splits = (DECAY_RANK, DECAY_RANK + DA, DECAY_RANK + DA + DV)

    og_first = output_gradient.reshape(per, BLOCK, wide)[:, 0]
    place = home
    size_z, size_x = lax.axis_size("hz"), lax.axis_size("hx")
    apart = (home // per) ^ head
    turn_x, turn_row = apart % size_x, (apart // size_x) * per + home % per
    local = lax.dynamic_slice_in_dim(order, head * per, per)
    group = all_gather(tokens[None], HEAD_AXES)
    og_rows = in_order(grown(grown(og_first[None], "hz"), "hx"), HEAD_AXES)
    og_parts = seq_gather(output_gradient)

    quarter = channel_key_weight.shape[1] // seqs
    pair = jnp.stack([channel_key_weight, channel_value_weight], 0).reshape(2, weight_rows, seqs, quarter)
    pair = lax.all_to_all(
        pair.transpose(2, 0, 1, 3), ("ys", "core"), split_axis=0, concat_axis=0, tiled=True
    )
    columns = (
        jnp.stack([receptance_matrix, key_matrix, value_matrix], 1)
        .reshape(weight_rows * 3, heads_axis, width)
        .transpose(1, 0, 2)
    )
    columns = lax.all_to_all(columns, HEAD_AXES, split_axis=0, concat_axis=0, tiled=True)
    def rank_columns(weight):
        return jnp.split(weight, (DECAY_RANK + DA, DECAY_RANK + DA + DV), 1)

    (down_pair, down_value, down_gate), (up_pair, up_value, up_gate) = [
        rank_columns(w) for w in (branch_down_weight, branch_up_weight)
    ]
    count = channel_settings.shape[1]
    blank = [jnp.zeros((weight_rows, n), LOW) for n in (32 - count, 32)]
    small = jnp.concatenate(
        [
            down_pair, down_gate, down_value, channel_settings, blank[0], up_value, blank[1],
            up_pair, up_gate,
        ],
        1,
    )[None]
    for axis in HEAD_AXES + ("ys", "core"):
        small = grown(small, axis)
    small = in_order(small, HEAD_AXES + ("ys", "core"))
    columns = columns.reshape(1, heads_axis * weight_rows, 3 * width)
    columns = in_order(grown(grown(columns, "ys"), "core"), ("ys", "core"))
    settings = small[:, 256 + DV : 256 + DV + count].astype(F32).T
    up = lax.dynamic_slice_in_dim(small, head * width, width, 0)
    own = lax.dynamic_slice_in_dim(settings, head * width, width, 1)
    own = jnp.concatenate([own[13:16], own[8:13]], 0)
    out_shards = grown(grown(output_matrix[None], "hz"), "hx")
    columns, small, settings, up, own, og_parts, pair, first_sent, out_shards = (
        lax.optimization_barrier(
            (
                columns, small, settings, up, own, og_parts, pair, leading_layer_value, out_shards,
            )
        )
    )
    first_group = lax.all_to_all(
        first_sent.reshape(rows_here, heads_axis, width).transpose(1, 0, 2),
        HEAD_AXES, split_axis=0, concat_axis=0, tiled=True,
    ).reshape(blocks, BLOCK, width)
    weights = [columns, small, up]

    out_shards = grown(out_shards, "ys")

    def gathered(half):
        return all_gather(half[None], HEAD_AXES).transpose(1, 0, 2, 3)

    whole_quarter = quarter == wide
    if whole_quarter:
        every = all_gather(pair.transpose(1, 0, 2, 3).reshape(1, -1, weight_rows, wide), HEAD_AXES)
    else:
        every = (gathered(pair[:, 0]), gathered(pair[:, 1]))

    ends, parts, gate, pre, *mids = project(group, settings, own, weights, place, begins, per)
    parts, out_shards = lax.optimization_barrier((parts, out_shards))
    out_shards = grown(out_shards, "core")
    values, out_in, joined, scanned, states, mats = scan_forward(
        parts, pre, first_group, gate, own, home, begins, PASSES
    )

    before, follow = jnp.maximum(order - 1, 0), jnp.minimum(order + 1, blocks - 1)
    in_blocks = out_in.reshape(blocks, BLOCK, width)
    extended = jnp.concatenate(
        [
            taken_blocks(in_blocks, order),
            taken_blocks(in_blocks[:, BLOCK - 1], before)[:, None],
            taken_blocks(in_blocks[:, 0], follow)[:, None],
            jnp.zeros((blocks, 14, width), LOW),
        ],
        1,
    )
    extended, out_shards, ends, og_rows = lax.optimization_barrier((extended, out_shards, ends, og_rows))
    out_ext = lax.all_to_all(
        extended.reshape(heads_axis, per, TALL, width), HEAD_AXES, split_axis=0, concat_axis=0, tiled=True
    )
    out_weight = in_order(out_shards, HEAD_AXES + ("ys", "core"))
    local = lax.dynamic_slice_in_dim(order, head * per, per)
    after_seq = local + 1
    after_live = (after_seq < blocks).astype(LOW)[:, None]
    after = jnp.minimum(after_seq, blocks - 1)
    row_before = taken_blocks(ends, jnp.maximum(local - 1, 0))[:, 31]
    row_after = taken_blocks(ends, after)[:, 0]
    og_after = taken_blocks(og_rows, taken_blocks(home, after)) * after_live
    none = jnp.zeros((per, 14, wide), LOW)
    extra_parts = seq_gather(jnp.concatenate([none[:, :1], og_after[:, None], none], 1).reshape(-1, wide))
    out_ext, out_weight = lax.optimization_barrier((out_ext, out_weight))
    tokens_b = tokens.reshape(per, BLOCK, wide)
    tokens_ext = jnp.concatenate([tokens_b, row_before[:, None], row_after[:, None], none], 1)
    middle, ffn_in, out_rows = middle_rows(
        out_ext, tokens_ext.reshape(-1, wide), out_weight, settings, local, begins
    )
    ffn_in, every = lax.optimization_barrier((ffn_in, every))
    if whole_quarter:
        every = every.reshape(heads_axis, 2, seqs, weight_rows, wide)
        value_part = every[:, 1].transpose(1, 0, 2, 3).reshape(wide, wide)
        ffn_parts = [ffn_in, swap(ffn_in, "core"), swap(ffn_in, "ys")]
        *near, own_part, core_part = channel_mix(ffn_parts[:2], og_parts[:2], extra_parts[:2], every)
        ffn_parts[2], near, own_part, core_part, out_rows = lax.optimization_barrier(
            (ffn_parts[2], near, own_part, core_part, out_rows)
        )
        ffn_parts.append(swap(ffn_parts[2], "core"))
        *far, far_part, diagonal = channel_mix(ffn_parts[2:], og_parts[2:], extra_parts[2:], every)
        came_core, came_far = seq_return(own_part, core_part, far_part, diagonal)
        grads_here = channel_grads(
            og_parts, ffn_parts, (near[0], far[0]), (near[1], far[1]), wide // seqs
        )
        came_far, grads_here = lax.optimization_barrier((came_far, grads_here))
        hidden = [near[0], far[0]]
    else:
        key_part, value_part = [x.reshape(wide, quarter) for x in every]
        ffn_parts = seq_gather(ffn_in)
        rows = jnp.concatenate(ffn_parts, 0)
        og_rows = jnp.concatenate(
            [
                jnp.concatenate([g.reshape(per, BLOCK, wide), x.reshape(per, 16, wide)], 1).reshape(-1, wide)
                for g, x in zip(og_parts, extra_parts)
            ],
            0,
        )
        active = jax.nn.relu(dot(rows, key_part, NN))
        hidden = [(active * active).astype(LOW)]
        grad_pre = (dot(og_rows, value_part, NN) * 2.0 * active).astype(LOW)
        own_part = dot(grad_pre, key_part, NT).reshape(seqs, per * TALL, wide)
        own_part = lax.psum_scatter(own_part, ("ys", "core"), scatter_dimension=0, tiled=True)[0]
        came_core, came_far = jnp.zeros_like(own_part), jnp.zeros_like(ffn_in)
        is_main = (jnp.arange(rows.shape[0]) % TALL < BLOCK).astype(LOW)[:, None]
        grads_here = [dot(og_rows * is_main, hidden[0], TN), dot(rows * is_main, grad_pre, TN)]
    grad_middle, middle_low, grad_out, cols_ffn = middle_back(
        own_part, came_core, came_far, middle, output_gradient, out_weight, settings, local, begins, heads_axis
    )
    grad_heads = lax.all_to_all(grad_out, HEAD_AXES, split_axis=0, concat_axis=0, tiled=True)
    out_parts, low_parts = seq_gather(out_rows), seq_gather(middle_low)
    which = lax.axis_index(("ys", "core"))
    if whole_quarter:
        grads_here = output_grads(out_parts, low_parts, which[None], grads_here)
    else:
        right = jnp.concatenate(low_parts, 0).reshape(seqs * per * TALL, seqs, -1)
        right = lax.dynamic_index_in_dim(right, which, 1, keepdims=False)
        grads_here.append(dot(jnp.concatenate(out_parts, 0), right, TN))
        grads_here = jnp.concatenate(grads_here, 1).astype(LOW)
    grad_heads, grads_here = lax.optimization_barrier((grad_heads, grads_here))
    grads_here = lax.psum_scatter(grads_here, HEAD_AXES, scatter_dimension=0, tiled=True)

    scan_grads, first_grad, cols_scan = scan_backward(
        parts, values, joined, scanned, gate, grad_heads.reshape(blocks, BLOCK, width), pre, first_group,
        own, states, mats, home, begins, PASSES,
    )
    first_grad = taken_blocks(first_grad.reshape(blocks, BLOCK, width), order)
    first_value_grad = lax.all_to_all(
        first_grad.reshape(heads_axis, rows_here, width), HEAD_AXES, split_axis=0, concat_axis=2, tiled=True
    ).reshape(rows_here, wide).astype(F32)

    share = wide // seqs
    thin = low_rank // seqs
    fold = heads_axis // seqs

    def over_ys(left, right, up_sums):
        up_sums = up_sums.astype(LOW).reshape(seqs, thin, width)
        if ys != 2:
            rows_out = jnp.concatenate([left, right], 1)
            return rows_out.reshape(-1, seqs, share).transpose(1, 0, 2), up_sums
        index = lax.axis_index("ys")
        came = swap(jnp.where(index == 0, right, left), "ys")
        total = jnp.where(index == 0, left, right).astype(F32) + came.astype(F32)
        return total.reshape(-1, 2, share), seq_step(up_sums, "ys")

    def over_core(rows_out, up_sums):
        if ys != 2:
            return [
                lax.psum_scatter(x, ("ys", "core"), scatter_dimension=0, tiled=True)[0].astype(F32)
                for x in (rows_out, up_sums)
            ]
        sent = lax.dynamic_index_in_dim(rows_out, 1 - core, 1, keepdims=False).astype(LOW)
        kept_rows = lax.dynamic_index_in_dim(rows_out, core, 1, keepdims=False)
        return kept_rows + swap(sent, "core").astype(F32), seq_step(up_sums, "core")

    def to_owners(rows_out):
        rows_low = rows_out.astype(LOW)
        squares = rows_low[: 3 * width].reshape(3 * width, fold, width)
        mixed = rows_low[3 * width : 3 * width + low_rank].reshape(seqs, thin, fold, width)
        mixed = mixed.transpose(0, 2, 1, 3).reshape(heads_axis, thin, width)
        cols_part = rows_low[3 * width + low_rank :][:count].reshape(count, heads_axis, -1)
        cols_part = jnp.pad(
            cols_part.transpose(1, 0, 2), ((0, 0), (0, -count % 8), (0, width - cols_part.shape[2]))
        )
        mixed = lax.all_to_all(
            jnp.concatenate([mixed, cols_part], 1), HEAD_AXES, split_axis=0, concat_axis=0, tiled=True
        )
        came = []
        for k in range(fold):
            sent = lax.dynamic_index_in_dim(squares, (head + k) % fold, 1, keepdims=False)
            came.append(
                lax.ppermute(
                    sent, every_axis, [(q * heads_axis + h, owner(q, h, (h + k) % fold)) for q, h in pairs]
                )
            )
        return mixed, came

    every_axis = ("ys", "core") + HEAD_AXES
    pairs = [(q, h) for q in range(seqs) for h in range(heads_axis)]

    def owner(q, h, j):
        return (h // fold) * heads_axis + q * fold + j

    sizes = (size_z, size_x)

    def others_x(blocks_back):
        return [
            lax.ppermute(blocks_back[k], "hx", [(i, i ^ k) for i in range(size_x)])
            for k in range(1, size_x)
        ]

    def after_x(kept_blocks, came):
        total = kept_blocks.astype(F32)
        for x in came:
            total = total + x.astype(F32)
        total = total.reshape(size_z, rows_here, -1)
        return total[0], [total[k].astype(LOW) for k in range(1, size_z)]

    def others_z(sent):
        return [
            lax.ppermute(x, "hz", [(i, i ^ k) for i in range(size_z)]) for k, x in enumerate(sent, 1)
        ]

    def half_back(part, grads):
        outs = project_back(
            part, 2, group, grads, mids, (cols_scan, cols_ffn), settings, weights, place, turn_x, turn_row,
            begins, head[None], per, sizes,
        )
        return outs[:size_x], outs[size_x:]

    left_blocks, (left_sum, up_sums) = half_back(0, scan_grads)
    left_came = others_x(left_blocks)
    scan_grads, left_sum = lax.optimization_barrier((scan_grads, left_sum))
    right_blocks, (right_sum,) = half_back(1, scan_grads)
    right_blocks, left_came, right_sum, first_value_grad = lax.optimization_barrier(
        (right_blocks, left_came, right_sum, first_value_grad)
    )
    right_came = others_x(right_blocks)
    left_own, left_sent = after_x(left_blocks[0], left_came)
    left_sent, right_sum, hidden = lax.optimization_barrier((left_sent, right_sum, hidden))
    left_z = others_z(left_sent)
    rows_out, up_sums = over_ys(left_sum, right_sum, up_sums)
    outs = [dot(h, value_part, NT) for h in hidden]
    right_came, outs, grads_here = lax.optimization_barrier((right_came, outs, grads_here))
    right_own, right_sent = after_x(right_blocks[0], right_came)
    right_sent, left_z, rows_out, up_sums, outs = lax.optimization_barrier(
        (right_sent, left_z, rows_out, up_sums, outs)
    )
    right_z = others_z(right_sent)
    rows_out, up_sums = over_core(rows_out, up_sums)
    mixed, came = to_owners(rows_out)
    if whole_quarter:
        came_core, came_far = seq_return(*[x for out in outs for x in jnp.split(out, 2, 0)])
        right_z, came_core, came_far = lax.optimization_barrier((right_z, came_core, came_far))
    right_z, up_sums, mixed, came = lax.optimization_barrier((right_z, up_sums, mixed, came))
    back = jnp.concatenate(
        [own + sum(x.astype(F32) for x in z) for own, z in ((left_own, left_z), (right_own, right_z))], 1
    )
    value_sum, key_sum, out_sum = jnp.split(grads_here.astype(F32), (quarter, 2 * quarter), 1)

    unit, scale = norm_rows(tokens.astype(F32))
    tokens_grad = grad_middle + norm_back(back, unit, scale, settings[0])
    mixed = jnp.sum(mixed.astype(F32), 0)
    channel_grad = mixed[thin : thin + count, :weight_rows].T
    down_grad = lax.ppermute(
        mixed[:thin].astype(LOW), every_axis, [(q * heads_axis + h, owner(q, h, h % fold)) for q, h in pairs]
    ).T.astype(F32)

    def main_of(x):
        return x.reshape(-1, per, TALL, wide)[:, :, :BLOCK].reshape(-1, rows_here, wide)

    layer_out = main_of(middle)[0]
    if whole_quarter:
        own_out = jnp.split(outs[0], 2, 0)[0]
        layer_out = layer_out + main_of(own_out)[0] + main_of(came_core)[0] + main_of(came_far)[0].astype(F32)
    else:
        layer_out = layer_out + lax.psum_scatter(
            main_of(outs[0]), ("ys", "core"), scatter_dimension=0, tiled=True
        )[0]
    came = jnp.stack(came, 0)
    came = taken_blocks(came, (head - jnp.arange(fold, dtype=jnp.int32)) % fold)
    came = came.reshape(fold, 3, width, width).transpose(1, 3, 0, 2).reshape(3, width, share)
    recept_grad, key_grad, value_grad = [came[i].astype(F32) for i in range(3)]
    up_grad = up_sums.T
    return (
        layer_out.astype(LOW),
        tokens_grad,
        first_value_grad,
        channel_grad,
        recept_grad,
        key_grad,
        value_grad,
        out_sum,
        down_grad,
        up_grad,
        key_sum,
        value_sum,
    )


def solution(mesh):
    seqs, heads = mesh.devices.shape
    split = Mesh(mesh.devices.reshape(seqs // 2, 2, 4, heads // 4), ("ys", "core") + HEAD_AXES)
    rows = P(("ys", "core") + HEAD_AXES, None)
    table = P(("ys", "core"), None)
    square = P(HEAD_AXES, ("ys", "core"))
    return jax.shard_map(
        body,
        mesh=split,
        in_specs=(rows,) * 3 + (table,) * 3 + (rows,) * 9,
        out_specs=(rows,) * 4 + (square,) * 8,
        check_vma=False,
    )
```

```python
import functools
import jax
import jax.numpy as jnp
from jax import lax
from jax.experimental import pallas as pl
from jax.experimental.pallas import tpu as pltpu
from jax.sharding import Mesh
from jax.sharding import PartitionSpec as P

DECAY_RANK = 64
DA = 64
DV = 32
BLOCK = 128
SPAN = 64
HEAD = 64
FORWARD_CHUNKS = 8
BACKWARD_CHUNKS = 4
LOW = jnp.bfloat16
F32 = jnp.float32
NN = (((1,), (0,)), ((), ()))
NT = (((1,), (1,)), ((), ()))
TN = (((0,), (0,)), ((), ()))
PASSES = {"pair": 3, "inv": 3, "val": 3, "chain": 3, "bpair": 3}


def work(micros):
    return pl.CostEstimate(flops=0, bytes_accessed=int(micros * 3_000), transcendentals=0)


def dot(a, b, dims):
    return lax.dot_general(a, b, dims, preferred_element_type=F32)


def halves(x):
    high = x.astype(LOW)
    return high, (x - high.astype(F32)).astype(LOW)


def product(a, b, dims, passes):
    if passes == 1:
        return dot(a.astype(LOW), b.astype(LOW), dims)
    la, lb = dims[0][0][0], dims[0][1][0]
    a_high, a_low = halves(a)
    if passes == 2:
        b = b.astype(LOW)
        return dot(jnp.concatenate([a_high, a_low], la), jnp.concatenate([b, b], lb), dims)
    b_high, b_low = halves(b)
    first = dot(jnp.concatenate([a_high, a_low], la), jnp.concatenate([b_high, b_high], lb), dims)
    return first + dot(a_high, b_low, dims)


def head_masks(heads):
    lane = lax.broadcasted_iota(jnp.int32, (1, heads * HEAD), 1) // HEAD
    return [(lane == h).astype(F32) for h in range(heads)]


def stacked(x, masks):
    if len(masks) == 1:
        return x
    return jnp.concatenate([x * m for m in masks], 0)


def unstacked(x, heads):
    rows = x.shape[0] // heads
    out = x[:rows]
    for h in range(1, heads):
        out = out + x[h * rows : (h + 1) * rows]
    return out


def head_ones(width):
    row = lax.broadcasted_iota(jnp.int32, (width, width), 0) // HEAD
    col = lax.broadcasted_iota(jnp.int32, (width, width), 1) // HEAD
    return (row == col).astype(LOW)


def head_sum(x, ones):
    high, low = halves(x)
    return dot(jnp.concatenate([high, low], 1), jnp.concatenate([ones, ones], 0), NN)


class Chunk:
    def __init__(self, r, lw, k, kn, a, begins, start, heads):
        self.heads = heads
        masks = head_masks(heads)
        rows = heads * SPAN
        local = [jnp.where(b >= start, b - start, SPAN) for b in begins]
        row_t = lax.broadcasted_iota(jnp.int32, (rows, 1), 0) % SPAN
        col_t = lax.broadcasted_iota(jnp.int32, (1, rows), 1) % SPAN
        row_seg = sum((row_t >= b).astype(jnp.int32) for b in local)
        col_seg = sum((col_t >= b).astype(jnp.int32) for b in local)
        last = sum((b < SPAN).astype(jnp.int32) for b in local)
        same = row_seg == col_seg
        self.strict = same & (row_t > col_t)
        self.upto = same & (row_t >= col_t)
        self.carried = (row_seg == 0).astype(F32)
        self.final = (row_seg == last).astype(F32)
        self.whole = (last == 0).astype(F32)
        tri_r = lax.broadcasted_iota(jnp.int32, (SPAN, SPAN), 0)
        tri_c = lax.broadcasted_iota(jnp.int32, (SPAN, SPAN), 1)
        running = dot((tri_r >= tri_c).astype(LOW), lw, NN)
        lw = lw.astype(F32)
        decay = jnp.exp(running)
        before = jnp.exp(running - lw)
        inverse = jnp.exp(-running)
        end = running[SPAN - 1 : SPAN]
        to_end = jnp.exp(end - running)
        self.end = jnp.exp(end)
        kn = kn.astype(F32)
        beta = kn * a.astype(F32)
        k = k.astype(F32)
        self.decay, self.before, self.inverse, self.to_end = decay, before, inverse, to_end
        self.a_hat = stacked(-kn * before, masks)
        self.r_hat = stacked(r.astype(F32) * decay, masks)
        self.b_hat = stacked(beta * inverse, masks)
        self.k_hat = stacked(k * inverse, masks)
        self.b_end = stacked(beta * to_end, masks) * self.final
        self.k_end = stacked(k * to_end, masks) * self.final


def block_inverses(all_pairs, passes):
    rows = all_pairs[0].shape[0]
    row = lax.broadcasted_iota(jnp.int32, (rows, rows), 0)
    col = lax.broadcasted_iota(jnp.int32, (rows, rows), 1)
    eye = (row == col).astype(F32)

    def products(left, right):
        return [product(a, b, NN, passes) for a, b in zip(left, right)]

    within = row // 8 == col // 8
    small = [jnp.where(within, pairs, 0.0) for pairs in all_pairs]
    square = products(small, small)
    fourth = products(square, square)
    first = [eye + x for x in small]
    inverse = [a + b for a, b in zip(first, products(first, square))]
    inverse = [a + b for a, b in zip(inverse, products(inverse, fourth))]
    size = 8
    while size < SPAN:
        within = (row // (2 * size) == col // (2 * size)) & (row // size != col // size)
        cross = [jnp.where(within, pairs, 0.0) for pairs in all_pairs]
        step = products(products(inverse, cross), inverse)
        inverse = [a + b for a, b in zip(inverse, step)]
        size *= 2
    return inverse


def group_norm_parts(scanned, ones):
    center = scanned - head_sum(scanned, ones) * (1.0 / HEAD)
    spread = head_sum(center * center, ones) * (1.0 / HEAD)
    scale = lax.rsqrt(spread + 0.00064)
    return center * scale, scale


def scan_forward_kernel(
    heads, p, home_ref, begins_ref, parts_ref, pre_ref, gate_ref, cols_ref, *rest,
):
    first_refs, rest = rest[: FORWARD_CHUNKS * SPAN // BLOCK], rest[FORWARD_CHUNKS * SPAN // BLOCK :]
    values_ref, out_ref, joined_ref, scanned_ref, state_ref, mats_ref, state = rest
    step = pl.program_id(0)
    width = heads * HEAD

    @pl.when(step == 0)
    def _():
        state[...] = jnp.zeros_like(state)

    begins = [begins_ref[i] for i in range(begins_ref.shape[0])]
    masks = head_masks(heads)
    n = heads * SPAN
    eye = (
        lax.broadcasted_iota(jnp.int32, (width, width), 0)
        == lax.broadcasted_iota(jnp.int32, (width, width), 1)
    ).astype(F32)
    first = jnp.concatenate([ref[0] for ref in first_refs], 0).astype(F32)
    mix = jax.nn.sigmoid(cols_ref[5:6] + pre_ref[4])
    values = (pre_ref[1] + (first - pre_ref[1]) * mix).astype(LOW)
    values_ref[...] = values
    held = []
    for c in range(FORWARD_CHUNKS):
        rows = pl.ds(c * SPAN, SPAN)
        r, lw, k, kn, a = [parts_ref[i, rows] for i in range(5)]
        v = values[c * SPAN : (c + 1) * SPAN]
        q = Chunk(r, lw, k, kn, a, begins, (step * FORWARD_CHUNKS + c) * SPAN, heads)
        v_st = stacked(v.astype(F32), masks).astype(LOW)
        held.append((q, r, k, v, v_st))
    all_pairs = [
        product(
            jnp.concatenate([q.a_hat, q.r_hat], 0), jnp.concatenate([q.b_hat, q.k_hat], 0), NT, p["pair"]
        )
        for q, *_ in held
    ]
    l_ab = [jnp.where(h[0].strict, x[:n, :n], 0.0) for h, x in zip(held, all_pairs)]
    l_ak = [jnp.where(h[0].strict, x[:n, n:], 0.0) for h, x in zip(held, all_pairs)]
    l_rb = [jnp.where(h[0].upto, x[n:, :n], 0.0) for h, x in zip(held, all_pairs)]
    l_rk = [jnp.where(h[0].upto, x[n:, n:], 0.0) for h, x in zip(held, all_pairs)]
    both_v = [
        product(jnp.concatenate([ak, rk], 0), h[4], NN, 2 if p["val"] == 3 else 1)
        for ak, rk, h in zip(l_ak, l_rk, held)
    ]
    inverses = block_inverses(l_ab, p["inv"])
    solved = [
        product(t, jnp.concatenate([h[0].a_hat * h[0].carried, b[:n]], 1), NN, p["val"])
        for t, h, b in zip(inverses, held, both_v)
    ]
    ends = [product(x, h[0].b_end, TN, p["val"]) for x, h in zip(solved, held)]
    grown = []
    for q, _, _, _, v_st in held:
        if p["val"] == 3:
            k_high, k_low = halves(q.k_end)
            grown.append(dot(jnp.concatenate([v_st, v_st], 0), jnp.concatenate([k_high, k_low], 0), TN))
        else:
            grown.append(dot(v_st, q.k_end.astype(LOW), TN))
    ready = []
    for c in range(FORWARD_CHUNKS):
        q, r, k, v, _ = held[c]
        through = product(l_rb[c], solved[c], NN, p["val"])
        r_thru = q.r_hat * q.carried + through[:, :width]
        o_val = both_v[c][n:] + through[:, width:]
        move = eye * (q.end * q.whole) + ends[c][:width]
        gain = ends[c][width:] + grown[c]
        mats = [
            inverses[c], l_ak[c], l_rb[c], l_rk[c], solved[c][:, :width], solved[c][:, width:], move, r_thru,
        ]
        for i, m in enumerate(mats):
            mats_ref[c, i] = m
        ready.append((move, gain, r_thru, o_val, r, k, v))
    ones = head_ones(width)
    now = state[...]
    begun = []
    for c in range(FORWARD_CHUNKS):
        begun.append(now)
        state_ref[c] = now
        now = product(now, ready[c][0], NN, p["chain"]) + ready[c][1]
    state[...] = now
    for c in range(FORWARD_CHUNKS):
        rows = pl.ds(c * SPAN, SPAN)
        _, _, r_thru, o_val, r, k, v = ready[c]
        scanned = unstacked(o_val + product(r_thru, begun[c], NT, p["val"]), heads)
        scanned_ref[rows] = scanned
        unit, _ = group_norm_parts(scanned, ones)
        bonus = head_sum(r.astype(F32) * k.astype(F32) * cols_ref[0:1], ones)
        joined = unit * cols_ref[1:2] + cols_ref[2:3] + bonus * v.astype(F32)
        joined = joined.astype(LOW)
        joined_ref[rows] = joined
        out_ref[rows] = (joined.astype(F32) * gate_ref[rows]).astype(LOW)


def scan_forward(parts, pre, first, gate, cols, home, begins, p):
    _, total, width = parts.shape
    heads = width // HEAD
    rows = FORWARD_CHUNKS * SPAN
    n = heads * SPAN
    spans = total // SPAN
    assert n == width
    row_spec = pl.BlockSpec((rows, width), lambda i, *_: (i, 0))
    per_step = rows // BLOCK

    def stored(which):
        return pl.BlockSpec((1, BLOCK, width), lambda i, home, b: (home[per_step * i + which], 0, 0))

    return pl.pallas_call(
        functools.partial(scan_forward_kernel, heads, p),
        grid_spec=pltpu.PrefetchScalarGridSpec(
            num_scalar_prefetch=2,
            grid=(total // rows,),
            in_specs=[
                pl.BlockSpec((5, rows, width), lambda i, *_: (0, i, 0)),
                pl.BlockSpec((5, rows, width), lambda i, *_: (0, i, 0)),
                row_spec,
                pl.BlockSpec(cols.shape, lambda i, *_: (0, 0)),
            ]
            + [stored(w) for w in range(per_step)],
            out_specs=[
                row_spec,
                row_spec,
                row_spec,
                row_spec,
                pl.BlockSpec((FORWARD_CHUNKS, width, width), lambda i, *_: (i, 0, 0)),
                pl.BlockSpec((FORWARD_CHUNKS, 8, n, width), lambda i, *_: (i, 0, 0, 0)),
            ],
            scratch_shapes=[pltpu.VMEM((width, width), F32)],
        ),
        out_shape=[
            jax.ShapeDtypeStruct((total, width), LOW),
            jax.ShapeDtypeStruct((total, width), LOW),
            jax.ShapeDtypeStruct((total, width), LOW),
            jax.ShapeDtypeStruct((total, width), F32),
            jax.ShapeDtypeStruct((spans, width, width), F32),
            jax.ShapeDtypeStruct((spans, 8, n, width), F32),
        ],
        compiler_params=pltpu.CompilerParams(vmem_limit_bytes=48 * 1024 * 1024),
        cost_estimate=work(80),
    )(home, begins, parts, pre, gate, cols, *[first] * per_step)


def scan_backward_kernel(
    heads, p, home_ref, begins_ref, parts_ref, values_ref, joined_ref, scanned_ref, gate_ref, grad_a_ref,
    grad_b_ref, pre_ref, first_a_ref, first_b_ref, cols_ref, state_ref, mats_ref, *rest,
):
    steps = pl.num_programs(0)
    step = steps - 1 - pl.program_id(0)
    grads_ref, first_grad_ref, col_grad_ref, state = rest
    width = heads * HEAD
    n = heads * SPAN

    @pl.when(pl.program_id(0) == 0)
    def _():
        state[...] = jnp.zeros_like(state)
        col_grad_ref[...] = jnp.zeros_like(col_grad_ref)

    begins = [begins_ref[i] for i in range(begins_ref.shape[0])]
    masks = head_masks(heads)
    ones = head_ones(width)
    tri_r = lax.broadcasted_iota(jnp.int32, (SPAN, SPAN), 0)
    tri_c = lax.broadcasted_iota(jnp.int32, (SPAN, SPAN), 1)
    later = (tri_c >= tri_r).astype(LOW)
    after = (tri_c > tri_r).astype(LOW)
    sums = [jnp.zeros((1, width), F32) for _ in range(8)]

    def add(slot, value):
        sums[slot] = sums[slot] + jnp.sum(value, 0, keepdims=True)

    c13, c14 = cols_ref[0:1], cols_ref[1:2]
    grads = jnp.concatenate([grad_a_ref[0], grad_b_ref[0]], 0).astype(F32)
    firsts = jnp.concatenate([first_a_ref[0], first_b_ref[0]], 0).astype(F32)
    ready = []
    for c in range(BACKWARD_CHUNKS):
        rows = pl.ds(c * SPAN, SPAN)
        r, lw, k, kn, a = [parts_ref[i, rows] for i in range(5)]
        v = values_ref[rows]
        q = Chunk(r, lw, k, kn, a, begins, (step * BACKWARD_CHUNKS + c) * SPAN, heads)
        r, k, v = r.astype(F32), k.astype(F32), v.astype(F32)
        unit, scale = group_norm_parts(scanned_ref[rows], ones)
        grad_out = grads[c * SPAN : (c + 1) * SPAN]
        grad_joined = (grad_out * gate_ref[rows]).astype(LOW).astype(F32)
        grad_gate = (grad_out * joined_ref[rows].astype(F32)).astype(LOW)
        add(6, grad_joined * unit)
        add(7, grad_joined)
        grad_unit = grad_joined * c14
        grad_scan = scale * (
            grad_unit
            - head_sum(grad_unit, ones) * (1.0 / HEAD)
            - unit * (head_sum(grad_unit * unit, ones) * (1.0 / HEAD))
        )
        bonus = head_sum(r * k * c13, ones)
        grad_bonus = head_sum(grad_joined * v, ones)
        add(5, grad_bonus * r * k)
        own_r = grad_bonus * k * c13
        own_k = grad_bonus * r * c13
        own_v = grad_joined * bonus
        d_out = stacked(grad_scan, masks)
        flow = product(d_out, mats_ref[c, 7], TN, p["val"])
        ready.append((q, d_out, flow, own_r, own_k, own_v, grad_gate))
    now = state[...]
    ended = [None] * BACKWARD_CHUNKS
    for c in reversed(range(BACKWARD_CHUNKS)):
        ended[c] = now
        now = product(now, mats_ref[c, 6], NT, p["chain"]) + ready[c][2]
    state[...] = now
    span = range(BACKWARD_CHUNKS)
    mats = [[mats_ref[c, i] for i in range(6)] for c in span]
    begin = [state_ref[c] for c in span]
    chunks = [ready[c][0] for c in span]
    d_outs = [ready[c][1] for c in span]
    v_st = [stacked(values_ref[pl.ds(c * SPAN, SPAN)].astype(F32), masks) for c in span]
    update = [mats[c][5] + product(mats[c][4], begin[c], NT, p["val"]) for c in span]
    through = [product(mats[c][2], d_outs[c], TN, p["val"]) for c in span]
    through = [
        through[c] + product(chunks[c].b_end, ended[c], NT, p["val"]) for c in span
    ]
    back = [product(mats[c][0], through[c], TN, p["val"]) for c in span]
    left = [jnp.concatenate([back[c], d_outs[c]], 0) for c in span]
    right = [jnp.concatenate([update[c], v_st[c]], 0) for c in span]
    d_hats = [product(left[c], begin[c], NN, p["val"]) for c in span]
    pair_grads = [product(left[c], right[c], NT, p["bpair"]) for c in span]
    for c in span:
        strict, upto = chunks[c].strict.astype(F32), chunks[c].upto.astype(F32)
        mask = jnp.concatenate(
            [jnp.concatenate([strict, strict], 1), jnp.concatenate([upto, upto], 1)], 0
        )
        pair_grads[c] = pair_grads[c] * mask
    all_asks = []
    for c in span:
        q = chunks[c]
        keys = jnp.concatenate([q.b_hat, q.k_hat], 0)
        carried = jnp.concatenate([q.carried, q.carried], 0)
        all_asks.append(d_hats[c] * carried + product(pair_grads[c], keys, NN, p["bpair"]))
    all_keys = [
        product(
            pair_grads[c], jnp.concatenate([chunks[c].a_hat, chunks[c].r_hat], 0), TN, p["bpair"]
        )
        for c in span
    ]
    all_ends = [product(right[c], ended[c], NN, p["val"]) for c in span]
    all_vals = [
        product(jnp.concatenate([mats[c][1], mats[c][3]], 0), left[c], TN, p["val"]) for c in span
    ]
    all_vals = [
        all_vals[c] + product(chunks[c].k_end, ended[c], NT, p["val"]) for c in span
    ]
    for c in span:
        rows = pl.ds(c * SPAN, SPAN)
        q, _, _, own_r, own_k, own_v, grad_gate = ready[c]
        end_grad, begin_now = ended[c], begin[c]
        r, lw, k, kn, a = [parts_ref[i, rows].astype(F32) for i in range(5)]
        v = values_ref[rows].astype(F32)
        d_asks, d_keys, d_val = all_asks[c], all_keys[c], all_vals[c]
        d_ends = all_ends[c] * jnp.concatenate([q.final, q.final], 0)
        d_a, d_r = unstacked(d_asks[:n], heads) * q.before, unstacked(d_asks[n:], heads) * q.decay
        d_b = unstacked(d_keys[:n], heads) * q.inverse
        d_k = unstacked(d_keys[n:], heads) * q.inverse
        e_b = unstacked(d_ends[:n], heads) * q.to_end
        e_k = unstacked(d_ends[n:], heads) * q.to_end
        d_v = unstacked(d_val, heads) + own_v
        beta = kn * a
        end_part = e_b * beta + e_k * k
        here = d_r * r - d_b * beta - d_k * k - end_part
        ahead = -d_a * kn
        at_end = jnp.sum(end_part, 0, keepdims=True) + q.whole * q.end * jnp.sum(
            begin_now * end_grad, 0, keepdims=True
        )
        high, low = halves(here)
        high2, low2 = halves(ahead)
        d_lw = at_end + dot(
            jnp.concatenate([later, later, after, after], 1),
            jnp.concatenate([high, low, high2, low2], 0),
            NN,
        )
        d_b = d_b + e_b
        d_k = d_k + e_k + own_k
        d_r = d_r + own_r
        d_kn = d_b * a - d_a
        d_rate = d_b * kn
        g_r, g_lw, g_k, g_kn, g_a, g_v = [
            x.astype(LOW).astype(F32) for x in (d_r, d_lw, d_k, d_kn, d_rate, d_v)
        ]
        key_pre, value_pre, decay_up, rate_up, value_up = [pre_ref[i, rows] for i in range(5)]
        first = firsts[c * SPAN : (c + 1) * SPAN]
        c8, c9, c10, c11, c12 = [cols_ref[i : i + 1] for i in range(3, 8)]
        sig = jax.nn.sigmoid(c8 + decay_up)
        log_decay = -0.6065306597126334 * sig
        g_decay = g_lw * log_decay * (1.0 - sig)
        add(0, g_decay)
        rate = jax.nn.sigmoid(c9 + rate_up)
        g_rate = (g_a + g_k * key_pre * c12) * rate * (1.0 - rate)
        add(1, g_rate)
        g_key = g_k * (1.0 + (rate - 1.0) * c12)
        add(4, g_k * key_pre * (rate - 1.0))
        scaled = key_pre * c11
        norm = lax.rsqrt(head_sum(scaled * scaled, ones) + 1e-06)
        unit = scaled * norm
        g_scaled = norm * (g_kn - unit * head_sum(g_kn * unit, ones))
        g_key = g_key + g_scaled * c11
        add(3, g_scaled * key_pre)
        mix = jax.nn.sigmoid(c10 + value_up)
        g_value = g_v * (1.0 - mix)
        first_grad_ref[rows] = (g_v * mix).astype(first_grad_ref.dtype)
        g_vup = g_v * (first - value_pre) * mix * (1.0 - mix)
        add(2, g_vup)
        for i, x in enumerate((g_r, g_key, g_value, g_decay, g_rate, g_vup)):
            grads_ref[i, rows] = x.astype(LOW)
        grads_ref[6, rows] = grad_gate
    col_grad_ref[...] += jnp.concatenate(sums, 0)


def scan_backward(parts, values, joined, scanned, gate, grad, pre, first, cols, states, mats, home, begins, p):
    _, total, width = parts.shape
    heads = width // HEAD
    rows = BACKWARD_CHUNKS * SPAN
    n = heads * SPAN
    steps = total // rows
    row_spec = pl.BlockSpec((rows, width), lambda i, *_: (steps - 1 - i, 0))
    assert rows == 2 * BLOCK

    def stored(which):
        return pl.BlockSpec(
            (1, BLOCK, width), lambda i, home, b: (home[2 * (steps - 1 - i) + which], 0, 0)
        )

    return pl.pallas_call(
        functools.partial(scan_backward_kernel, heads, p),
        grid_spec=pltpu.PrefetchScalarGridSpec(
            num_scalar_prefetch=2,
            grid=(steps,),
            in_specs=[
                pl.BlockSpec((5, rows, width), lambda i, *_: (0, steps - 1 - i, 0)),
                row_spec,
                row_spec,
                row_spec,
                row_spec,
                stored(0),
                stored(1),
                pl.BlockSpec((5, rows, width), lambda i, *_: (0, steps - 1 - i, 0)),
                stored(0),
                stored(1),
                pl.BlockSpec(cols.shape, lambda i, *_: (0, 0)),
                pl.BlockSpec((BACKWARD_CHUNKS, width, width), lambda i, *_: (steps - 1 - i, 0, 0)),
                pl.BlockSpec((BACKWARD_CHUNKS, 8, n, width), lambda i, *_: (steps - 1 - i, 0, 0, 0)),
            ],
            out_specs=[
                pl.BlockSpec((7, rows, width), lambda i, *_: (0, steps - 1 - i, 0)),
                row_spec,
                pl.BlockSpec((8, width), lambda i, *_: (0, 0)),
            ],
            scratch_shapes=[pltpu.VMEM((width, width), F32)],
        ),
        out_shape=[
            jax.ShapeDtypeStruct((7, total, width), LOW),
            jax.ShapeDtypeStruct((total, width), LOW),
            jax.ShapeDtypeStruct((8, width), F32),
        ],
        compiler_params=pltpu.CompilerParams(vmem_limit_bytes=56 * 1024 * 1024),
        cost_estimate=work(60),
    )(home, begins, parts, values, joined, scanned, gate, grad, grad, pre, first, first, cols, states, mats)


def norm_rows(x):
    center = x - jnp.mean(x, -1, keepdims=True)
    scale = lax.rsqrt(jnp.mean(center * center, -1, keepdims=True) + 1e-05)
    return center * scale, scale


def keep_rows(rows, first, begins):
    position = first + lax.broadcasted_iota(jnp.int32, (rows, 1), 0)
    hit = position == begins[0]
    for b in begins[1:]:
        hit = hit | (position == b)
    return 1.0 - hit.astype(F32)


def rows_down(x, edge):
    row = lax.broadcasted_iota(jnp.int32, (x.shape[0], 1), 0)
    return jnp.where(row == 0, edge, pltpu.roll(x, 1, 0))


def rows_up(x, edge):
    row = lax.broadcasted_iota(jnp.int32, (x.shape[0], 1), 0)
    return jnp.where(row == x.shape[0] - 1, edge, pltpu.roll(x, x.shape[0] - 1, 0))


def lane_below(limit):
    return lax.broadcasted_iota(jnp.int32, (1, 128), 1) < limit


def kept(x, mask):
    return jnp.where(mask, x, jnp.zeros_like(x))


class SmallWeights:
    def __init__(self, small, up):
        self.pair, self.gate, self.value = small[:, :128], small[:, 128:256], small[:, 256:384]
        self.up_pair, self.up_gate = up[:, 384:512], up[:, 512:640]
        self.up_value = jnp.concatenate([up[:, 320:352], jnp.zeros((up.shape[0], 96), LOW)], 1)


PROJECT_BLOCKS = 4
BACK_BLOCKS = 4


def project_kernel(place_ref, begins_ref, *refs):
    x_refs, refs = refs[:PROJECT_BLOCKS], refs[PROJECT_BLOCKS:]
    cols_ref, own_ref, columns_ref, small_ref, up_ref, ends_ref, stats_ref, parts_ref, gate_ref = refs[:9]
    pre_ref, pair_ref, vm_ref, gs_ref, edge = refs[9:]
    step = pl.program_id(0)

    @pl.when(step == 0)
    def _():
        edge[...] = jnp.zeros_like(edge)

    begins = [begins_ref[i] for i in range(begins_ref.shape[0])]
    for i, ref in enumerate(x_refs):
        ends_ref[i] = jnp.concatenate([ref[0, :16], ref[0, BLOCK - 16 :]], 0)
    x = jnp.concatenate([ref[0] for ref in x_refs], 0).astype(F32)
    rows = x.shape[0]
    mean = jnp.mean(x, -1, keepdims=True)
    center = x - mean
    scale = lax.rsqrt(jnp.mean(center * center, -1, keepdims=True) + 1e-05)
    unit = center * scale
    stats_ref[...] = jnp.concatenate([mean, scale], 1)
    normed = unit * cols_ref[0:1] + cols_ref[1:2]
    moved = rows_down(normed, edge[0:1]) * keep_rows(rows, step * rows, begins)
    edge[0:1] = normed[rows - 1 : rows]
    diff = moved - normed
    mixed = [(normed + diff * cols_ref[i : i + 1]).astype(LOW) for i in range(2, 8)]
    in_r, in_d, in_k, in_v, in_a, in_g = mixed
    low = SmallWeights(small_ref[...], up_ref[...])
    width = own_ref.shape[1]
    recept = dot(in_r, columns_ref[:, :width], NN)
    key_pre = dot(in_k, columns_ref[:, width : 2 * width], NN)
    values = dot(in_v, jnp.concatenate([columns_ref[:, 2 * width :], low.value], 1), NN)
    value_pre = values[:, :width]
    value_mid = kept(values[:, width:], lane_below(DV)).astype(LOW)
    decay, rate = dot(in_d, low.pair, NN), dot(in_a, low.pair, NN)
    pair = jnp.where(lane_below(DECAY_RANK), jnp.tanh(decay), rate)
    pair_low = pair.astype(LOW)
    gate_sig = jax.nn.sigmoid(dot(in_g, low.gate, NN))
    decay_up = dot(kept(pair_low, lane_below(DECAY_RANK)), low.up_pair, NT)
    rate_up = dot(kept(pair_low, ~lane_below(DECAY_RANK)), low.up_pair, NT)
    value_up = dot(value_mid, low.up_value, NT)
    gate_ref[...] = dot(gate_sig.astype(LOW), low.up_gate, NT)
    pair_ref[...] = pair
    vm_ref[...] = value_mid
    gs_ref[...] = gate_sig
    for i, value in enumerate((key_pre, value_pre, decay_up, rate_up, value_up)):
        pre_ref[i] = value
    c8, c9, _, c11, c12 = [own_ref[i : i + 1] for i in range(3, 8)]
    ones = head_ones(recept.shape[1])
    log_decay = -jnp.exp(-jax.nn.softplus(-(c8 + decay_up)) - 0.5)
    rate = jax.nn.sigmoid(c9 + rate_up)
    scaled = key_pre * c11
    key_norm = scaled * lax.rsqrt(head_sum(scaled * scaled, ones) + 1e-06)
    key_main = key_pre * (1.0 + (rate - 1.0) * c12)
    for i, value in enumerate((recept, log_decay, key_main, key_norm, rate)):
        parts_ref[i] = value.astype(LOW)


def block_spec(per, which, rows, width, blocks, back, each, lanes=0):
    def index(i, *tables):
        step = blocks // each - 1 - i if back else i
        stored = tables[0][jnp.maximum(each * step + which, 0)]
        return (stored // per, (stored % per) * (BLOCK // rows) + BLOCK // rows - 1, lanes)

    return pl.BlockSpec((1, rows, width), index)


def whole_spec(array):
    return pl.BlockSpec(array.shape, lambda i, *_: (0,) * array.ndim)


def project(x, cols, own, weights, place, begins, per):
    blocks = place.shape[0]
    total = blocks * BLOCK
    rows = PROJECT_BLOCKS * BLOCK
    width = own.shape[1]
    span = lambda w: pl.BlockSpec((rows, w), lambda i, *_: (i, 0))
    deep = lambda n: pl.BlockSpec((n, rows, width), lambda i, *_: (0, i, 0))
    shape = jax.ShapeDtypeStruct
    return pl.pallas_call(
        project_kernel,
        grid_spec=pltpu.PrefetchScalarGridSpec(
            num_scalar_prefetch=2,
            grid=(blocks // PROJECT_BLOCKS,),
            in_specs=[
                block_spec(per, b, BLOCK, x.shape[2], blocks, False, PROJECT_BLOCKS)
                for b in range(PROJECT_BLOCKS)
            ]
            + [whole_spec(cols), whole_spec(own)]
            + [whole_spec(w) for w in weights],
            out_specs=[
                pl.BlockSpec((PROJECT_BLOCKS, 32, x.shape[2]), lambda i, *_: (i, 0, 0)),
                span(2), deep(5), span(width), deep(5), span(128), span(128), span(128),
            ],
            scratch_shapes=[pltpu.VMEM((8, x.shape[2]), F32)],
        ),
        out_shape=[
            shape((blocks, 32, x.shape[2]), LOW),
            shape((total, 2), F32),
            shape((5, total, width), LOW),
            shape((total, width), F32),
            shape((5, total, width), F32),
            shape((total, 128), F32),
            shape((total, 128), LOW),
            shape((total, 128), F32),
        ],
        compiler_params=pltpu.CompilerParams(vmem_limit_bytes=56 * 1024 * 1024),
        cost_estimate=work(20),
    )(place, begins, *[x] * PROJECT_BLOCKS, cols, own, *weights)


def project_back_kernel(
    part, parts, place_ref, turn_ref, row_ref, begins_ref, head_ref, *refs,
):
    x_refs, refs = refs[:BACK_BLOCKS], refs[BACK_BLOCKS:]
    xp_ref, stats_ref, prior_stats_ref, grads_ref, pair_ref, vm_ref, gs_ref, scan_ref, ffn_ref = refs[:9]
    cols_ref, columns_ref, small_ref, up_ref, *rest = refs[9:]
    sizes_x = len(rest) - 6 - (2 if part == 0 else 1)
    back_refs, rest = rest[:sizes_x], rest[sizes_x:]
    if part == 0:
        low_sum_ref, up_sum_ref, edge, sum_ref, columns_t, small_t, buffer, sems = rest
    else:
        low_sum_ref, edge, sum_ref, columns_t, small_t, buffer, sems = rest
    turn = pl.program_id(0)
    step = pl.num_programs(0) - 1 - turn
    wide = columns_ref.shape[0]

    @pl.when(turn == 0)
    def _():
        for ref in (edge, sum_ref) + ((up_sum_ref,) if part == 0 else ()):
            ref[...] = jnp.zeros_like(ref)
        columns_t[...] = columns_ref[...].T
        small_t[...] = small_ref[:, :384].T

    begins = [begins_ref[i] for i in range(begins_ref.shape[0])]

    x = jnp.concatenate([ref[0] for ref in x_refs], 0).astype(F32)
    unit = (x - stats_ref[:, 0:1]) * stats_ref[:, 1:2]
    rows = unit.shape[0]
    normed = unit * cols_ref[0:1] + cols_ref[1:2]
    last = xp_ref[0, 8:].astype(F32)
    prior = (last - prior_stats_ref[:, 0:1]) * prior_stats_ref[:, 1:2] * cols_ref[0:1] + cols_ref[1:2]
    keep = keep_rows(rows, step * rows, begins)
    diff = rows_down(normed, prior[prior.shape[0] - 1 :]) * keep - normed
    up = up_ref[...]
    up_pair, up_gate = up[:, 384:512], up[:, 512:640]
    up_value = jnp.concatenate([up[:, 320:352], jnp.zeros((up.shape[0], 96), LOW)], 1)
    width = grads_ref.shape[2]
    g_r, g_k, g_v, g_decay, g_rate, g_vup, g_gate = [grads_ref[i] for i in range(7)]
    pair, sig = pair_ref[...], gs_ref[...]
    is_decay = lane_below(DECAY_RANK)
    m_pair = jnp.where(
        is_decay, dot(g_decay, up_pair, NN) * (1.0 - pair * pair), dot(g_rate, up_pair, NN)
    ).astype(LOW)
    m_v = kept(dot(g_vup, up_value, NN), lane_below(DV)).astype(LOW)
    m_g = (dot(g_gate, up_gate, NN) * sig * (1.0 - sig)).astype(LOW)
    near = jnp.zeros_like(unit)
    far = jnp.zeros_like(unit)
    value_weights = jnp.concatenate([columns_t[2 * width :], small_t[256:384]], 0)
    pair_weights = small_t[:128]
    cut = DECAY_RANK + DA + 3 * width
    grads = (
        (2, g_r, columns_t[:width], ((0, g_r),)),
        (3, kept(m_pair, is_decay), pair_weights, ((3 * width, m_pair[:, :DECAY_RANK]),)),
        (4, g_k, columns_t[width : 2 * width], ((width, g_k),)),
        (5, jnp.concatenate([g_v, m_v], 1), value_weights, ((2 * width, g_v), (cut, m_v[:, :DV]))),
        (6, kept(m_pair, ~is_decay), pair_weights, ((3 * width + DECAY_RANK, m_pair[:, DECAY_RANK:]),)),
        (7, m_g, small_t[128:256], ((cut + DV, m_g),)),
    )
    col_sums = []
    for slot, grad, weight, pieces in grads:
        mix = cols_ref[slot : slot + 1]
        mixed = (normed + diff * mix).astype(LOW)
        total = dot(grad, weight, NN)
        for start, piece in pieces:
            sum_ref[start : start + piece.shape[1]] += dot(piece, mixed, TN)
        near = near + total
        far = far + total * mix
        col_sums.append(jnp.sum(total * diff, 0, keepdims=True))
    if part == 0:
        start = 0
        pair_low = pair.astype(LOW)
        for mid, grad in (
            (pair_low[:, :DECAY_RANK], g_decay),
            (pair_low[:, DECAY_RANK:], g_rate),
            (vm_ref[:, :DV], g_vup),
            (sig.astype(LOW), g_gate),
        ):
            up_sum_ref[start : start + mid.shape[1]] += dot(mid, grad, TN)
            start += mid.shape[1]
    moved = far * keep
    back = near - far + rows_up(moved, edge[0:1])
    edge[0:1] = moved[0:1]
    first = [jnp.sum(back * unit, 0, keepdims=True), jnp.sum(back, 0, keepdims=True)]
    sum_ref[sum_ref.shape[0] - 8 :] += jnp.concatenate(first + col_sums, 0)

    slot = turn % 2

    def leave(where):
        for which in range(BACK_BLOCKS):
            pltpu.make_async_copy(
                buffer.at[where, which], back_refs[0].at[0], sems.at[where, which]
            ).wait()

    @pl.when(turn >= 2)
    def _():
        leave(slot)

    buffer[slot] = back.astype(LOW).reshape(BACK_BLOCKS, BLOCK, wide)
    for which in range(BACK_BLOCKS):
        block = BACK_BLOCKS * step + which
        for x, ref in enumerate(back_refs):

            @pl.when(turn_ref[block] == x)
            def _():
                pltpu.make_async_copy(
                    buffer.at[slot, which], ref.at[row_ref[block]], sems.at[slot, which]
                ).start()

    @pl.when(step == 0)
    def _():
        held = sum_ref.shape[0]
        low_sum_ref[:held] = sum_ref[...].astype(LOW)
        lane = lax.broadcasted_iota(jnp.int32, (1, wide), 1) + part * wide
        spread = jnp.concatenate([scan_ref[...]] * (wide // width), 1)
        spread = jnp.where(lane // width == head_ref[0], spread, 0.0)
        low_sum_ref[held : held + 16] = jnp.concatenate([spread, ffn_ref[...]], 0).astype(LOW)
        low_sum_ref[held + 16 :] = jnp.zeros_like(low_sum_ref[held + 16 :])
        leave(1 - slot)
        leave(slot)


def project_back(
    part, parts, x, stats, grads, mids, extra_cols, cols, weights, place, turn, row, begins, head, per, sizes
):
    blocks = place.shape[0]
    rows = BACK_BLOCKS * BLOCK
    steps = blocks // BACK_BLOCKS
    wide = x.shape[2] // parts
    width = grads.shape[2]
    size_z, size_x = sizes
    low_rank = DECAY_RANK + DA + DV + 128
    span = lambda w: pl.BlockSpec((rows, w), lambda i, *_: (steps - 1 - i, 0))
    shape = jax.ShapeDtypeStruct
    held = 3 * width + low_rank + 8
    sums = [shape((held + 16 + -(held + 16) % 16, wide), LOW)]
    if part == 0:
        sums.append(shape((low_rank, width), F32))
    columns, small, up = weights
    assert steps > 1
    return pl.pallas_call(
        functools.partial(project_back_kernel, part, parts),
        grid_spec=pltpu.PrefetchScalarGridSpec(
            num_scalar_prefetch=5,
            grid=(steps,),
            in_specs=[
                *[
                    block_spec(per, b, BLOCK, wide, blocks, True, BACK_BLOCKS, part)
                    for b in range(BACK_BLOCKS)
                ],
                block_spec(per, -1, 16, wide, blocks, True, BACK_BLOCKS, part),
                span(2),
                pl.BlockSpec(
                    (8, 2), lambda i, *_: (jnp.maximum((steps - 1 - i) * (rows // 8) - 1, 0), 0)
                ),
                pl.BlockSpec((7, rows, width), lambda i, *_: (0, steps - 1 - i, 0)),
            ]
            + [span(m.shape[1]) for m in mids]
            + [
                whole_spec(extra_cols[0]),
                pl.BlockSpec((8, wide), lambda i, *_: (0, part)),
                pl.BlockSpec((cols.shape[0], wide), lambda i, *_: (0, part)),
                pl.BlockSpec((wide, columns.shape[1]), lambda i, *_: (part, 0)),
                pl.BlockSpec((wide, small.shape[1]), lambda i, *_: (part, 0)),
                whole_spec(up),
            ],
            out_specs=[pl.BlockSpec(memory_space=pl.ANY)] * size_x + [whole_spec(s) for s in sums],
            scratch_shapes=[
                pltpu.VMEM((8, wide), F32),
                pltpu.VMEM((held, wide), F32),
                pltpu.VMEM((columns.shape[1], wide), LOW),
                pltpu.VMEM((384, wide), LOW),
                pltpu.VMEM((2, BACK_BLOCKS, BLOCK, wide), LOW),
                pltpu.SemaphoreType.DMA((2, BACK_BLOCKS)),
            ],
        ),
        out_shape=[shape((size_z * per, BLOCK, wide), LOW)] * size_x + sums,
        compiler_params=pltpu.CompilerParams(vmem_limit_bytes=56 * 1024 * 1024),
        cost_estimate=work(17000),
    )(
        place, turn, row, begins, head, *[x] * (BACK_BLOCKS + 1), stats, stats, grads, *mids, *extra_cols, cols, columns, small, up
    )


TALL = BLOCK + 16


def block_keeps(local_ref, begins_ref, j):
    begins = [begins_ref[i] for i in range(begins_ref.shape[0])]
    first = local_ref[j] * BLOCK
    after = jnp.float32(1.0)
    for b in begins:
        after = jnp.where(first + BLOCK == b, 0.0, after)
    return keep_rows(BLOCK, first, begins), after


def middle_kernel(
    per, local_ref, begins_ref, table_ref, out_ref, tokens_ref, cols_ref, near_ref, far_ref, middle_ref, ffn_ref,
    rows_ref, weight_ref,
):
    count, height, _ = near_ref.shape
    for i in range(2 * count):
        slot = table_ref[i]
        other = lax.rem(slot, count)
        weight_ref[i * height : (i + 1) * height] = jnp.where(slot < count, near_ref[other], far_ref[other])
    heads = out_ref.shape[0]
    rows = [jnp.concatenate([out_ref[h, j] for h in range(heads)], 1) for j in range(per)]
    rows = jnp.concatenate(rows, 0)
    rows_ref[...] = rows
    middle = tokens_ref[...].astype(F32) + dot(rows, weight_ref[...], NN)
    middle_ref[...] = middle
    unit, _ = norm_rows(middle)
    normed = unit * cols_ref[16:17] + cols_ref[17:18]
    c18 = cols_ref[18:19]
    extra_row = lax.broadcasted_iota(jnp.int32, (TALL - BLOCK, 1), 0)
    for j in range(per):
        main = normed[j * TALL : j * TALL + BLOCK]
        extra = normed[j * TALL + BLOCK : (j + 1) * TALL]
        keep, keep_after = block_keeps(local_ref, begins_ref, j)
        moved = rows_down(main, extra[0:1]) * keep
        ffn_ref[j * TALL : j * TALL + BLOCK] = (main + (moved - main) * c18).astype(LOW)
        after = extra + (main[BLOCK - 1 :] * keep_after - extra) * c18
        ffn_ref[j * TALL + BLOCK : (j + 1) * TALL] = jnp.where(extra_row == 1, after, 0.0).astype(LOW)


def middle_rows(out, tokens_ext, near, far, table, cols, local, begins):
    _, per, _, _ = out.shape
    wide = near.shape[2]
    shape = jax.ShapeDtypeStruct
    weight = shape((wide, wide), LOW)
    return pl.pallas_call(
        functools.partial(middle_kernel, per),
        grid_spec=pltpu.PrefetchScalarGridSpec(
            num_scalar_prefetch=3,
            grid=(1,),
            in_specs=[whole_spec(x) for x in (out, tokens_ext, cols, near, far)],
            out_specs=[whole_spec(tokens_ext)] * 3 + [whole_spec(weight)],
        ),
        out_shape=[
            shape((per * TALL, wide), F32),
            shape((per * TALL, wide), LOW),
            shape((per * TALL, wide), LOW),
            weight,
        ],
        compiler_params=pltpu.CompilerParams(vmem_limit_bytes=48 * 1024 * 1024),
        cost_estimate=work(6),
    )(local, begins, table, out, tokens_ext, cols, near, far)


def with_extra(main, extra):
    per = main.shape[0] // BLOCK
    pieces = []
    for j in range(per):
        pieces += [main[j * BLOCK : (j + 1) * BLOCK], extra[j * 16 : (j + 1) * 16]]
    return pieces


def weight_rows_of(ref):
    heads, _, seqs, _, _ = ref.shape
    return jnp.concatenate([ref[h, 0, s] for s in range(seqs) for h in range(heads)], 0)


def channel_kernel(
    xa_ref, xb_ref, ga_ref, gb_ref, ea_ref, eb_ref, key_ref, value_ref, hidden_ref, pre_ref, a_ref, b_ref
):
    rows = xa_ref.shape[0]
    x = jnp.concatenate([xa_ref[...], xb_ref[...]], 0)
    g = jnp.concatenate(with_extra(ga_ref, ea_ref) + with_extra(gb_ref, eb_ref), 0)
    key, value = weight_rows_of(key_ref), weight_rows_of(value_ref)
    active = jnp.maximum(dot(x, key, NN), 0.0)
    hidden_ref[...] = (active * active).astype(LOW)
    grad = (dot(g, value, NN) * 2.0 * active).astype(LOW)
    pre_ref[...] = grad
    back = dot(grad, key, NT)

    @pl.when(pl.program_id(0) == 0)
    def _():
        a_ref[...] = back[:rows]
        b_ref[...] = back[rows:]

    @pl.when(pl.program_id(0) > 0)
    def _():
        a_ref[...] += back[:rows]
        b_ref[...] += back[rows:]


def channel_mix(x, g, extra, weights):
    rows, wide = x[0].shape
    heads, _, seqs, weight_rows, columns = weights.shape
    part = columns // 4

    def weight(which):
        return pl.BlockSpec(
            (heads, 1, seqs, weight_rows, part), lambda i: (0, which, 0, 0, i)
        )

    piece = pl.BlockSpec((2 * rows, part), lambda i: (0, i))
    shape = jax.ShapeDtypeStruct
    return pl.pallas_call(
        channel_kernel,
        grid=(4,),
        in_specs=[whole_spec(a) for a in (*x, *g, *extra)]
        + [weight(0), weight(1)],
        out_specs=[piece, piece, whole_spec(x[0]), whole_spec(x[0])],
        out_shape=[
            shape((2 * rows, columns), LOW),
            shape((2 * rows, columns), LOW),
            shape((rows, wide), F32),
            shape((rows, wide), F32),
        ],
        compiler_params=pltpu.CompilerParams(vmem_limit_bytes=48 * 1024 * 1024),
        cost_estimate=work(8),
    )(*x, *g, *extra, weights, weights)


def main_rows(refs):
    pieces = []
    for ref in refs:
        for start in range(0, ref.shape[0], TALL):
            pieces.append(ref[start : start + BLOCK])
    return jnp.concatenate(pieces, 0)


def channel_grad_kernel(count, *refs):
    og, x = jnp.concatenate([r[...] for r in refs[:count]], 0), main_rows(refs[count : 2 * count])
    hidden, pre = main_rows(refs[2 * count : 2 * count + 2]), main_rows(refs[2 * count + 2 : 2 * count + 4])
    out = refs[2 * count + 4]
    columns = hidden.shape[1]
    out[:, :columns] = dot(og, hidden, TN).astype(LOW)
    out[:, columns : 2 * columns] = dot(x, pre, TN).astype(LOW)


def channel_grads(og, x, hidden, pre, extra):
    wide = og[0].shape[1]
    part = 256
    columns = hidden[0].shape[1]
    return pl.pallas_call(
        functools.partial(channel_grad_kernel, len(og)),
        grid=(wide // part,),
        in_specs=[pl.BlockSpec((a.shape[0], part), lambda i: (0, i)) for a in (*og, *x)]
        + [whole_spec(h) for h in (*hidden, *pre)],
        out_specs=pl.BlockSpec((part, 2 * columns + extra), lambda i: (i, 0)),
        out_shape=jax.ShapeDtypeStruct((wide, 2 * columns + extra), LOW),
        compiler_params=pltpu.CompilerParams(vmem_limit_bytes=48 * 1024 * 1024),
        cost_estimate=work(9),
    )(*og, *x, *hidden, *pre)


def output_grad_kernel(count, *refs):
    rows, grads, out = refs[:count], refs[count : 2 * count], refs[-1]
    left = jnp.concatenate([r[...] for r in rows], 0)
    right = jnp.concatenate([r[...] for r in grads], 0)
    out[...] = dot(left, right, TN).astype(LOW)


def output_grads(rows, grads, room):
    tall, wide = rows[0].shape
    part = grads[0].shape[1]
    last = room.shape[1] // part - 1
    return pl.pallas_call(
        functools.partial(output_grad_kernel, len(rows)),
        grid=(wide // part,),
        in_specs=[pl.BlockSpec((tall, part), lambda i: (0, i))] * len(rows)
        + [whole_spec(g) for g in grads]
        + [pl.BlockSpec(memory_space=pl.ANY)],
        out_specs=pl.BlockSpec((part, part), lambda i: (i, last)),
        out_shape=jax.ShapeDtypeStruct(room.shape, LOW),
        input_output_aliases={2 * len(rows): 0},
        compiler_params=pltpu.CompilerParams(vmem_limit_bytes=48 * 1024 * 1024),
        cost_estimate=work(2),
    )(*rows, *grads, room)


def middle_back_kernel(
    per, local_ref, begins_ref, near_ref, core_ref, far_ref, middle_ref, og_ref, weight_ref, cols_ref,
    grad_ref, low_ref, heads_ref, sums_ref,
):
    c16, c17, c18 = [cols_ref[i : i + 1] for i in (16, 17, 18)]
    grad_in = near_ref[...] + core_ref[...] + far_ref[...].astype(F32)
    sums = [jnp.zeros((1, c16.shape[1]), F32) for _ in range(3)]
    lows = []
    for j in range(per):
        start = j * TALL
        grad, after = grad_in[start : start + BLOCK], grad_in[start + BLOCK + 1 : start + BLOCK + 2]
        keep, keep_after = block_keeps(local_ref, begins_ref, j)
        ahead = rows_up(grad * keep, after * keep_after)
        grad_normed = grad + (ahead - grad) * c18
        unit, scale = norm_rows(middle_ref[start : start + BLOCK])
        prior, _ = norm_rows(middle_ref[start + BLOCK : start + TALL])
        normed = unit * c16 + c17
        diff = rows_down(normed, prior[0:1] * c16 + c17) * keep - normed
        for i, value in enumerate((grad_normed * unit, grad_normed, grad * diff)):
            sums[i] = sums[i] + jnp.sum(value, 0, keepdims=True)
        og = og_ref[j * BLOCK : (j + 1) * BLOCK].astype(F32)
        total = og + norm_back(grad_normed, unit, scale, c16)
        grad_ref[j * BLOCK : (j + 1) * BLOCK] = total
        lows.append(total.astype(LOW))
        quarter = low_ref.shape[2]
        for s in range(low_ref.shape[0]):
            low_ref[s, start : start + BLOCK] = lows[-1][:, s * quarter : (s + 1) * quarter]
            low_ref[s, start + BLOCK : start + TALL] = jnp.zeros((TALL - BLOCK, quarter), LOW)
    sums_ref[...] = jnp.concatenate(sums + [jnp.zeros((5, c16.shape[1]), F32)], 0)
    out = dot(jnp.concatenate(lows, 0), weight_ref[...], NT).astype(LOW)
    width = heads_ref.shape[2]
    for h in range(heads_ref.shape[0]):
        heads_ref[h] = out[:, h * width : (h + 1) * width]


def norm_back(grad, unit, scale, gain):
    grad = grad * gain
    return scale * (
        grad - jnp.mean(grad, -1, keepdims=True) - unit * jnp.mean(grad * unit, -1, keepdims=True)
    )


def middle_back(near, core, far, middle, og, weight, cols, local, begins, heads, seqs):
    tall, wide = near.shape
    per = tall // TALL
    shape = jax.ShapeDtypeStruct
    outs = [
        shape((per * BLOCK, wide), F32),
        shape((seqs, tall, wide // seqs), LOW),
        shape((heads, per * BLOCK, wide // heads), LOW),
        shape((8, wide), F32),
    ]
    operands = (near, core, far, middle, og, weight, cols)
    return pl.pallas_call(
        functools.partial(middle_back_kernel, per),
        grid_spec=pltpu.PrefetchScalarGridSpec(
            num_scalar_prefetch=2,
            grid=(1,),
            in_specs=[whole_spec(x) for x in operands],
            out_specs=[whole_spec(x) for x in outs],
        ),
        out_shape=outs,
        compiler_params=pltpu.CompilerParams(vmem_limit_bytes=48 * 1024 * 1024),
        cost_estimate=work(8),
    )(local, begins, *operands)


HEAD_AXES = ("hz", "hx")


def all_gather(x, axes):
    return lax.all_gather(x, axes, axis=0, tiled=True)


def steps_along(x, axis):
    size = lax.axis_size(axis)
    return [lax.ppermute(x, axis, [(i, i ^ k) for i in range(size)]) for k in range(1, size)]


def grown(x, axis):
    return jnp.concatenate([x] + steps_along(x, axis), 0)


def order_table(axes):
    strides, stride = {}, 1
    for axis in axes:
        strides[axis] = stride
        stride *= lax.axis_size(axis)
    index = jnp.arange(stride, dtype=jnp.int32)
    place, below = jnp.zeros((), jnp.int32), stride
    for axis in ("ys", "core") + HEAD_AXES:
        if axis in axes:
            below //= lax.axis_size(axis)
            there = (index // below) % lax.axis_size(axis)
            place = place + (there ^ lax.axis_index(axis)) * strides[axis]
    return place


def in_order(x, axes):
    x = taken_blocks(x, order_table(axes))
    return x.reshape((x.shape[0] * x.shape[1],) + x.shape[2:])


def swap(x, axis):
    return lax.ppermute(x, axis, [(0, 1), (1, 0)])


def seq_gather(x):
    if lax.axis_size("ys") != 2:
        return list(lax.all_gather(x, ("ys", "core"), axis=0))
    far = swap(x, "ys")
    return [x, swap(x, "core"), far, swap(far, "core")]


def seq_return(near, core, far, diagonal):
    return swap(core, "core"), swap((far + swap(diagonal, "core")).astype(LOW), "ys")


def seq_step(x, axis):
    if lax.axis_size("ys") != 2:
        if axis == "ys":
            return x
        return lax.psum_scatter(x, ("ys", "core"), scatter_dimension=0, tiled=True)[0].astype(F32)
    if axis == "ys":
        x = x.reshape((2, 2) + x.shape[1:])
    index = lax.axis_index(axis)
    sent = swap(lax.dynamic_index_in_dim(x, 1 - index, 0, keepdims=False).astype(LOW), axis)
    return lax.dynamic_index_in_dim(x, index, 0, keepdims=False).astype(F32) + sent.astype(F32)


def taken_blocks(x, table):
    return x.at[table].get(mode="promise_in_bounds")


def start_flags(positions, begins):
    return jnp.any(positions[..., None] == begins, -1).astype(F32)


def body(
    tokens,
    leading_layer_value,
    output_gradient,
    lengths,
    sequence_block_of,
    stored_block_of,
    channel_settings,
    receptance_matrix,
    key_matrix,
    value_matrix,
    output_matrix,
    branch_down_weight,
    branch_up_weight,
    channel_key_weight,
    channel_value_weight,
):
    rows_here, wide = tokens.shape
    per = rows_here // BLOCK
    ys, heads_axis = lax.axis_size("ys"), lax.axis_size("hz") * lax.axis_size("hx")
    seqs = 2 * ys
    head = lax.axis_index(HEAD_AXES)
    core = lax.axis_index("core")
    width = wide // heads_axis
    weight_rows = receptance_matrix.shape[0]
    low_rank = branch_down_weight.shape[1]
    order, home = sequence_block_of[0], stored_block_of[0]
    blocks = order.shape[0]
    begins = (jnp.cumsum(lengths[0]) - lengths[0]).astype(jnp.int32)
    splits = (DECAY_RANK, DECAY_RANK + DA, DECAY_RANK + DA + DV)

    og_first = output_gradient.reshape(per, BLOCK, wide)[:, 0]
    place = home
    out_table = order_table(HEAD_AXES + ("ys", "core"))
    size_z, size_x = lax.axis_size("hz"), lax.axis_size("hx")
    apart = (home // per) ^ head
    turn_x, turn_row = apart % size_x, (apart // size_x) * per + home % per
    local = lax.dynamic_slice_in_dim(order, head * per, per)
    group = all_gather(tokens[None], HEAD_AXES)
    og_rows = in_order(grown(grown(og_first[None], "hz"), "hx"), HEAD_AXES)
    og_parts = seq_gather(output_gradient)

    quarter = channel_key_weight.shape[1] // seqs
    pair = jnp.stack([channel_key_weight, channel_value_weight], 0).reshape(2, weight_rows, seqs, quarter)
    pair = lax.all_to_all(
        pair.transpose(2, 0, 1, 3), ("ys", "core"), split_axis=0, concat_axis=0, tiled=True
    )
    columns = (
        jnp.stack([receptance_matrix, key_matrix, value_matrix], 1)
        .reshape(weight_rows * 3, heads_axis, width)
        .transpose(1, 0, 2)
    )
    columns = lax.all_to_all(columns, HEAD_AXES, split_axis=0, concat_axis=0, tiled=True)
    def rank_columns(weight):
        return jnp.split(weight, (DECAY_RANK + DA, DECAY_RANK + DA + DV), 1)

    (down_pair, down_value, down_gate), (up_pair, up_value, up_gate) = [
        rank_columns(w) for w in (branch_down_weight, branch_up_weight)
    ]
    count = channel_settings.shape[1]
    blank = [jnp.zeros((weight_rows, n), LOW) for n in (32 - count, 32)]
    small = jnp.concatenate(
        [
            down_pair, down_gate, down_value, channel_settings, blank[0], up_value, blank[1],
            up_pair, up_gate,
        ],
        1,
    )[None]
    for axis in HEAD_AXES + ("ys", "core"):
        small = grown(small, axis)
    small = in_order(small, HEAD_AXES + ("ys", "core"))
    columns = columns.reshape(1, heads_axis * weight_rows, 3 * width)
    columns = in_order(grown(grown(columns, "ys"), "core"), ("ys", "core"))
    settings = small[:, 256 + DV : 256 + DV + count].astype(F32).T
    up = lax.dynamic_slice_in_dim(small, head * width, width, 0)
    own = lax.dynamic_slice_in_dim(settings, head * width, width, 1)
    own = jnp.concatenate([own[13:16], own[8:13]], 0)
    out_shards = grown(grown(output_matrix[None], "hz"), "hx")
    columns, small, settings, up, own, og_parts, pair, first_sent, out_shards = (
        lax.optimization_barrier(
            (
                columns, small, settings, up, own, og_parts, pair, leading_layer_value, out_shards,
            )
        )
    )
    first_group = lax.all_to_all(
        first_sent.reshape(rows_here, heads_axis, width).transpose(1, 0, 2),
        HEAD_AXES, split_axis=0, concat_axis=0, tiled=True,
    ).reshape(blocks, BLOCK, width)
    weights = [columns, small, up]

    out_shards = grown(out_shards, "ys")

    def gathered(half):
        return all_gather(half[None], HEAD_AXES).transpose(1, 0, 2, 3)

    whole_quarter = quarter == wide
    if whole_quarter:
        every = all_gather(pair.transpose(1, 0, 2, 3).reshape(1, -1, weight_rows, wide), HEAD_AXES)
    else:
        every = (gathered(pair[:, 0]), gathered(pair[:, 1]))

    ends, stats, parts, gate, pre, *mids = project(group, settings, own, weights, place, begins, per)
    parts, out_shards = lax.optimization_barrier((parts, out_shards))
    far_shards = swap(out_shards, "core")
    values, out_in, joined, scanned, states, mats = scan_forward(
        parts, pre, first_group, gate, own, home, begins, PASSES
    )

    before, follow = jnp.maximum(order - 1, 0), jnp.minimum(order + 1, blocks - 1)
    in_blocks = out_in.reshape(blocks, BLOCK, width)
    extended = jnp.concatenate(
        [
            taken_blocks(in_blocks, order),
            taken_blocks(in_blocks[:, BLOCK - 1], before)[:, None],
            taken_blocks(in_blocks[:, 0], follow)[:, None],
            jnp.zeros((blocks, 14, width), LOW),
        ],
        1,
    )
    extended, far_shards, ends, og_rows = lax.optimization_barrier((extended, far_shards, ends, og_rows))
    out_ext = lax.all_to_all(
        extended.reshape(heads_axis, per, TALL, width), HEAD_AXES, split_axis=0, concat_axis=0, tiled=True
    )
    local = lax.dynamic_slice_in_dim(order, head * per, per)
    after_seq = local + 1
    after_live = (after_seq < blocks).astype(LOW)[:, None]
    after = jnp.minimum(after_seq, blocks - 1)
    row_before = taken_blocks(ends, jnp.maximum(local - 1, 0))[:, 31]
    row_after = taken_blocks(ends, after)[:, 0]
    og_after = taken_blocks(og_rows, taken_blocks(home, after)) * after_live
    none = jnp.zeros((per, 14, wide), LOW)
    extra_parts = seq_gather(jnp.concatenate([none[:, :1], og_after[:, None], none], 1).reshape(-1, wide))
    tokens_b = tokens.reshape(per, BLOCK, wide)
    tokens_ext = jnp.concatenate([tokens_b, row_before[:, None], row_after[:, None], none], 1)
    middle, ffn_in, out_rows, out_weight = middle_rows(
        out_ext, tokens_ext.reshape(-1, wide), out_shards, far_shards, out_table, settings, local, begins
    )
    ffn_in, every = lax.optimization_barrier((ffn_in, every))
    if whole_quarter:
        every = every.reshape(heads_axis, 2, seqs, weight_rows, wide)
        value_part = every[:, 1].transpose(1, 0, 2, 3).reshape(wide, wide)
        ffn_parts = [ffn_in, swap(ffn_in, "core"), swap(ffn_in, "ys")]
        *near, own_part, core_part = channel_mix(ffn_parts[:2], og_parts[:2], extra_parts[:2], every)
        ffn_parts[2], near, own_part, core_part, out_rows = lax.optimization_barrier(
            (ffn_parts[2], near, own_part, core_part, out_rows)
        )
        ffn_parts.append(swap(ffn_parts[2], "core"))
        *far, far_part, diagonal = channel_mix(ffn_parts[2:], og_parts[2:], extra_parts[2:], every)
        came_core, came_far = seq_return(own_part, core_part, far_part, diagonal)
        grads_here = channel_grads(
            og_parts, ffn_parts, (near[0], far[0]), (near[1], far[1]), wide // seqs
        )
        came_far, grads_here = lax.optimization_barrier((came_far, grads_here))
        hidden = [near[0], far[0]]
    else:
        key_part, value_part = [x.reshape(wide, quarter) for x in every]
        ffn_parts = seq_gather(ffn_in)
        rows = jnp.concatenate(ffn_parts, 0)
        og_rows = jnp.concatenate(
            [
                jnp.concatenate([g.reshape(per, BLOCK, wide), x.reshape(per, 16, wide)], 1).reshape(-1, wide)
                for g, x in zip(og_parts, extra_parts)
            ],
            0,
        )
        active = jax.nn.relu(dot(rows, key_part, NN))
        hidden = [(active * active).astype(LOW)]
        grad_pre = (dot(og_rows, value_part, NN) * 2.0 * active).astype(LOW)
        own_part = dot(grad_pre, key_part, NT).reshape(seqs, per * TALL, wide)
        own_part = lax.psum_scatter(own_part, ("ys", "core"), scatter_dimension=0, tiled=True)[0]
        came_core, came_far = jnp.zeros_like(own_part), jnp.zeros_like(ffn_in)
        is_main = (jnp.arange(rows.shape[0]) % TALL < BLOCK).astype(LOW)[:, None]
        grads_here = [dot(og_rows * is_main, hidden[0], TN), dot(rows * is_main, grad_pre, TN)]
    grad_middle, middle_low, grad_out, cols_ffn = middle_back(
        own_part, came_core, came_far, middle, output_gradient, out_weight, settings, local, begins, heads_axis,
        seqs,
    )
    grad_heads = lax.all_to_all(grad_out, HEAD_AXES, split_axis=0, concat_axis=0, tiled=True)
    out_parts = seq_gather(out_rows)
    which = lax.axis_index(("ys", "core"))
    if whole_quarter:

        def quarter_from(k):
            sent = lax.dynamic_index_in_dim(middle_low, which ^ k, 0, keepdims=False)
            return lax.ppermute(sent, ("ys", "core"), [(i, i ^ k) for i in range(seqs)])

        low_parts = [lax.dynamic_index_in_dim(middle_low, which, 0, keepdims=False)]
        low_parts += [quarter_from(k) for k in (1, 2, 3)]
        grads_here = output_grads(out_parts, low_parts, grads_here)
    else:
        right = lax.all_to_all(middle_low, ("ys", "core"), split_axis=0, concat_axis=0, tiled=True)
        grads_here.append(dot(jnp.concatenate(out_parts, 0), right.reshape(-1, right.shape[2]), TN))
        grads_here = jnp.concatenate(grads_here, 1).astype(LOW)
    grad_heads, grads_here = lax.optimization_barrier((grad_heads, grads_here))
    grads_here = lax.psum_scatter(grads_here, HEAD_AXES, scatter_dimension=0, tiled=True)

    scan_grads, first_grad, cols_scan = scan_backward(
        parts, values, joined, scanned, gate, grad_heads.reshape(blocks, BLOCK, width), pre, first_group,
        own, states, mats, home, begins, PASSES,
    )
    first_grad = taken_blocks(first_grad.reshape(blocks, BLOCK, width), order)
    first_came = lax.all_to_all(
        first_grad.reshape(heads_axis, rows_here, width), HEAD_AXES, split_axis=0, concat_axis=0, tiled=True
    )

    share = wide // seqs
    thin = low_rank // seqs
    fold = heads_axis // seqs

    cut = 3 * width
    end = cut + low_rank

    def over_ys(left, right, up_sums):
        up_sums = up_sums.astype(LOW).reshape(seqs, thin, width)
        if ys != 2:
            rows_out = jnp.concatenate([left, right], 1)
            by_feature = jnp.concatenate([rows_out[:cut], rows_out[end:]], 0)
            by_feature = by_feature.reshape(-1, seqs, share).transpose(1, 0, 2)
            return by_feature, rows_out[cut:end].reshape(seqs, thin, wide), up_sums
        index = lax.axis_index("ys")

        def part_of(which):
            half = jnp.where(which == 0, left, right)
            rank = [lax.dynamic_slice_in_dim(x, cut + which * 2 * thin, 2 * thin, 0) for x in (left, right)]
            return jnp.concatenate([half[:cut], half[end:]] + rank, 0)

        total = part_of(index).astype(F32) + swap(part_of(1 - index), "ys").astype(F32)
        features = total.shape[0] - 4 * thin
        by_rank = total[features:].reshape(2, 2, thin, -1).transpose(1, 2, 0, 3)
        return total[:features].reshape(-1, 2, share), by_rank, seq_step(up_sums, "ys")

    def over_core(by_feature, by_rank, up_sums):
        if ys != 2:
            return [
                lax.psum_scatter(x, ("ys", "core"), scatter_dimension=0, tiled=True)[0].astype(F32)
                for x in (by_feature, by_rank, up_sums)
            ]

        def step(x, dim):
            sent = lax.dynamic_index_in_dim(x, 1 - core, dim, keepdims=False).astype(LOW)
            return lax.dynamic_index_in_dim(x, core, dim, keepdims=False) + swap(sent, "core").astype(F32)

        return step(by_feature, 1), step(by_rank, 0).reshape(thin, wide), step(up_sums, 0)

    def to_owners(by_feature, by_rank):
        rows_low = by_feature.astype(LOW)
        squares = rows_low[:cut].reshape(cut, fold, width)
        mixed = by_rank.astype(LOW).reshape(thin, heads_axis, width).transpose(1, 0, 2)
        cols_part = rows_low[cut:][:count].reshape(count, heads_axis, -1)
        cols_part = jnp.pad(
            cols_part.transpose(1, 0, 2), ((0, 0), (0, -count % 8), (0, width - cols_part.shape[2]))
        )
        mixed = lax.all_to_all(
            jnp.concatenate([mixed, cols_part], 1), HEAD_AXES, split_axis=0, concat_axis=0, tiled=True
        )
        came = []
        for k in range(fold):
            sent = lax.dynamic_index_in_dim(squares, (head + k) % fold, 1, keepdims=False)
            came.append(
                lax.ppermute(
                    sent, every_axis, [(q * heads_axis + h, owner(q, h, (h + k) % fold)) for q, h in pairs]
                )
            )
        return mixed, came

    every_axis = ("ys", "core") + HEAD_AXES
    pairs = [(q, h) for q in range(seqs) for h in range(heads_axis)]

    def owner(q, h, j):
        return (h // fold) * heads_axis + q * fold + j

    sizes = (size_z, size_x)

    def others_x(blocks_back):
        return [
            lax.ppermute(blocks_back[k], "hx", [(i, i ^ k) for i in range(size_x)])
            for k in range(1, size_x)
        ]

    def after_x(kept_blocks, came):
        total = kept_blocks.astype(F32)
        for x in came:
            total = total + x.astype(F32)
        total = total.reshape(size_z, rows_here, -1)
        return total[0], [total[k].astype(LOW) for k in range(1, size_z)]

    def others_z(sent):
        return [
            lax.ppermute(x, "hz", [(i, i ^ k) for i in range(size_z)]) for k, x in enumerate(sent, 1)
        ]

    def half_back(part, grads):
        outs = project_back(
            part, 2, group, stats, grads, mids, (cols_scan, cols_ffn), settings, weights, place, turn_x, turn_row,
            begins, head[None], per, sizes,
        )
        return outs[:size_x], outs[size_x:]

    left_blocks, (left_sum, up_sums) = half_back(0, scan_grads)
    left_came = others_x(left_blocks)
    scan_grads, left_sum, first_came = lax.optimization_barrier((scan_grads, left_sum, first_came))
    right_blocks, (right_sum,) = half_back(1, scan_grads)
    right_blocks, left_came = lax.optimization_barrier((right_blocks, left_came))
    right_came = others_x(right_blocks)
    left_own, left_sent = after_x(left_blocks[0], left_came)
    left_sent, right_sum, hidden = lax.optimization_barrier((left_sent, right_sum, hidden))
    left_z = others_z(left_sent)
    sums = over_ys(left_sum, right_sum, up_sums)
    outs = [dot(h, value_part, NT) for h in hidden]
    right_came, outs, grads_here = lax.optimization_barrier((right_came, outs, grads_here))
    right_own, right_sent = after_x(right_blocks[0], right_came)
    right_sent, left_z, sums, outs = lax.optimization_barrier((right_sent, left_z, sums, outs))
    right_z = others_z(right_sent)
    by_feature, by_rank, up_sums = over_core(*sums)
    right_z[0], by_feature, by_rank = lax.optimization_barrier((right_z[0], by_feature, by_rank))
    mixed, came = to_owners(by_feature, by_rank)
    if whole_quarter:
        came_core, came_far = seq_return(*[x for out in outs for x in jnp.split(out, 2, 0)])
        right_z, came_core, came_far = lax.optimization_barrier((right_z, came_core, came_far))
    right_z[0], first_came = lax.optimization_barrier((right_z[0], first_came))
    first_value_grad = first_came.transpose(1, 0, 2).reshape(rows_here, wide).astype(F32)
    right_z, up_sums, mixed, came = lax.optimization_barrier((right_z, up_sums, mixed, came))
    back = jnp.concatenate(
        [own + sum(x.astype(F32) for x in z) for own, z in ((left_own, left_z), (right_own, right_z))], 1
    )
    value_sum, key_sum, out_sum = jnp.split(grads_here.astype(F32), (quarter, 2 * quarter), 1)

    unit, scale = norm_rows(tokens.astype(F32))
    tokens_grad = grad_middle + norm_back(back, unit, scale, settings[0])
    mixed = jnp.sum(mixed.astype(F32), 0)
    channel_grad = mixed[thin : thin + count, :weight_rows].T
    down_grad = mixed[:thin].T

    def main_of(x):
        return x.reshape(-1, per, TALL, wide)[:, :, :BLOCK].reshape(-1, rows_here, wide)

    layer_out = main_of(middle)[0]
    if whole_quarter:
        own_out = jnp.split(outs[0], 2, 0)[0]
        layer_out = layer_out + main_of(own_out)[0] + main_of(came_core)[0] + main_of(came_far)[0].astype(F32)
    else:
        layer_out = layer_out + lax.psum_scatter(
            main_of(outs[0]), ("ys", "core"), scatter_dimension=0, tiled=True
        )[0]
    came = jnp.stack(came, 0)
    came = taken_blocks(came, (head - jnp.arange(fold, dtype=jnp.int32)) % fold)
    came = came.reshape(fold, 3, width, width).transpose(1, 3, 0, 2).reshape(3, width, share)
    recept_grad, key_grad, value_grad = [came[i].astype(F32) for i in range(3)]
    up_grad = up_sums.T
    return (
        layer_out.astype(LOW),
        tokens_grad,
        first_value_grad,
        channel_grad,
        recept_grad,
        key_grad,
        value_grad,
        out_sum,
        down_grad,
        up_grad,
        key_sum,
        value_sum,
    )


def solution(mesh):
    seqs, heads = mesh.devices.shape
    split = Mesh(mesh.devices.reshape(seqs // 2, 2, 4, heads // 4), ("ys", "core") + HEAD_AXES)
    rows = P(("ys", "core") + HEAD_AXES, None)
    table = P(("ys", "core"), None)
    square = P(HEAD_AXES, ("ys", "core"))
    return jax.shard_map(
        body,
        mesh=split,
        in_specs=(rows,) * 3 + (table,) * 3 + (rows,) * 9,
        out_specs=(rows,) * 4 + (square,) * 8,
        check_vma=False,
    )
```

```python
import functools
import jax
import jax.numpy as jnp
from jax import lax
from jax.experimental import pallas as pl
from jax.experimental.pallas import tpu as pltpu
from jax.sharding import Mesh
from jax.sharding import PartitionSpec as P

DECAY_RANK = 64
DA = 64
DV = 32
BLOCK = 128
SPAN = 64
HEAD = 64
FORWARD_CHUNKS = 8
BACKWARD_CHUNKS = 4
LOW = jnp.bfloat16
F32 = jnp.float32
NN = (((1,), (0,)), ((), ()))
NT = (((1,), (1,)), ((), ()))
TN = (((0,), (0,)), ((), ()))
PASSES = {"pair": 3, "inv": 3, "val": 3, "chain": 3, "bpair": 3}


def work(micros):
    return pl.CostEstimate(flops=0, bytes_accessed=int(micros * 3_000), transcendentals=0)


def dot(a, b, dims):
    return lax.dot_general(a, b, dims, preferred_element_type=F32)


def halves(x):
    high = x.astype(LOW)
    return high, (x - high.astype(F32)).astype(LOW)


def product(a, b, dims, passes):
    if passes == 1:
        return dot(a.astype(LOW), b.astype(LOW), dims)
    la, lb = dims[0][0][0], dims[0][1][0]
    a_high, a_low = halves(a)
    if passes == 2:
        b = b.astype(LOW)
        return dot(jnp.concatenate([a_high, a_low], la), jnp.concatenate([b, b], lb), dims)
    b_high, b_low = halves(b)
    first = dot(jnp.concatenate([a_high, a_low], la), jnp.concatenate([b_high, b_high], lb), dims)
    return first + dot(a_high, b_low, dims)


def head_masks(heads):
    lane = lax.broadcasted_iota(jnp.int32, (1, heads * HEAD), 1) // HEAD
    return [(lane == h).astype(F32) for h in range(heads)]


def stacked(x, masks):
    if len(masks) == 1:
        return x
    return jnp.concatenate([x * m for m in masks], 0)


def unstacked(x, heads):
    rows = x.shape[0] // heads
    out = x[:rows]
    for h in range(1, heads):
        out = out + x[h * rows : (h + 1) * rows]
    return out


def head_ones(width):
    row = lax.broadcasted_iota(jnp.int32, (width, width), 0) // HEAD
    col = lax.broadcasted_iota(jnp.int32, (width, width), 1) // HEAD
    return (row == col).astype(LOW)


def head_sum(x, ones):
    high, low = halves(x)
    return dot(jnp.concatenate([high, low], 1), jnp.concatenate([ones, ones], 0), NN)


class Chunk:
    def __init__(self, r, lw, k, kn, a, begins, start, heads):
        self.heads = heads
        masks = head_masks(heads)
        rows = heads * SPAN
        local = [jnp.where(b >= start, b - start, SPAN) for b in begins]
        row_t = lax.broadcasted_iota(jnp.int32, (rows, 1), 0) % SPAN
        col_t = lax.broadcasted_iota(jnp.int32, (1, rows), 1) % SPAN
        row_seg = sum((row_t >= b).astype(jnp.int32) for b in local)
        col_seg = sum((col_t >= b).astype(jnp.int32) for b in local)
        last = sum((b < SPAN).astype(jnp.int32) for b in local)
        same = row_seg == col_seg
        self.strict = same & (row_t > col_t)
        self.upto = same & (row_t >= col_t)
        self.carried = (row_seg == 0).astype(F32)
        self.final = (row_seg == last).astype(F32)
        self.whole = (last == 0).astype(F32)
        tri_r = lax.broadcasted_iota(jnp.int32, (SPAN, SPAN), 0)
        tri_c = lax.broadcasted_iota(jnp.int32, (SPAN, SPAN), 1)
        running = dot((tri_r >= tri_c).astype(LOW), lw, NN)
        lw = lw.astype(F32)
        decay = jnp.exp(running)
        before = jnp.exp(running - lw)
        inverse = jnp.exp(-running)
        end = running[SPAN - 1 : SPAN]
        to_end = jnp.exp(end - running)
        self.end = jnp.exp(end)
        kn = kn.astype(F32)
        beta = kn * a.astype(F32)
        k = k.astype(F32)
        self.decay, self.before, self.inverse, self.to_end = decay, before, inverse, to_end
        self.a_hat = stacked(-kn * before, masks)
        self.r_hat = stacked(r.astype(F32) * decay, masks)
        self.b_hat = stacked(beta * inverse, masks)
        self.k_hat = stacked(k * inverse, masks)
        self.b_end = stacked(beta * to_end, masks) * self.final
        self.k_end = stacked(k * to_end, masks) * self.final


def block_inverses(all_pairs, passes):
    rows = all_pairs[0].shape[0]
    row = lax.broadcasted_iota(jnp.int32, (rows, rows), 0)
    col = lax.broadcasted_iota(jnp.int32, (rows, rows), 1)
    eye = (row == col).astype(F32)

    def products(left, right):
        return [product(a, b, NN, passes) for a, b in zip(left, right)]

    within = row // 8 == col // 8
    small = [jnp.where(within, pairs, 0.0) for pairs in all_pairs]
    square = products(small, small)
    fourth = products(square, square)
    first = [eye + x for x in small]
    inverse = [a + b for a, b in zip(first, products(first, square))]
    inverse = [a + b for a, b in zip(inverse, products(inverse, fourth))]
    size = 8
    while size < SPAN:
        within = (row // (2 * size) == col // (2 * size)) & (row // size != col // size)
        cross = [jnp.where(within, pairs, 0.0) for pairs in all_pairs]
        step = products(products(inverse, cross), inverse)
        inverse = [a + b for a, b in zip(inverse, step)]
        size *= 2
    return inverse


def group_norm_parts(scanned, ones):
    center = scanned - head_sum(scanned, ones) * (1.0 / HEAD)
    spread = head_sum(center * center, ones) * (1.0 / HEAD)
    scale = lax.rsqrt(spread + 0.00064)
    return center * scale, scale


def scan_forward_kernel(
    heads, p, home_ref, begins_ref, parts_ref, pre_ref, gate_ref, cols_ref, *rest,
):
    first_refs, rest = rest[: FORWARD_CHUNKS * SPAN // BLOCK], rest[FORWARD_CHUNKS * SPAN // BLOCK :]
    values_ref, out_ref, joined_ref, scanned_ref, state_ref, mats_ref, state = rest
    step = pl.program_id(0)
    width = heads * HEAD

    @pl.when(step == 0)
    def _():
        state[...] = jnp.zeros_like(state)

    begins = [begins_ref[i] for i in range(begins_ref.shape[0])]
    masks = head_masks(heads)
    n = heads * SPAN
    eye = (
        lax.broadcasted_iota(jnp.int32, (width, width), 0)
        == lax.broadcasted_iota(jnp.int32, (width, width), 1)
    ).astype(F32)
    first = jnp.concatenate([ref[0] for ref in first_refs], 0).astype(F32)
    mix = jax.nn.sigmoid(cols_ref[5:6] + pre_ref[4])
    values = (pre_ref[1] + (first - pre_ref[1]) * mix).astype(LOW)
    values_ref[...] = values
    held = []
    for c in range(FORWARD_CHUNKS):
        rows = pl.ds(c * SPAN, SPAN)
        r, lw, k, kn, a = [parts_ref[i, rows] for i in range(5)]
        v = values[c * SPAN : (c + 1) * SPAN]
        q = Chunk(r, lw, k, kn, a, begins, (step * FORWARD_CHUNKS + c) * SPAN, heads)
        v_st = stacked(v.astype(F32), masks).astype(LOW)
        held.append((q, r, k, v, v_st))
    all_pairs = [
        product(
            jnp.concatenate([q.a_hat, q.r_hat], 0), jnp.concatenate([q.b_hat, q.k_hat], 0), NT, p["pair"]
        )
        for q, *_ in held
    ]
    l_ab = [jnp.where(h[0].strict, x[:n, :n], 0.0) for h, x in zip(held, all_pairs)]
    l_ak = [jnp.where(h[0].strict, x[:n, n:], 0.0) for h, x in zip(held, all_pairs)]
    l_rb = [jnp.where(h[0].upto, x[n:, :n], 0.0) for h, x in zip(held, all_pairs)]
    l_rk = [jnp.where(h[0].upto, x[n:, n:], 0.0) for h, x in zip(held, all_pairs)]
    both_v = [
        product(jnp.concatenate([ak, rk], 0), h[4], NN, 2 if p["val"] == 3 else 1)
        for ak, rk, h in zip(l_ak, l_rk, held)
    ]
    inverses = block_inverses(l_ab, p["inv"])
    solved = [
        product(t, jnp.concatenate([h[0].a_hat * h[0].carried, b[:n]], 1), NN, p["val"])
        for t, h, b in zip(inverses, held, both_v)
    ]
    ends = [product(x, h[0].b_end, TN, p["val"]) for x, h in zip(solved, held)]
    grown = []
    for q, _, _, _, v_st in held:
        if p["val"] == 3:
            k_high, k_low = halves(q.k_end)
            grown.append(dot(jnp.concatenate([v_st, v_st], 0), jnp.concatenate([k_high, k_low], 0), TN))
        else:
            grown.append(dot(v_st, q.k_end.astype(LOW), TN))
    ready = []
    for c in range(FORWARD_CHUNKS):
        q, r, k, v, _ = held[c]
        through = product(l_rb[c], solved[c], NN, p["val"])
        r_thru = q.r_hat * q.carried + through[:, :width]
        o_val = both_v[c][n:] + through[:, width:]
        move = eye * (q.end * q.whole) + ends[c][:width]
        gain = ends[c][width:] + grown[c]
        mats = [
            inverses[c], l_ak[c], l_rb[c], l_rk[c], solved[c][:, :width], solved[c][:, width:], move, r_thru,
        ]
        for i, m in enumerate(mats):
            mats_ref[c, i] = m
        ready.append((move, gain, r_thru, o_val, r, k, v))
    ones = head_ones(width)
    now = state[...]
    begun = []
    for c in range(FORWARD_CHUNKS):
        begun.append(now)
        state_ref[c] = now
        now = product(now, ready[c][0], NN, p["chain"]) + ready[c][1]
    state[...] = now
    for c in range(FORWARD_CHUNKS):
        rows = pl.ds(c * SPAN, SPAN)
        _, _, r_thru, o_val, r, k, v = ready[c]
        scanned = unstacked(o_val + product(r_thru, begun[c], NT, p["val"]), heads)
        scanned_ref[rows] = scanned
        unit, _ = group_norm_parts(scanned, ones)
        bonus = head_sum(r.astype(F32) * k.astype(F32) * cols_ref[0:1], ones)
        joined = unit * cols_ref[1:2] + cols_ref[2:3] + bonus * v.astype(F32)
        joined = joined.astype(LOW)
        joined_ref[rows] = joined
        out_ref[rows] = (joined.astype(F32) * gate_ref[rows]).astype(LOW)


def scan_forward(parts, pre, first, gate, cols, home, begins, p):
    _, total, width = parts.shape
    heads = width // HEAD
    rows = FORWARD_CHUNKS * SPAN
    n = heads * SPAN
    spans = total // SPAN
    assert n == width
    row_spec = pl.BlockSpec((rows, width), lambda i, *_: (i, 0))
    per_step = rows // BLOCK

    def stored(which):
        return pl.BlockSpec((1, BLOCK, width), lambda i, home, b: (home[per_step * i + which], 0, 0))

    return pl.pallas_call(
        functools.partial(scan_forward_kernel, heads, p),
        grid_spec=pltpu.PrefetchScalarGridSpec(
            num_scalar_prefetch=2,
            grid=(total // rows,),
            in_specs=[
                pl.BlockSpec((5, rows, width), lambda i, *_: (0, i, 0)),
                pl.BlockSpec((5, rows, width), lambda i, *_: (0, i, 0)),
                row_spec,
                pl.BlockSpec(cols.shape, lambda i, *_: (0, 0)),
            ]
            + [stored(w) for w in range(per_step)],
            out_specs=[
                row_spec,
                row_spec,
                row_spec,
                row_spec,
                pl.BlockSpec((FORWARD_CHUNKS, width, width), lambda i, *_: (i, 0, 0)),
                pl.BlockSpec((FORWARD_CHUNKS, 8, n, width), lambda i, *_: (i, 0, 0, 0)),
            ],
            scratch_shapes=[pltpu.VMEM((width, width), F32)],
        ),
        out_shape=[
            jax.ShapeDtypeStruct((total, width), LOW),
            jax.ShapeDtypeStruct((total, width), LOW),
            jax.ShapeDtypeStruct((total, width), LOW),
            jax.ShapeDtypeStruct((total, width), F32),
            jax.ShapeDtypeStruct((spans, width, width), F32),
            jax.ShapeDtypeStruct((spans, 8, n, width), F32),
        ],
        compiler_params=pltpu.CompilerParams(vmem_limit_bytes=60 * 1024 * 1024),
        cost_estimate=work(80),
    )(home, begins, parts, pre, gate, cols, *[first] * per_step)


def scan_backward_kernel(
    heads, p, home_ref, begins_ref, parts_ref, values_ref, joined_ref, scanned_ref, gate_ref, grad_a_ref,
    grad_b_ref, pre_ref, first_a_ref, first_b_ref, cols_ref, state_ref, mats_ref, *rest,
):
    steps = pl.num_programs(0)
    step = steps - 1 - pl.program_id(0)
    grads_ref, first_grad_ref, col_grad_ref, state = rest
    width = heads * HEAD
    n = heads * SPAN

    @pl.when(pl.program_id(0) == 0)
    def _():
        state[...] = jnp.zeros_like(state)
        col_grad_ref[...] = jnp.zeros_like(col_grad_ref)

    begins = [begins_ref[i] for i in range(begins_ref.shape[0])]
    masks = head_masks(heads)
    ones = head_ones(width)
    tri_r = lax.broadcasted_iota(jnp.int32, (SPAN, SPAN), 0)
    tri_c = lax.broadcasted_iota(jnp.int32, (SPAN, SPAN), 1)
    later = (tri_c >= tri_r).astype(LOW)
    after = (tri_c > tri_r).astype(LOW)
    sums = [jnp.zeros((1, width), F32) for _ in range(8)]

    def add(slot, value):
        sums[slot] = sums[slot] + jnp.sum(value, 0, keepdims=True)

    c13, c14 = cols_ref[0:1], cols_ref[1:2]
    grads = jnp.concatenate([grad_a_ref[0], grad_b_ref[0]], 0).astype(F32)
    firsts = jnp.concatenate([first_a_ref[0], first_b_ref[0]], 0).astype(F32)
    ready = []
    for c in range(BACKWARD_CHUNKS):
        rows = pl.ds(c * SPAN, SPAN)
        r, lw, k, kn, a = [parts_ref[i, rows] for i in range(5)]
        v = values_ref[rows]
        q = Chunk(r, lw, k, kn, a, begins, (step * BACKWARD_CHUNKS + c) * SPAN, heads)
        r, k, v = r.astype(F32), k.astype(F32), v.astype(F32)
        unit, scale = group_norm_parts(scanned_ref[rows], ones)
        grad_out = grads[c * SPAN : (c + 1) * SPAN]
        grad_joined = (grad_out * gate_ref[rows]).astype(LOW).astype(F32)
        grad_gate = (grad_out * joined_ref[rows].astype(F32)).astype(LOW)
        add(6, grad_joined * unit)
        add(7, grad_joined)
        grad_unit = grad_joined * c14
        grad_scan = scale * (
            grad_unit
            - head_sum(grad_unit, ones) * (1.0 / HEAD)
            - unit * (head_sum(grad_unit * unit, ones) * (1.0 / HEAD))
        )
        bonus = head_sum(r * k * c13, ones)
        grad_bonus = head_sum(grad_joined * v, ones)
        add(5, grad_bonus * r * k)
        own_r = grad_bonus * k * c13
        own_k = grad_bonus * r * c13
        own_v = grad_joined * bonus
        d_out = stacked(grad_scan, masks)
        flow = product(d_out, mats_ref[c, 7], TN, p["val"])
        ready.append((q, d_out, flow, own_r, own_k, own_v, grad_gate))
    now = state[...]
    ended = [None] * BACKWARD_CHUNKS
    for c in reversed(range(BACKWARD_CHUNKS)):
        ended[c] = now
        now = product(now, mats_ref[c, 6], NT, p["chain"]) + ready[c][2]
    state[...] = now
    span = range(BACKWARD_CHUNKS)
    mats = [[mats_ref[c, i] for i in range(6)] for c in span]
    begin = [state_ref[c] for c in span]
    chunks = [ready[c][0] for c in span]
    d_outs = [ready[c][1] for c in span]
    v_st = [stacked(values_ref[pl.ds(c * SPAN, SPAN)].astype(F32), masks) for c in span]
    update = [mats[c][5] + product(mats[c][4], begin[c], NT, p["val"]) for c in span]
    through = [product(mats[c][2], d_outs[c], TN, p["val"]) for c in span]
    through = [
        through[c] + product(chunks[c].b_end, ended[c], NT, p["val"]) for c in span
    ]
    back = [product(mats[c][0], through[c], TN, p["val"]) for c in span]
    left = [jnp.concatenate([back[c], d_outs[c]], 0) for c in span]
    right = [jnp.concatenate([update[c], v_st[c]], 0) for c in span]
    d_hats = [product(left[c], begin[c], NN, p["val"]) for c in span]
    pair_grads = [product(left[c], right[c], NT, p["bpair"]) for c in span]
    for c in span:
        strict, upto = chunks[c].strict.astype(F32), chunks[c].upto.astype(F32)
        mask = jnp.concatenate(
            [jnp.concatenate([strict, strict], 1), jnp.concatenate([upto, upto], 1)], 0
        )
        pair_grads[c] = pair_grads[c] * mask
    all_asks = []
    for c in span:
        q = chunks[c]
        keys = jnp.concatenate([q.b_hat, q.k_hat], 0)
        carried = jnp.concatenate([q.carried, q.carried], 0)
        all_asks.append(d_hats[c] * carried + product(pair_grads[c], keys, NN, p["bpair"]))
    all_keys = [
        product(
            pair_grads[c], jnp.concatenate([chunks[c].a_hat, chunks[c].r_hat], 0), TN, p["bpair"]
        )
        for c in span
    ]
    all_ends = [product(right[c], ended[c], NN, p["val"]) for c in span]
    all_vals = [
        product(jnp.concatenate([mats[c][1], mats[c][3]], 0), left[c], TN, p["val"]) for c in span
    ]
    all_vals = [
        all_vals[c] + product(chunks[c].k_end, ended[c], NT, p["val"]) for c in span
    ]
    for c in span:
        rows = pl.ds(c * SPAN, SPAN)
        q, _, _, own_r, own_k, own_v, grad_gate = ready[c]
        end_grad, begin_now = ended[c], begin[c]
        r, lw, k, kn, a = [parts_ref[i, rows].astype(F32) for i in range(5)]
        v = values_ref[rows].astype(F32)
        d_asks, d_keys, d_val = all_asks[c], all_keys[c], all_vals[c]
        d_ends = all_ends[c] * jnp.concatenate([q.final, q.final], 0)
        d_a, d_r = unstacked(d_asks[:n], heads) * q.before, unstacked(d_asks[n:], heads) * q.decay
        d_b = unstacked(d_keys[:n], heads) * q.inverse
        d_k = unstacked(d_keys[n:], heads) * q.inverse
        e_b = unstacked(d_ends[:n], heads) * q.to_end
        e_k = unstacked(d_ends[n:], heads) * q.to_end
        d_v = unstacked(d_val, heads) + own_v
        beta = kn * a
        end_part = e_b * beta + e_k * k
        here = d_r * r - d_b * beta - d_k * k - end_part
        ahead = -d_a * kn
        at_end = jnp.sum(end_part, 0, keepdims=True) + q.whole * q.end * jnp.sum(
            begin_now * end_grad, 0, keepdims=True
        )
        high, low = halves(here)
        high2, low2 = halves(ahead)
        d_lw = at_end + dot(
            jnp.concatenate([later, later, after, after], 1),
            jnp.concatenate([high, low, high2, low2], 0),
            NN,
        )
        d_b = d_b + e_b
        d_k = d_k + e_k + own_k
        d_r = d_r + own_r
        d_kn = d_b * a - d_a
        d_rate = d_b * kn
        g_r, g_lw, g_k, g_kn, g_a, g_v = [
            x.astype(LOW).astype(F32) for x in (d_r, d_lw, d_k, d_kn, d_rate, d_v)
        ]
        key_pre, value_pre, decay_up, rate_up, value_up = [pre_ref[i, rows] for i in range(5)]
        first = firsts[c * SPAN : (c + 1) * SPAN]
        c8, c9, c10, c11, c12 = [cols_ref[i : i + 1] for i in range(3, 8)]
        sig = jax.nn.sigmoid(c8 + decay_up)
        log_decay = -0.6065306597126334 * sig
        g_decay = g_lw * log_decay * (1.0 - sig)
        add(0, g_decay)
        rate = jax.nn.sigmoid(c9 + rate_up)
        g_rate = (g_a + g_k * key_pre * c12) * rate * (1.0 - rate)
        add(1, g_rate)
        g_key = g_k * (1.0 + (rate - 1.0) * c12)
        add(4, g_k * key_pre * (rate - 1.0))
        scaled = key_pre * c11
        norm = lax.rsqrt(head_sum(scaled * scaled, ones) + 1e-06)
        unit = scaled * norm
        g_scaled = norm * (g_kn - unit * head_sum(g_kn * unit, ones))
        g_key = g_key + g_scaled * c11
        add(3, g_scaled * key_pre)
        mix = jax.nn.sigmoid(c10 + value_up)
        g_value = g_v * (1.0 - mix)
        first_grad_ref[rows] = (g_v * mix).astype(first_grad_ref.dtype)
        g_vup = g_v * (first - value_pre) * mix * (1.0 - mix)
        add(2, g_vup)
        for i, x in enumerate((g_r, g_key, g_value, g_decay, g_rate, g_vup)):
            grads_ref[i, rows] = x.astype(LOW)
        grads_ref[6, rows] = grad_gate
    col_grad_ref[...] += jnp.concatenate(sums, 0)


def scan_backward(parts, values, joined, scanned, gate, grad, pre, first, cols, states, mats, home, begins, p):
    _, total, width = parts.shape
    heads = width // HEAD
    rows = BACKWARD_CHUNKS * SPAN
    n = heads * SPAN
    steps = total // rows
    row_spec = pl.BlockSpec((rows, width), lambda i, *_: (steps - 1 - i, 0))
    assert rows == 2 * BLOCK

    def stored(which):
        return pl.BlockSpec(
            (1, BLOCK, width), lambda i, home, b: (home[2 * (steps - 1 - i) + which], 0, 0)
        )

    return pl.pallas_call(
        functools.partial(scan_backward_kernel, heads, p),
        grid_spec=pltpu.PrefetchScalarGridSpec(
            num_scalar_prefetch=2,
            grid=(steps,),
            in_specs=[
                pl.BlockSpec((5, rows, width), lambda i, *_: (0, steps - 1 - i, 0)),
                row_spec,
                row_spec,
                row_spec,
                row_spec,
                stored(0),
                stored(1),
                pl.BlockSpec((5, rows, width), lambda i, *_: (0, steps - 1 - i, 0)),
                stored(0),
                stored(1),
                pl.BlockSpec(cols.shape, lambda i, *_: (0, 0)),
                pl.BlockSpec((BACKWARD_CHUNKS, width, width), lambda i, *_: (steps - 1 - i, 0, 0)),
                pl.BlockSpec((BACKWARD_CHUNKS, 8, n, width), lambda i, *_: (steps - 1 - i, 0, 0, 0)),
            ],
            out_specs=[
                pl.BlockSpec((7, rows, width), lambda i, *_: (0, steps - 1 - i, 0)),
                row_spec,
                pl.BlockSpec((8, width), lambda i, *_: (0, 0)),
            ],
            scratch_shapes=[pltpu.VMEM((width, width), F32)],
        ),
        out_shape=[
            jax.ShapeDtypeStruct((7, total, width), LOW),
            jax.ShapeDtypeStruct((total, width), LOW),
            jax.ShapeDtypeStruct((8, width), F32),
        ],
        compiler_params=pltpu.CompilerParams(vmem_limit_bytes=60 * 1024 * 1024),
        cost_estimate=work(60),
    )(home, begins, parts, values, joined, scanned, gate, grad, grad, pre, first, first, cols, states, mats)


def norm_rows(x):
    center = x - jnp.mean(x, -1, keepdims=True)
    scale = lax.rsqrt(jnp.mean(center * center, -1, keepdims=True) + 1e-05)
    return center * scale, scale


def keep_rows(rows, first, begins):
    position = first + lax.broadcasted_iota(jnp.int32, (rows, 1), 0)
    hit = position == begins[0]
    for b in begins[1:]:
        hit = hit | (position == b)
    return 1.0 - hit.astype(F32)


def rows_down(x, edge):
    row = lax.broadcasted_iota(jnp.int32, (x.shape[0], 1), 0)
    return jnp.where(row == 0, edge, pltpu.roll(x, 1, 0))


def rows_up(x, edge):
    row = lax.broadcasted_iota(jnp.int32, (x.shape[0], 1), 0)
    return jnp.where(row == x.shape[0] - 1, edge, pltpu.roll(x, x.shape[0] - 1, 0))


def lane_below(limit):
    return lax.broadcasted_iota(jnp.int32, (1, 128), 1) < limit


def kept(x, mask):
    return jnp.where(mask, x, jnp.zeros_like(x))


class SmallWeights:
    def __init__(self, small, up):
        self.pair, self.gate, self.value = small[:, :128], small[:, 128:256], small[:, 256:384]
        self.up_pair, self.up_gate = up[:, 384:512], up[:, 512:640]
        self.up_value = jnp.concatenate([up[:, 320:352], jnp.zeros((up.shape[0], 96), LOW)], 1)


PROJECT_BLOCKS = 4
BACK_BLOCKS = 4


def project_kernel(place_ref, begins_ref, *refs):
    x_refs, refs = refs[:PROJECT_BLOCKS], refs[PROJECT_BLOCKS:]
    cols_ref, own_ref, columns_ref, small_ref, up_ref, ends_ref, stats_ref, parts_ref, gate_ref = refs[:9]
    pre_ref, pair_ref, vm_ref, gs_ref, edge = refs[9:]
    step = pl.program_id(0)

    @pl.when(step == 0)
    def _():
        edge[...] = jnp.zeros_like(edge)

    begins = [begins_ref[i] for i in range(begins_ref.shape[0])]
    for i, ref in enumerate(x_refs):
        ends_ref[i] = jnp.concatenate([ref[0, :16], ref[0, BLOCK - 16 :]], 0)
    x = jnp.concatenate([ref[0] for ref in x_refs], 0).astype(F32)
    rows = x.shape[0]
    mean = jnp.mean(x, -1, keepdims=True)
    center = x - mean
    scale = lax.rsqrt(jnp.mean(center * center, -1, keepdims=True) + 1e-05)
    unit = center * scale
    stats_ref[...] = jnp.concatenate([mean, scale], 1)
    normed = unit * cols_ref[0:1] + cols_ref[1:2]
    moved = rows_down(normed, edge[0:1]) * keep_rows(rows, step * rows, begins)
    edge[0:1] = normed[rows - 1 : rows]
    diff = moved - normed
    mixed = [(normed + diff * cols_ref[i : i + 1]).astype(LOW) for i in range(2, 8)]
    in_r, in_d, in_k, in_v, in_a, in_g = mixed
    low = SmallWeights(small_ref[...], up_ref[...])
    width = own_ref.shape[1]
    recept = dot(in_r, columns_ref[:, :width], NN)
    key_pre = dot(in_k, columns_ref[:, width : 2 * width], NN)
    values = dot(in_v, jnp.concatenate([columns_ref[:, 2 * width :], low.value], 1), NN)
    value_pre = values[:, :width]
    value_mid = kept(values[:, width:], lane_below(DV)).astype(LOW)
    decay, rate = dot(in_d, low.pair, NN), dot(in_a, low.pair, NN)
    pair = jnp.where(lane_below(DECAY_RANK), jnp.tanh(decay), rate)
    pair_low = pair.astype(LOW)
    gate_sig = jax.nn.sigmoid(dot(in_g, low.gate, NN))
    decay_up = dot(kept(pair_low, lane_below(DECAY_RANK)), low.up_pair, NT)
    rate_up = dot(kept(pair_low, ~lane_below(DECAY_RANK)), low.up_pair, NT)
    value_up = dot(value_mid, low.up_value, NT)
    gate_ref[...] = dot(gate_sig.astype(LOW), low.up_gate, NT)
    pair_ref[...] = pair
    vm_ref[...] = value_mid
    gs_ref[...] = gate_sig
    for i, value in enumerate((key_pre, value_pre, decay_up, rate_up, value_up)):
        pre_ref[i] = value
    c8, c9, _, c11, c12 = [own_ref[i : i + 1] for i in range(3, 8)]
    ones = head_ones(recept.shape[1])
    log_decay = -jnp.exp(-jax.nn.softplus(-(c8 + decay_up)) - 0.5)
    rate = jax.nn.sigmoid(c9 + rate_up)
    scaled = key_pre * c11
    key_norm = scaled * lax.rsqrt(head_sum(scaled * scaled, ones) + 1e-06)
    key_main = key_pre * (1.0 + (rate - 1.0) * c12)
    for i, value in enumerate((recept, log_decay, key_main, key_norm, rate)):
        parts_ref[i] = value.astype(LOW)


def block_spec(per, which, rows, width, blocks, back, each, lanes=0):
    def index(i, *tables):
        step = blocks // each - 1 - i if back else i
        stored = tables[0][jnp.maximum(each * step + which, 0)]
        return (stored // per, (stored % per) * (BLOCK // rows) + BLOCK // rows - 1, lanes)

    return pl.BlockSpec((1, rows, width), index)


def whole_spec(array):
    return pl.BlockSpec(array.shape, lambda i, *_: (0,) * array.ndim)


def project(x, cols, own, weights, place, begins, per):
    blocks = place.shape[0]
    total = blocks * BLOCK
    rows = PROJECT_BLOCKS * BLOCK
    width = own.shape[1]
    span = lambda w: pl.BlockSpec((rows, w), lambda i, *_: (i, 0))
    deep = lambda n: pl.BlockSpec((n, rows, width), lambda i, *_: (0, i, 0))
    shape = jax.ShapeDtypeStruct
    return pl.pallas_call(
        project_kernel,
        grid_spec=pltpu.PrefetchScalarGridSpec(
            num_scalar_prefetch=2,
            grid=(blocks // PROJECT_BLOCKS,),
            in_specs=[
                block_spec(per, b, BLOCK, x.shape[2], blocks, False, PROJECT_BLOCKS)
                for b in range(PROJECT_BLOCKS)
            ]
            + [whole_spec(cols), whole_spec(own)]
            + [whole_spec(w) for w in weights],
            out_specs=[
                pl.BlockSpec((PROJECT_BLOCKS, 32, x.shape[2]), lambda i, *_: (i, 0, 0)),
                span(2), deep(5), span(width), deep(5), span(128), span(128), span(128),
            ],
            scratch_shapes=[pltpu.VMEM((8, x.shape[2]), F32)],
        ),
        out_shape=[
            shape((blocks, 32, x.shape[2]), LOW),
            shape((total, 2), F32),
            shape((5, total, width), LOW),
            shape((total, width), F32),
            shape((5, total, width), F32),
            shape((total, 128), F32),
            shape((total, 128), LOW),
            shape((total, 128), F32),
        ],
        compiler_params=pltpu.CompilerParams(vmem_limit_bytes=56 * 1024 * 1024),
        cost_estimate=work(20),
    )(place, begins, *[x] * PROJECT_BLOCKS, cols, own, *weights)


def project_back_kernel(
    part, parts, place_ref, turn_ref, row_ref, begins_ref, head_ref, *refs,
):
    x_refs, refs = refs[:BACK_BLOCKS], refs[BACK_BLOCKS:]
    xp_ref, stats_ref, prior_stats_ref, grads_ref, pair_ref, vm_ref, gs_ref, scan_ref, ffn_ref = refs[:9]
    cols_ref, columns_ref, small_ref, up_ref, *rest = refs[9:]
    sizes_x = len(rest) - 6 - (2 if part == 0 else 1)
    back_refs, rest = rest[:sizes_x], rest[sizes_x:]
    if part == 0:
        low_sum_ref, up_sum_ref, edge, sum_ref, columns_t, small_t, buffer, sems = rest
    else:
        low_sum_ref, edge, sum_ref, columns_t, small_t, buffer, sems = rest
    turn = pl.program_id(0)
    step = pl.num_programs(0) - 1 - turn
    wide = columns_ref.shape[0]

    @pl.when(turn == 0)
    def _():
        for ref in (edge, sum_ref) + ((up_sum_ref,) if part == 0 else ()):
            ref[...] = jnp.zeros_like(ref)
        columns_t[...] = columns_ref[...].T
        small_t[...] = small_ref[:, :384].T

    begins = [begins_ref[i] for i in range(begins_ref.shape[0])]

    x = jnp.concatenate([ref[0] for ref in x_refs], 0).astype(F32)
    unit = (x - stats_ref[:, 0:1]) * stats_ref[:, 1:2]
    rows = unit.shape[0]
    normed = unit * cols_ref[0:1] + cols_ref[1:2]
    last = xp_ref[0].astype(F32)[8:]
    prior = (last - prior_stats_ref[:, 0:1]) * prior_stats_ref[:, 1:2] * cols_ref[0:1] + cols_ref[1:2]
    keep = keep_rows(rows, step * rows, begins)
    diff = rows_down(normed, prior[prior.shape[0] - 1 :]) * keep - normed
    up = up_ref[...]
    up_pair, up_gate = up[:, 384:512], up[:, 512:640]
    up_value = jnp.concatenate([up[:, 320:352], jnp.zeros((up.shape[0], 96), LOW)], 1)
    width = grads_ref.shape[2]
    g_r, g_k, g_v, g_decay, g_rate, g_vup, g_gate = [grads_ref[i] for i in range(7)]
    pair, sig = pair_ref[...], gs_ref[...]
    is_decay = lane_below(DECAY_RANK)
    m_pair = jnp.where(
        is_decay, dot(g_decay, up_pair, NN) * (1.0 - pair * pair), dot(g_rate, up_pair, NN)
    ).astype(LOW)
    m_v = kept(dot(g_vup, up_value, NN), lane_below(DV)).astype(LOW)
    m_g = (dot(g_gate, up_gate, NN) * sig * (1.0 - sig)).astype(LOW)
    near = jnp.zeros_like(unit)
    far = jnp.zeros_like(unit)
    value_weights = jnp.concatenate([columns_t[2 * width :], small_t[256:384]], 0)
    pair_weights = small_t[:128]
    cut = DECAY_RANK + DA + 3 * width
    grads = (
        (2, g_r, columns_t[:width], ((0, g_r),)),
        (3, kept(m_pair, is_decay), pair_weights, ((3 * width, m_pair[:, :DECAY_RANK]),)),
        (4, g_k, columns_t[width : 2 * width], ((width, g_k),)),
        (5, jnp.concatenate([g_v, m_v], 1), value_weights, ((2 * width, g_v), (cut, m_v[:, :DV]))),
        (6, kept(m_pair, ~is_decay), pair_weights, ((3 * width + DECAY_RANK, m_pair[:, DECAY_RANK:]),)),
        (7, m_g, small_t[128:256], ((cut + DV, m_g),)),
    )
    col_sums = []
    for slot, grad, weight, pieces in grads:
        mix = cols_ref[slot : slot + 1]
        mixed = (normed + diff * mix).astype(LOW)
        total = dot(grad, weight, NN)
        for start, piece in pieces:
            sum_ref[start : start + piece.shape[1]] += dot(piece, mixed, TN)
        near = near + total
        far = far + total * mix
        col_sums.append(jnp.sum(total * diff, 0, keepdims=True))
    if part == 0:
        start = 0
        pair_low = pair.astype(LOW)
        for mid, grad in (
            (pair_low[:, :DECAY_RANK], g_decay),
            (pair_low[:, DECAY_RANK:], g_rate),
            (vm_ref[:, :DV], g_vup),
            (sig.astype(LOW), g_gate),
        ):
            up_sum_ref[start : start + mid.shape[1]] += dot(mid, grad, TN)
            start += mid.shape[1]
    moved = far * keep
    back = near - far + rows_up(moved, edge[0:1])
    edge[0:1] = moved[0:1]
    first = [jnp.sum(back * unit, 0, keepdims=True), jnp.sum(back, 0, keepdims=True)]
    sum_ref[sum_ref.shape[0] - 8 :] += jnp.concatenate(first + col_sums, 0)

    slot = turn % 2

    def leave(where):
        for which in range(BACK_BLOCKS):
            pltpu.make_async_copy(
                buffer.at[where, which], back_refs[0].at[0], sems.at[where, which]
            ).wait()

    @pl.when(turn >= 2)
    def _():
        leave(slot)

    buffer[slot] = back.astype(LOW).reshape(BACK_BLOCKS, BLOCK, wide)
    for which in range(BACK_BLOCKS):
        block = BACK_BLOCKS * step + which
        for x, ref in enumerate(back_refs):

            @pl.when(turn_ref[block] == x)
            def _():
                pltpu.make_async_copy(
                    buffer.at[slot, which], ref.at[row_ref[block]], sems.at[slot, which]
                ).start()

    @pl.when(step == 0)
    def _():
        lane = lax.broadcasted_iota(jnp.int32, (1, wide), 1) + part * wide
        spread = jnp.concatenate([scan_ref[...]] * (wide // width), 1)
        spread = jnp.where(lane // width == head_ref[0], spread, 0.0)
        rest_rows = low_sum_ref.shape[0] - sum_ref.shape[0] - 16
        low_sum_ref[...] = jnp.concatenate(
            [sum_ref[...], spread, ffn_ref[...], jnp.zeros((rest_rows, wide), F32)], 0
        ).astype(LOW)
        leave(1 - slot)
        leave(slot)


def project_back(
    part, parts, x, stats, grads, mids, extra_cols, cols, weights, place, turn, row, begins, head, per, sizes
):
    blocks = place.shape[0]
    rows = BACK_BLOCKS * BLOCK
    steps = blocks // BACK_BLOCKS
    wide = x.shape[2] // parts
    width = grads.shape[2]
    size_z, size_x = sizes
    low_rank = DECAY_RANK + DA + DV + 128
    span = lambda w: pl.BlockSpec((rows, w), lambda i, *_: (steps - 1 - i, 0))
    shape = jax.ShapeDtypeStruct
    held = 3 * width + low_rank + 8
    sums = [shape((held + 16 + -(held + 16) % 16, wide), LOW)]
    if part == 0:
        sums.append(shape((low_rank, width), F32))
    columns, small, up = weights
    assert steps > 1
    return pl.pallas_call(
        functools.partial(project_back_kernel, part, parts),
        grid_spec=pltpu.PrefetchScalarGridSpec(
            num_scalar_prefetch=5,
            grid=(steps,),
            in_specs=[
                *[
                    block_spec(per, b, BLOCK, wide, blocks, True, BACK_BLOCKS, part)
                    for b in range(BACK_BLOCKS)
                ],
                block_spec(per, -1, 16, wide, blocks, True, BACK_BLOCKS, part),
                span(2),
                pl.BlockSpec(
                    (8, 2), lambda i, *_: (jnp.maximum((steps - 1 - i) * (rows // 8) - 1, 0), 0)
                ),
                pl.BlockSpec((7, rows, width), lambda i, *_: (0, steps - 1 - i, 0)),
            ]
            + [span(m.shape[1]) for m in mids]
            + [
                whole_spec(extra_cols[0]),
                pl.BlockSpec((8, wide), lambda i, *_: (0, part)),
                pl.BlockSpec((cols.shape[0], wide), lambda i, *_: (0, part)),
                pl.BlockSpec((wide, columns.shape[1]), lambda i, *_: (part, 0)),
                pl.BlockSpec((wide, small.shape[1]), lambda i, *_: (part, 0)),
                whole_spec(up),
            ],
            out_specs=[pl.BlockSpec(memory_space=pl.ANY)] * size_x + [whole_spec(s) for s in sums],
            scratch_shapes=[
                pltpu.VMEM((8, wide), F32),
                pltpu.VMEM((held, wide), F32),
                pltpu.VMEM((columns.shape[1], wide), LOW),
                pltpu.VMEM((384, wide), LOW),
                pltpu.VMEM((2, BACK_BLOCKS, BLOCK, wide), LOW),
                pltpu.SemaphoreType.DMA((2, BACK_BLOCKS)),
            ],
        ),
        out_shape=[shape((size_z * per, BLOCK, wide), LOW)] * size_x + sums,
        compiler_params=pltpu.CompilerParams(vmem_limit_bytes=56 * 1024 * 1024),
        cost_estimate=work(17000),
    )(
        place, turn, row, begins, head, *[x] * (BACK_BLOCKS + 1), stats, stats, grads, *mids, *extra_cols, cols, columns, small, up
    )


TALL = BLOCK + 16


def block_keeps(local_ref, begins_ref, j):
    begins = [begins_ref[i] for i in range(begins_ref.shape[0])]
    first = local_ref[j] * BLOCK
    after = jnp.float32(1.0)
    for b in begins:
        after = jnp.where(first + BLOCK == b, 0.0, after)
    return keep_rows(BLOCK, first, begins), after


def middle_kernel(
    per, local_ref, begins_ref, table_ref, out_ref, tokens_ref, cols_ref, near_ref, far_ref, middle_ref, ffn_ref,
    rows_ref, weight_ref,
):
    count, height, _ = near_ref.shape
    for i in range(2 * count):
        slot = table_ref[i]
        other = lax.rem(slot, count)
        weight_ref[i * height : (i + 1) * height] = jnp.where(slot < count, near_ref[other], far_ref[other])
    heads = out_ref.shape[0]
    rows = [jnp.concatenate([out_ref[h, j] for h in range(heads)], 1) for j in range(per)]
    rows = jnp.concatenate(rows, 0)
    rows_ref[...] = rows
    middle = tokens_ref[...].astype(F32) + dot(rows, weight_ref[...], NN)
    middle_ref[...] = middle
    unit, _ = norm_rows(middle)
    normed = unit * cols_ref[16:17] + cols_ref[17:18]
    c18 = cols_ref[18:19]
    extra_row = lax.broadcasted_iota(jnp.int32, (TALL - BLOCK, 1), 0)
    for j in range(per):
        main = normed[j * TALL : j * TALL + BLOCK]
        extra = normed[j * TALL + BLOCK : (j + 1) * TALL]
        keep, keep_after = block_keeps(local_ref, begins_ref, j)
        moved = rows_down(main, extra[0:1]) * keep
        ffn_ref[j * TALL : j * TALL + BLOCK] = (main + (moved - main) * c18).astype(LOW)
        after = extra + (main[BLOCK - 1 :] * keep_after - extra) * c18
        ffn_ref[j * TALL + BLOCK : (j + 1) * TALL] = jnp.where(extra_row == 1, after, 0.0).astype(LOW)


def middle_rows(out, tokens_ext, near, far, table, cols, local, begins):
    _, per, _, _ = out.shape
    wide = near.shape[2]
    shape = jax.ShapeDtypeStruct
    weight = shape((wide, wide), LOW)
    return pl.pallas_call(
        functools.partial(middle_kernel, per),
        grid_spec=pltpu.PrefetchScalarGridSpec(
            num_scalar_prefetch=3,
            grid=(1,),
            in_specs=[whole_spec(x) for x in (out, tokens_ext, cols, near, far)],
            out_specs=[whole_spec(tokens_ext)] * 3 + [whole_spec(weight)],
        ),
        out_shape=[
            shape((per * TALL, wide), F32),
            shape((per * TALL, wide), LOW),
            shape((per * TALL, wide), LOW),
            weight,
        ],
        compiler_params=pltpu.CompilerParams(vmem_limit_bytes=48 * 1024 * 1024),
        cost_estimate=work(6),
    )(local, begins, table, out, tokens_ext, cols, near, far)


def with_extra(main, extra):
    per = main.shape[0] // BLOCK
    pieces = []
    for j in range(per):
        pieces += [main[j * BLOCK : (j + 1) * BLOCK], extra[j * 16 : (j + 1) * 16]]
    return pieces


def weight_rows_of(ref):
    heads, _, seqs, _, _ = ref.shape
    return jnp.concatenate([ref[h, 0, s] for s in range(seqs) for h in range(heads)], 0)


def channel_kernel(
    xa_ref, xb_ref, ga_ref, gb_ref, ea_ref, eb_ref, key_ref, value_ref, hidden_ref, pre_ref, a_ref, b_ref
):
    rows = xa_ref.shape[0]
    x = jnp.concatenate([xa_ref[...], xb_ref[...]], 0)
    g = jnp.concatenate(with_extra(ga_ref, ea_ref) + with_extra(gb_ref, eb_ref), 0)
    key, value = weight_rows_of(key_ref), weight_rows_of(value_ref)
    active = jnp.maximum(dot(x, key, NN), 0.0)
    hidden_ref[...] = (active * active).astype(LOW)
    grad = (dot(g, value, NN) * 2.0 * active).astype(LOW)
    pre_ref[...] = grad
    back = dot(grad, key, NT)

    @pl.when(pl.program_id(0) == 0)
    def _():
        a_ref[...] = back[:rows]
        b_ref[...] = back[rows:]

    @pl.when(pl.program_id(0) > 0)
    def _():
        a_ref[...] += back[:rows]
        b_ref[...] += back[rows:]


def channel_mix(x, g, extra, weights):
    rows, wide = x[0].shape
    heads, _, seqs, weight_rows, columns = weights.shape
    part = columns // 4

    def weight(which):
        return pl.BlockSpec(
            (heads, 1, seqs, weight_rows, part), lambda i: (0, which, 0, 0, i)
        )

    piece = pl.BlockSpec((2 * rows, part), lambda i: (0, i))
    shape = jax.ShapeDtypeStruct
    return pl.pallas_call(
        channel_kernel,
        grid=(4,),
        in_specs=[whole_spec(a) for a in (*x, *g, *extra)]
        + [weight(0), weight(1)],
        out_specs=[piece, piece, whole_spec(x[0]), whole_spec(x[0])],
        out_shape=[
            shape((2 * rows, columns), LOW),
            shape((2 * rows, columns), LOW),
            shape((rows, wide), F32),
            shape((rows, wide), F32),
        ],
        compiler_params=pltpu.CompilerParams(vmem_limit_bytes=48 * 1024 * 1024),
        cost_estimate=work(8),
    )(*x, *g, *extra, weights, weights)


def main_rows(refs):
    pieces = []
    for ref in refs:
        for start in range(0, ref.shape[0], TALL):
            pieces.append(ref[start : start + BLOCK])
    return jnp.concatenate(pieces, 0)


def channel_grad_kernel(count, *refs):
    og, x = jnp.concatenate([r[...] for r in refs[:count]], 0), main_rows(refs[count : 2 * count])
    hidden, pre = main_rows(refs[2 * count : 2 * count + 2]), main_rows(refs[2 * count + 2 : 2 * count + 4])
    out = refs[2 * count + 4]
    columns = hidden.shape[1]
    out[:, :columns] = dot(og, hidden, TN).astype(LOW)
    out[:, columns : 2 * columns] = dot(x, pre, TN).astype(LOW)


def channel_grads(og, x, hidden, pre, extra):
    wide = og[0].shape[1]
    part = 256
    columns = hidden[0].shape[1]
    return pl.pallas_call(
        functools.partial(channel_grad_kernel, len(og)),
        grid=(wide // part,),
        in_specs=[pl.BlockSpec((a.shape[0], part), lambda i: (0, i)) for a in (*og, *x)]
        + [whole_spec(h) for h in (*hidden, *pre)],
        out_specs=pl.BlockSpec((part, 2 * columns + extra), lambda i: (i, 0)),
        out_shape=jax.ShapeDtypeStruct((wide, 2 * columns + extra), LOW),
        compiler_params=pltpu.CompilerParams(vmem_limit_bytes=48 * 1024 * 1024),
        cost_estimate=work(9),
    )(*og, *x, *hidden, *pre)


def output_grad_kernel(count, *refs):
    rows, grads, out = refs[:count], refs[count : 2 * count], refs[-1]
    left = jnp.concatenate([r[...] for r in rows], 0)
    right = jnp.concatenate([r[...] for r in grads], 0)
    out[...] = dot(left, right, TN).astype(LOW)


def output_grads(rows, grads, room):
    tall, wide = rows[0].shape
    part = grads[0].shape[1]
    last = room.shape[1] // part - 1
    return pl.pallas_call(
        functools.partial(output_grad_kernel, len(rows)),
        grid=(wide // part,),
        in_specs=[pl.BlockSpec((tall, part), lambda i: (0, i))] * len(rows)
        + [whole_spec(g) for g in grads]
        + [pl.BlockSpec(memory_space=pl.ANY)],
        out_specs=pl.BlockSpec((part, part), lambda i: (i, last)),
        out_shape=jax.ShapeDtypeStruct(room.shape, LOW),
        input_output_aliases={2 * len(rows): 0},
        compiler_params=pltpu.CompilerParams(vmem_limit_bytes=48 * 1024 * 1024),
        cost_estimate=work(2),
    )(*rows, *grads, room)


def middle_back_kernel(
    per, local_ref, begins_ref, near_ref, core_ref, far_ref, middle_ref, og_ref, weight_ref, cols_ref,
    grad_ref, low_ref, heads_ref, sums_ref,
):
    c16, c17, c18 = [cols_ref[i : i + 1] for i in (16, 17, 18)]
    grad_in = near_ref[...] + core_ref[...] + far_ref[...].astype(F32)
    sums = [jnp.zeros((1, c16.shape[1]), F32) for _ in range(3)]
    lows = []
    for j in range(per):
        start = j * TALL
        grad, after = grad_in[start : start + BLOCK], grad_in[start + BLOCK + 1 : start + BLOCK + 2]
        keep, keep_after = block_keeps(local_ref, begins_ref, j)
        ahead = rows_up(grad * keep, after * keep_after)
        grad_normed = grad + (ahead - grad) * c18
        unit, scale = norm_rows(middle_ref[start : start + BLOCK])
        prior, _ = norm_rows(middle_ref[start + BLOCK : start + TALL])
        normed = unit * c16 + c17
        diff = rows_down(normed, prior[0:1] * c16 + c17) * keep - normed
        for i, value in enumerate((grad_normed * unit, grad_normed, grad * diff)):
            sums[i] = sums[i] + jnp.sum(value, 0, keepdims=True)
        og = og_ref[j * BLOCK : (j + 1) * BLOCK].astype(F32)
        total = og + norm_back(grad_normed, unit, scale, c16)
        grad_ref[j * BLOCK : (j + 1) * BLOCK] = total
        lows.append(total.astype(LOW))
        quarter = low_ref.shape[2]
        for s in range(low_ref.shape[0]):
            low_ref[s, start : start + BLOCK] = lows[-1][:, s * quarter : (s + 1) * quarter]
            low_ref[s, start + BLOCK : start + TALL] = jnp.zeros((TALL - BLOCK, quarter), LOW)
    sums_ref[...] = jnp.concatenate(sums + [jnp.zeros((5, c16.shape[1]), F32)], 0)
    out = dot(jnp.concatenate(lows, 0), weight_ref[...], NT).astype(LOW)
    width = heads_ref.shape[2]
    for h in range(heads_ref.shape[0]):
        heads_ref[h] = out[:, h * width : (h + 1) * width]


def norm_back(grad, unit, scale, gain):
    grad = grad * gain
    return scale * (
        grad - jnp.mean(grad, -1, keepdims=True) - unit * jnp.mean(grad * unit, -1, keepdims=True)
    )


def middle_back(near, core, far, middle, og, weight, cols, local, begins, heads, seqs):
    tall, wide = near.shape
    per = tall // TALL
    shape = jax.ShapeDtypeStruct
    outs = [
        shape((per * BLOCK, wide), F32),
        shape((seqs, tall, wide // seqs), LOW),
        shape((heads, per * BLOCK, wide // heads), LOW),
        shape((8, wide), F32),
    ]
    operands = (near, core, far, middle, og, weight, cols)
    return pl.pallas_call(
        functools.partial(middle_back_kernel, per),
        grid_spec=pltpu.PrefetchScalarGridSpec(
            num_scalar_prefetch=2,
            grid=(1,),
            in_specs=[whole_spec(x) for x in operands],
            out_specs=[whole_spec(x) for x in outs],
        ),
        out_shape=outs,
        compiler_params=pltpu.CompilerParams(vmem_limit_bytes=48 * 1024 * 1024),
        cost_estimate=work(8),
    )(local, begins, *operands)


HEAD_AXES = ("hz", "hx")


def all_gather(x, axes):
    return lax.all_gather(x, axes, axis=0, tiled=True)


def steps_along(x, axis):
    size = lax.axis_size(axis)
    return [lax.ppermute(x, axis, [(i, i ^ k) for i in range(size)]) for k in range(1, size)]


def grown(x, axis):
    return jnp.concatenate([x] + steps_along(x, axis), 0)


def order_table(axes):
    strides, stride = {}, 1
    for axis in axes:
        strides[axis] = stride
        stride *= lax.axis_size(axis)
    index = jnp.arange(stride, dtype=jnp.int32)
    place, below = jnp.zeros((), jnp.int32), stride
    for axis in ("ys", "core") + HEAD_AXES:
        if axis in axes:
            below //= lax.axis_size(axis)
            there = (index // below) % lax.axis_size(axis)
            place = place + (there ^ lax.axis_index(axis)) * strides[axis]
    return place


def in_order(x, axes):
    x = taken_blocks(x, order_table(axes))
    return x.reshape((x.shape[0] * x.shape[1],) + x.shape[2:])


def swap(x, axis):
    return lax.ppermute(x, axis, [(0, 1), (1, 0)])


def seq_gather(x):
    if lax.axis_size("ys") != 2:
        return list(lax.all_gather(x, ("ys", "core"), axis=0))
    far = swap(x, "ys")
    return [x, swap(x, "core"), far, swap(far, "core")]


def seq_return(near, core, far, diagonal):
    return swap(core, "core"), swap((far + swap(diagonal, "core")).astype(LOW), "ys")


def seq_step(x, axis):
    if lax.axis_size("ys") != 2:
        if axis == "ys":
            return x
        return lax.psum_scatter(x, ("ys", "core"), scatter_dimension=0, tiled=True)[0].astype(F32)
    if axis == "ys":
        x = x.reshape((2, 2) + x.shape[1:])
    index = lax.axis_index(axis)
    sent = swap(lax.dynamic_index_in_dim(x, 1 - index, 0, keepdims=False).astype(LOW), axis)
    return lax.dynamic_index_in_dim(x, index, 0, keepdims=False).astype(F32) + sent.astype(F32)


def taken_blocks(x, table):
    return x.at[table].get(mode="promise_in_bounds")


def start_flags(positions, begins):
    return jnp.any(positions[..., None] == begins, -1).astype(F32)


def body(
    tokens,
    leading_layer_value,
    output_gradient,
    lengths,
    sequence_block_of,
    stored_block_of,
    channel_settings,
    receptance_matrix,
    key_matrix,
    value_matrix,
    output_matrix,
    branch_down_weight,
    branch_up_weight,
    channel_key_weight,
    channel_value_weight,
):
    rows_here, wide = tokens.shape
    per = rows_here // BLOCK
    ys, heads_axis = lax.axis_size("ys"), lax.axis_size("hz") * lax.axis_size("hx")
    seqs = 2 * ys
    head = lax.axis_index(HEAD_AXES)
    core = lax.axis_index("core")
    width = wide // heads_axis
    weight_rows = receptance_matrix.shape[0]
    low_rank = branch_down_weight.shape[1]
    order, home = sequence_block_of[0], stored_block_of[0]
    blocks = order.shape[0]
    begins = (jnp.cumsum(lengths[0]) - lengths[0]).astype(jnp.int32)
    splits = (DECAY_RANK, DECAY_RANK + DA, DECAY_RANK + DA + DV)

    og_first = output_gradient.reshape(per, BLOCK, wide)[:, 0]
    place = home
    out_table = order_table(HEAD_AXES + ("ys", "core"))
    size_z, size_x = lax.axis_size("hz"), lax.axis_size("hx")
    apart = (home // per) ^ head
    turn_x, turn_row = apart % size_x, (apart // size_x) * per + home % per
    local = lax.dynamic_slice_in_dim(order, head * per, per)
    group = all_gather(tokens[None], HEAD_AXES)
    og_rows = in_order(grown(grown(og_first[None], "hz"), "hx"), HEAD_AXES)
    og_parts = seq_gather(output_gradient)

    quarter = channel_key_weight.shape[1] // seqs
    pair = jnp.stack([channel_key_weight, channel_value_weight], 0).reshape(2, weight_rows, seqs, quarter)
    pair = lax.all_to_all(
        pair.transpose(2, 0, 1, 3), ("ys", "core"), split_axis=0, concat_axis=0, tiled=True
    )
    columns = (
        jnp.stack([receptance_matrix, key_matrix, value_matrix], 1)
        .reshape(weight_rows * 3, heads_axis, width)
        .transpose(1, 0, 2)
    )
    columns = lax.all_to_all(columns, HEAD_AXES, split_axis=0, concat_axis=0, tiled=True)
    def rank_columns(weight):
        return jnp.split(weight, (DECAY_RANK + DA, DECAY_RANK + DA + DV), 1)

    (down_pair, down_value, down_gate), (up_pair, up_value, up_gate) = [
        rank_columns(w) for w in (branch_down_weight, branch_up_weight)
    ]
    count = channel_settings.shape[1]
    blank = [jnp.zeros((weight_rows, n), LOW) for n in (32 - count, 32)]
    small = jnp.concatenate(
        [
            down_pair, down_gate, down_value, channel_settings, blank[0], up_value, blank[1],
            up_pair, up_gate,
        ],
        1,
    )[None]
    for axis in HEAD_AXES + ("ys", "core"):
        small = grown(small, axis)
    small = in_order(small, HEAD_AXES + ("ys", "core"))
    columns = columns.reshape(1, heads_axis * weight_rows, 3 * width)
    columns = in_order(grown(grown(columns, "ys"), "core"), ("ys", "core"))
    settings = small[:, 256 + DV : 256 + DV + count].astype(F32).T
    up = lax.dynamic_slice_in_dim(small, head * width, width, 0)
    own = lax.dynamic_slice_in_dim(settings, head * width, width, 1)
    own = jnp.concatenate([own[13:16], own[8:13]], 0)
    out_shards = grown(grown(output_matrix[None], "hz"), "hx")
    columns, small, settings, up, own, og_parts, pair, first_sent, out_shards = (
        lax.optimization_barrier(
            (
                columns, small, settings, up, own, og_parts, pair, leading_layer_value, out_shards,
            )
        )
    )
    first_group = lax.all_to_all(
        first_sent.reshape(rows_here, heads_axis, width).transpose(1, 0, 2),
        HEAD_AXES, split_axis=0, concat_axis=0, tiled=True,
    ).reshape(blocks, BLOCK, width)
    weights = [columns, small, up]

    out_shards = grown(out_shards, "ys")

    def gathered(half):
        return all_gather(half[None], HEAD_AXES).transpose(1, 0, 2, 3)

    whole_quarter = quarter == wide
    if whole_quarter:
        every = all_gather(pair.transpose(1, 0, 2, 3).reshape(1, -1, weight_rows, wide), HEAD_AXES)
    else:
        every = (gathered(pair[:, 0]), gathered(pair[:, 1]))

    ends, stats, parts, gate, pre, *mids = project(group, settings, own, weights, place, begins, per)
    parts, out_shards = lax.optimization_barrier((parts, out_shards))
    far_shards = swap(out_shards, "core")
    values, out_in, joined, scanned, states, mats = scan_forward(
        parts, pre, first_group, gate, own, home, begins, PASSES
    )

    before, follow = jnp.maximum(order - 1, 0), jnp.minimum(order + 1, blocks - 1)
    in_blocks = out_in.reshape(blocks, BLOCK, width)
    extended = jnp.concatenate(
        [
            taken_blocks(in_blocks, order),
            taken_blocks(in_blocks[:, BLOCK - 1], before)[:, None],
            taken_blocks(in_blocks[:, 0], follow)[:, None],
            jnp.zeros((blocks, 14, width), LOW),
        ],
        1,
    )
    extended, far_shards, ends, og_rows = lax.optimization_barrier((extended, far_shards, ends, og_rows))
    out_ext = lax.all_to_all(
        extended.reshape(heads_axis, per, TALL, width), HEAD_AXES, split_axis=0, concat_axis=0, tiled=True
    )
    local = lax.dynamic_slice_in_dim(order, head * per, per)
    after_seq = local + 1
    after_live = (after_seq < blocks).astype(LOW)[:, None]
    after = jnp.minimum(after_seq, blocks - 1)
    row_before = taken_blocks(ends, jnp.maximum(local - 1, 0))[:, 31]
    row_after = taken_blocks(ends, after)[:, 0]
    og_after = taken_blocks(og_rows, taken_blocks(home, after)) * after_live
    none = jnp.zeros((per, 14, wide), LOW)
    extra_parts = seq_gather(jnp.concatenate([none[:, :1], og_after[:, None], none], 1).reshape(-1, wide))
    tokens_b = tokens.reshape(per, BLOCK, wide)
    tokens_ext = jnp.concatenate([tokens_b, row_before[:, None], row_after[:, None], none], 1)
    if weight_rows % 16:
        ordered = in_order(jnp.concatenate([out_shards, far_shards], 0), HEAD_AXES + ("ys", "core"))
        out_shards, far_shards = ordered.reshape(2, -1, 32, wide)
        out_table = jnp.arange(2 * out_shards.shape[0], dtype=jnp.int32)
    middle, ffn_in, out_rows, out_weight = middle_rows(
        out_ext, tokens_ext.reshape(-1, wide), out_shards, far_shards, out_table, settings, local, begins
    )
    ffn_in, every = lax.optimization_barrier((ffn_in, every))
    if whole_quarter:
        every = every.reshape(heads_axis, 2, seqs, weight_rows, wide)
        value_part = every[:, 1].transpose(1, 0, 2, 3).reshape(wide, wide)
        ffn_parts = [ffn_in, swap(ffn_in, "core"), swap(ffn_in, "ys")]
        *near, own_part, core_part = channel_mix(ffn_parts[:2], og_parts[:2], extra_parts[:2], every)
        ffn_parts[2], near, own_part, core_part, out_rows = lax.optimization_barrier(
            (ffn_parts[2], near, own_part, core_part, out_rows)
        )
        ffn_parts.append(swap(ffn_parts[2], "core"))
        *far, far_part, diagonal = channel_mix(ffn_parts[2:], og_parts[2:], extra_parts[2:], every)
        came_core, came_far = seq_return(own_part, core_part, far_part, diagonal)
        grads_here = channel_grads(
            og_parts, ffn_parts, (near[0], far[0]), (near[1], far[1]), wide // seqs
        )
        came_far, grads_here = lax.optimization_barrier((came_far, grads_here))
        hidden = [near[0], far[0]]
    else:
        key_part, value_part = [x.reshape(wide, quarter) for x in every]
        ffn_parts = seq_gather(ffn_in)
        rows = jnp.concatenate(ffn_parts, 0)
        og_rows = jnp.concatenate(
            [
                jnp.concatenate([g.reshape(per, BLOCK, wide), x.reshape(per, 16, wide)], 1).reshape(-1, wide)
                for g, x in zip(og_parts, extra_parts)
            ],
            0,
        )
        active = jax.nn.relu(dot(rows, key_part, NN))
        hidden = [(active * active).astype(LOW)]
        grad_pre = (dot(og_rows, value_part, NN) * 2.0 * active).astype(LOW)
        own_part = dot(grad_pre, key_part, NT).reshape(seqs, per * TALL, wide)
        own_part = lax.psum_scatter(own_part, ("ys", "core"), scatter_dimension=0, tiled=True)[0]
        came_core, came_far = jnp.zeros_like(own_part), jnp.zeros_like(ffn_in)
        is_main = (jnp.arange(rows.shape[0]) % TALL < BLOCK).astype(LOW)[:, None]
        grads_here = [dot(og_rows * is_main, hidden[0], TN), dot(rows * is_main, grad_pre, TN)]
    grad_middle, middle_low, grad_out, cols_ffn = middle_back(
        own_part, came_core, came_far, middle, output_gradient, out_weight, settings, local, begins, heads_axis,
        seqs,
    )
    grad_heads = lax.all_to_all(grad_out, HEAD_AXES, split_axis=0, concat_axis=0, tiled=True)
    out_parts = seq_gather(out_rows)
    which = lax.axis_index(("ys", "core"))
    if whole_quarter:

        def quarter_from(k):
            sent = lax.dynamic_index_in_dim(middle_low, which ^ k, 0, keepdims=False)
            return lax.ppermute(sent, ("ys", "core"), [(i, i ^ k) for i in range(seqs)])

        low_parts = [lax.dynamic_index_in_dim(middle_low, which, 0, keepdims=False)]
        low_parts += [quarter_from(k) for k in (1, 2, 3)]
        grads_here = output_grads(out_parts, low_parts, grads_here)
    else:
        right = lax.all_to_all(middle_low, ("ys", "core"), split_axis=0, concat_axis=0, tiled=True)
        grads_here.append(dot(jnp.concatenate(out_parts, 0), right.reshape(-1, right.shape[2]), TN))
        grads_here = jnp.concatenate(grads_here, 1).astype(LOW)
    grad_heads, grads_here = lax.optimization_barrier((grad_heads, grads_here))
    grads_here = lax.psum_scatter(grads_here, HEAD_AXES, scatter_dimension=0, tiled=True)

    scan_grads, first_grad, cols_scan = scan_backward(
        parts, values, joined, scanned, gate, grad_heads.reshape(blocks, BLOCK, width), pre, first_group,
        own, states, mats, home, begins, PASSES,
    )
    first_grad = taken_blocks(first_grad.reshape(blocks, BLOCK, width), order)
    first_came = lax.all_to_all(
        first_grad.reshape(heads_axis, rows_here, width), HEAD_AXES, split_axis=0, concat_axis=0, tiled=True
    )

    share = wide // seqs
    thin = low_rank // seqs
    fold = heads_axis // seqs

    cut = 3 * width
    end = cut + low_rank

    def over_ys(left, right, up_sums):
        up_sums = up_sums.astype(LOW).reshape(seqs, thin, width)
        if ys != 2:
            rows_out = jnp.concatenate([left, right], 1)
            by_feature = jnp.concatenate([rows_out[:cut], rows_out[end:]], 0)
            by_feature = by_feature.reshape(-1, seqs, share).transpose(1, 0, 2)
            return by_feature, rows_out[cut:end].reshape(seqs, thin, wide), up_sums
        index = lax.axis_index("ys")

        def part_of(which):
            half = jnp.where(which == 0, left, right)
            rank = [lax.dynamic_slice_in_dim(x, cut + which * 2 * thin, 2 * thin, 0) for x in (left, right)]
            return jnp.concatenate([half[:cut], half[end:]] + rank, 0)

        total = part_of(index).astype(F32) + swap(part_of(1 - index), "ys").astype(F32)
        features = total.shape[0] - 4 * thin
        by_rank = total[features:].reshape(2, 2, thin, -1).transpose(1, 2, 0, 3)
        return total[:features].reshape(-1, 2, share), by_rank, seq_step(up_sums, "ys")

    def over_core(by_feature, by_rank, up_sums):
        if ys != 2:
            return [
                lax.psum_scatter(x, ("ys", "core"), scatter_dimension=0, tiled=True)[0].astype(F32)
                for x in (by_feature, by_rank, up_sums)
            ]

        def step(x, dim):
            sent = lax.dynamic_index_in_dim(x, 1 - core, dim, keepdims=False).astype(LOW)
            return lax.dynamic_index_in_dim(x, core, dim, keepdims=False) + swap(sent, "core").astype(F32)

        return step(by_feature, 1), step(by_rank, 0).reshape(thin, wide), step(up_sums, 0)

    def to_owners(by_feature, by_rank):
        rows_low = by_feature.astype(LOW)
        squares = rows_low[:cut].reshape(cut, fold, width)
        mixed = by_rank.astype(LOW).reshape(thin, heads_axis, width).transpose(1, 0, 2)
        cols_part = rows_low[cut:][:count].reshape(count, heads_axis, -1)
        cols_part = jnp.pad(
            cols_part.transpose(1, 0, 2), ((0, 0), (0, -count % 8), (0, width - cols_part.shape[2]))
        )
        mixed = lax.all_to_all(
            jnp.concatenate([mixed, cols_part], 1), HEAD_AXES, split_axis=0, concat_axis=0, tiled=True
        )
        came = []
        for k in range(fold):
            sent = lax.dynamic_index_in_dim(squares, (head + k) % fold, 1, keepdims=False)
            came.append(
                lax.ppermute(
                    sent, every_axis, [(q * heads_axis + h, owner(q, h, (h + k) % fold)) for q, h in pairs]
                )
            )
        return mixed, came

    every_axis = ("ys", "core") + HEAD_AXES
    pairs = [(q, h) for q in range(seqs) for h in range(heads_axis)]

    def owner(q, h, j):
        return (h // fold) * heads_axis + q * fold + j

    sizes = (size_z, size_x)

    def others_x(blocks_back):
        return [
            lax.ppermute(blocks_back[k], "hx", [(i, i ^ k) for i in range(size_x)])
            for k in range(1, size_x)
        ]

    def after_x(kept_blocks, came):
        total = kept_blocks.astype(F32)
        for x in came:
            total = total + x.astype(F32)
        total = total.reshape(size_z, rows_here, -1)
        return total[0], [total[k].astype(LOW) for k in range(1, size_z)]

    def others_z(sent):
        return [
            lax.ppermute(x, "hz", [(i, i ^ k) for i in range(size_z)]) for k, x in enumerate(sent, 1)
        ]

    def half_back(part, grads):
        outs = project_back(
            part, 2, group, stats, grads, mids, (cols_scan, cols_ffn), settings, weights, place, turn_x, turn_row,
            begins, head[None], per, sizes,
        )
        return outs[:size_x], outs[size_x:]

    left_blocks, (left_sum, up_sums) = half_back(0, scan_grads)
    left_came = others_x(left_blocks)
    scan_grads, left_sum, first_came = lax.optimization_barrier((scan_grads, left_sum, first_came))
    right_blocks, (right_sum,) = half_back(1, scan_grads)
    right_blocks, left_came = lax.optimization_barrier((right_blocks, left_came))
    right_came = others_x(right_blocks)
    left_own, left_sent = after_x(left_blocks[0], left_came)
    left_sent, right_sum, hidden = lax.optimization_barrier((left_sent, right_sum, hidden))
    left_z = others_z(left_sent)
    sums = over_ys(left_sum, right_sum, up_sums)
    outs = [dot(h, value_part, NT) for h in hidden]
    right_came, outs, grads_here = lax.optimization_barrier((right_came, outs, grads_here))
    right_own, right_sent = after_x(right_blocks[0], right_came)
    right_sent, left_z, sums, outs = lax.optimization_barrier((right_sent, left_z, sums, outs))
    right_z = others_z(right_sent)
    by_feature, by_rank, up_sums = over_core(*sums)
    right_z[0], by_feature, by_rank = lax.optimization_barrier((right_z[0], by_feature, by_rank))
    mixed, came = to_owners(by_feature, by_rank)
    if whole_quarter:
        came_core, came_far = seq_return(*[x for out in outs for x in jnp.split(out, 2, 0)])
        right_z, came_core, came_far = lax.optimization_barrier((right_z, came_core, came_far))
    right_z[0], first_came = lax.optimization_barrier((right_z[0], first_came))
    first_value_grad = first_came.transpose(1, 0, 2).reshape(rows_here, wide).astype(F32)
    right_z, up_sums, mixed, came = lax.optimization_barrier((right_z, up_sums, mixed, came))
    back = jnp.concatenate(
        [own + sum(x.astype(F32) for x in z) for own, z in ((left_own, left_z), (right_own, right_z))], 1
    )
    value_sum, key_sum, out_sum = jnp.split(grads_here.astype(F32), (quarter, 2 * quarter), 1)

    unit, scale = norm_rows(tokens.astype(F32))
    tokens_grad = grad_middle + norm_back(back, unit, scale, settings[0])
    mixed = jnp.sum(mixed.astype(F32), 0)
    channel_grad = mixed[thin : thin + count, :weight_rows].T
    down_grad = mixed[:thin].T

    def main_of(x):
        return x.reshape(-1, per, TALL, wide)[:, :, :BLOCK].reshape(-1, rows_here, wide)

    layer_out = main_of(middle)[0]
    if whole_quarter:
        own_out = jnp.split(outs[0], 2, 0)[0]
        layer_out = layer_out + main_of(own_out)[0] + main_of(came_core)[0] + main_of(came_far)[0].astype(F32)
    else:
        layer_out = layer_out + lax.psum_scatter(
            main_of(outs[0]), ("ys", "core"), scatter_dimension=0, tiled=True
        )[0]
    came = jnp.stack(came, 0)
    came = taken_blocks(came, (head - jnp.arange(fold, dtype=jnp.int32)) % fold)
    came = came.reshape(fold, 3, width, width).transpose(1, 3, 0, 2).reshape(3, width, share)
    recept_grad, key_grad, value_grad = [came[i].astype(F32) for i in range(3)]
    up_grad = up_sums.T
    return (
        layer_out.astype(LOW),
        tokens_grad,
        first_value_grad,
        channel_grad,
        recept_grad,
        key_grad,
        value_grad,
        out_sum,
        down_grad,
        up_grad,
        key_sum,
        value_sum,
    )


def solution(mesh):
    seqs, heads = mesh.devices.shape
    split = Mesh(mesh.devices.reshape(seqs // 2, 2, 4, heads // 4), ("ys", "core") + HEAD_AXES)
    rows = P(("ys", "core") + HEAD_AXES, None)
    table = P(("ys", "core"), None)
    square = P(HEAD_AXES, ("ys", "core"))
    return jax.shard_map(
        body,
        mesh=split,
        in_specs=(rows,) * 3 + (table,) * 3 + (rows,) * 9,
        out_specs=(rows,) * 4 + (square,) * 8,
        check_vma=False,
    )
```

```python
import functools
import jax
import jax.numpy as jnp
from jax import lax
from jax.experimental import pallas as pl
from jax.experimental.pallas import tpu as pltpu
from jax.sharding import Mesh
from jax.sharding import PartitionSpec as P

DECAY_RANK = 64
DA = 64
DV = 32
BLOCK = 128
SPAN = 64
HEAD = 64
FORWARD_CHUNKS = 8
BACKWARD_CHUNKS = 4
LOW = jnp.bfloat16
F32 = jnp.float32
NN = (((1,), (0,)), ((), ()))
NT = (((1,), (1,)), ((), ()))
TN = (((0,), (0,)), ((), ()))
PASSES = {"pair": 3, "inv": 3, "val": 3, "chain": 3, "bpair": 3}


def work(micros):
    return pl.CostEstimate(flops=0, bytes_accessed=int(micros * 3_000), transcendentals=0)


def dot(a, b, dims):
    return lax.dot_general(a, b, dims, preferred_element_type=F32)


def halves(x):
    high = x.astype(LOW)
    return high, (x - high.astype(F32)).astype(LOW)


def product(a, b, dims, passes):
    if passes == 1:
        return dot(a.astype(LOW), b.astype(LOW), dims)
    la, lb = dims[0][0][0], dims[0][1][0]
    a_high, a_low = halves(a)
    if passes == 2:
        b = b.astype(LOW)
        return dot(jnp.concatenate([a_high, a_low], la), jnp.concatenate([b, b], lb), dims)
    b_high, b_low = halves(b)
    first = dot(jnp.concatenate([a_high, a_low], la), jnp.concatenate([b_high, b_high], lb), dims)
    return first + dot(a_high, b_low, dims)


def head_masks(heads):
    lane = lax.broadcasted_iota(jnp.int32, (1, heads * HEAD), 1) // HEAD
    return [(lane == h).astype(F32) for h in range(heads)]


def stacked(x, masks):
    if len(masks) == 1:
        return x
    return jnp.concatenate([x * m for m in masks], 0)


def unstacked(x, heads):
    rows = x.shape[0] // heads
    out = x[:rows]
    for h in range(1, heads):
        out = out + x[h * rows : (h + 1) * rows]
    return out


def head_ones(width):
    row = lax.broadcasted_iota(jnp.int32, (width, width), 0) // HEAD
    col = lax.broadcasted_iota(jnp.int32, (width, width), 1) // HEAD
    return (row == col).astype(LOW)


def head_sum(x, ones):
    high, low = halves(x)
    return dot(jnp.concatenate([high, low], 1), jnp.concatenate([ones, ones], 0), NN)


class Chunk:
    def __init__(self, r, lw, k, kn, a, begins, start, heads):
        self.heads = heads
        masks = head_masks(heads)
        rows = heads * SPAN
        local = [jnp.where(b >= start, b - start, SPAN) for b in begins]
        row_t = lax.broadcasted_iota(jnp.int32, (rows, 1), 0) % SPAN
        col_t = lax.broadcasted_iota(jnp.int32, (1, rows), 1) % SPAN
        row_seg = sum((row_t >= b).astype(jnp.int32) for b in local)
        col_seg = sum((col_t >= b).astype(jnp.int32) for b in local)
        last = sum((b < SPAN).astype(jnp.int32) for b in local)
        same = row_seg == col_seg
        self.strict = same & (row_t > col_t)
        self.upto = same & (row_t >= col_t)
        self.carried = (row_seg == 0).astype(F32)
        self.final = (row_seg == last).astype(F32)
        self.whole = (last == 0).astype(F32)
        tri_r = lax.broadcasted_iota(jnp.int32, (SPAN, SPAN), 0)
        tri_c = lax.broadcasted_iota(jnp.int32, (SPAN, SPAN), 1)
        running = dot((tri_r >= tri_c).astype(LOW), lw, NN)
        lw = lw.astype(F32)
        decay = jnp.exp(running)
        before = jnp.exp(running - lw)
        inverse = jnp.exp(-running)
        end = running[SPAN - 1 : SPAN]
        to_end = jnp.exp(end - running)
        self.end = jnp.exp(end)
        kn = kn.astype(F32)
        beta = kn * a.astype(F32)
        k = k.astype(F32)
        self.decay, self.before, self.inverse, self.to_end = decay, before, inverse, to_end
        self.a_hat = stacked(-kn * before, masks)
        self.r_hat = stacked(r.astype(F32) * decay, masks)
        self.b_hat = stacked(beta * inverse, masks)
        self.k_hat = stacked(k * inverse, masks)
        self.b_end = stacked(beta * to_end, masks) * self.final
        self.k_end = stacked(k * to_end, masks) * self.final


def block_inverses(all_pairs, passes):
    rows = all_pairs[0].shape[0]
    row = lax.broadcasted_iota(jnp.int32, (rows, rows), 0)
    col = lax.broadcasted_iota(jnp.int32, (rows, rows), 1)
    eye = (row == col).astype(F32)

    def products(left, right):
        return [product(a, b, NN, passes) for a, b in zip(left, right)]

    within = row // 8 == col // 8
    small = [jnp.where(within, pairs, 0.0) for pairs in all_pairs]
    square = products(small, small)
    fourth = products(square, square)
    first = [eye + x for x in small]
    inverse = [a + b for a, b in zip(first, products(first, square))]
    inverse = [a + b for a, b in zip(inverse, products(inverse, fourth))]
    size = 8
    while size < SPAN:
        within = (row // (2 * size) == col // (2 * size)) & (row // size != col // size)
        cross = [jnp.where(within, pairs, 0.0) for pairs in all_pairs]
        step = products(products(inverse, cross), inverse)
        inverse = [a + b for a, b in zip(inverse, step)]
        size *= 2
    return inverse


def group_norm_parts(scanned, ones):
    center = scanned - head_sum(scanned, ones) * (1.0 / HEAD)
    spread = head_sum(center * center, ones) * (1.0 / HEAD)
    scale = lax.rsqrt(spread + 0.00064)
    return center * scale, scale


def scan_forward_kernel(
    heads, p, home_ref, begins_ref, parts_ref, pre_ref, gate_ref, cols_ref, *rest,
):
    first_refs, rest = rest[: FORWARD_CHUNKS * SPAN // BLOCK], rest[FORWARD_CHUNKS * SPAN // BLOCK :]
    values_ref, out_ref, joined_ref, scanned_ref, state_ref, mats_ref, state = rest
    step = pl.program_id(0)
    width = heads * HEAD

    @pl.when(step == 0)
    def _():
        state[...] = jnp.zeros_like(state)

    begins = [begins_ref[i] for i in range(begins_ref.shape[0])]
    masks = head_masks(heads)
    n = heads * SPAN
    eye = (
        lax.broadcasted_iota(jnp.int32, (width, width), 0)
        == lax.broadcasted_iota(jnp.int32, (width, width), 1)
    ).astype(F32)
    first = jnp.concatenate([ref[0] for ref in first_refs], 0).astype(F32)
    mix = jax.nn.sigmoid(cols_ref[5:6] + pre_ref[4])
    values = (pre_ref[1] + (first - pre_ref[1]) * mix).astype(LOW)
    values_ref[...] = values
    held = []
    for c in range(FORWARD_CHUNKS):
        rows = pl.ds(c * SPAN, SPAN)
        r, lw, k, kn, a = [parts_ref[i, rows] for i in range(5)]
        v = values[c * SPAN : (c + 1) * SPAN]
        q = Chunk(r, lw, k, kn, a, begins, (step * FORWARD_CHUNKS + c) * SPAN, heads)
        v_st = stacked(v.astype(F32), masks).astype(LOW)
        held.append((q, r, k, v, v_st))
    all_pairs = [
        product(
            jnp.concatenate([q.a_hat, q.r_hat], 0), jnp.concatenate([q.b_hat, q.k_hat], 0), NT, p["pair"]
        )
        for q, *_ in held
    ]
    l_ab = [jnp.where(h[0].strict, x[:n, :n], 0.0) for h, x in zip(held, all_pairs)]
    l_ak = [jnp.where(h[0].strict, x[:n, n:], 0.0) for h, x in zip(held, all_pairs)]
    l_rb = [jnp.where(h[0].upto, x[n:, :n], 0.0) for h, x in zip(held, all_pairs)]
    l_rk = [jnp.where(h[0].upto, x[n:, n:], 0.0) for h, x in zip(held, all_pairs)]
    both_v = [
        product(jnp.concatenate([ak, rk], 0), h[4], NN, 2 if p["val"] == 3 else 1)
        for ak, rk, h in zip(l_ak, l_rk, held)
    ]
    inverses = block_inverses(l_ab, p["inv"])
    solved = [
        product(t, jnp.concatenate([h[0].a_hat * h[0].carried, b[:n]], 1), NN, p["val"])
        for t, h, b in zip(inverses, held, both_v)
    ]
    ends = [product(x, h[0].b_end, TN, p["val"]) for x, h in zip(solved, held)]
    grown = []
    for q, _, _, _, v_st in held:
        if p["val"] == 3:
            k_high, k_low = halves(q.k_end)
            grown.append(dot(jnp.concatenate([v_st, v_st], 0), jnp.concatenate([k_high, k_low], 0), TN))
        else:
            grown.append(dot(v_st, q.k_end.astype(LOW), TN))
    ready = []
    for c in range(FORWARD_CHUNKS):
        q, r, k, v, _ = held[c]
        through = product(l_rb[c], solved[c], NN, p["val"])
        r_thru = q.r_hat * q.carried + through[:, :width]
        o_val = both_v[c][n:] + through[:, width:]
        move = eye * (q.end * q.whole) + ends[c][:width]
        gain = ends[c][width:] + grown[c]
        mats = [
            inverses[c], l_ak[c], l_rb[c], l_rk[c], solved[c][:, :width], solved[c][:, width:], move, r_thru,
        ]
        for i, m in enumerate(mats):
            mats_ref[c, i] = m
        ready.append((move, gain, r_thru, o_val, r, k, v))
    ones = head_ones(width)
    now = state[...]
    begun = []
    for c in range(FORWARD_CHUNKS):
        begun.append(now)
        state_ref[c] = now
        now = product(now, ready[c][0], NN, p["chain"]) + ready[c][1]
    state[...] = now
    for c in range(FORWARD_CHUNKS):
        rows = pl.ds(c * SPAN, SPAN)
        _, _, r_thru, o_val, r, k, v = ready[c]
        scanned = unstacked(o_val + product(r_thru, begun[c], NT, p["val"]), heads)
        scanned_ref[rows] = scanned
        unit, _ = group_norm_parts(scanned, ones)
        bonus = head_sum(r.astype(F32) * k.astype(F32) * cols_ref[0:1], ones)
        joined = unit * cols_ref[1:2] + cols_ref[2:3] + bonus * v.astype(F32)
        joined = joined.astype(LOW)
        joined_ref[rows] = joined
        out_ref[rows] = (joined.astype(F32) * gate_ref[rows]).astype(LOW)


def scan_forward(parts, pre, first, gate, cols, home, begins, p):
    _, total, width = parts.shape
    heads = width // HEAD
    rows = FORWARD_CHUNKS * SPAN
    n = heads * SPAN
    spans = total // SPAN
    assert n == width
    row_spec = pl.BlockSpec((rows, width), lambda i, *_: (i, 0))
    per_step = rows // BLOCK

    def stored(which):
        return pl.BlockSpec((1, BLOCK, width), lambda i, home, b: (home[per_step * i + which], 0, 0))

    return pl.pallas_call(
        functools.partial(scan_forward_kernel, heads, p),
        grid_spec=pltpu.PrefetchScalarGridSpec(
            num_scalar_prefetch=2,
            grid=(total // rows,),
            in_specs=[
                pl.BlockSpec((5, rows, width), lambda i, *_: (0, i, 0)),
                pl.BlockSpec((5, rows, width), lambda i, *_: (0, i, 0)),
                row_spec,
                pl.BlockSpec(cols.shape, lambda i, *_: (0, 0)),
            ]
            + [stored(w) for w in range(per_step)],
            out_specs=[
                row_spec,
                row_spec,
                row_spec,
                row_spec,
                pl.BlockSpec((FORWARD_CHUNKS, width, width), lambda i, *_: (i, 0, 0)),
                pl.BlockSpec((FORWARD_CHUNKS, 8, n, width), lambda i, *_: (i, 0, 0, 0)),
            ],
            scratch_shapes=[pltpu.VMEM((width, width), F32)],
        ),
        out_shape=[
            jax.ShapeDtypeStruct((total, width), LOW),
            jax.ShapeDtypeStruct((total, width), LOW),
            jax.ShapeDtypeStruct((total, width), LOW),
            jax.ShapeDtypeStruct((total, width), F32),
            jax.ShapeDtypeStruct((spans, width, width), F32),
            jax.ShapeDtypeStruct((spans, 8, n, width), F32),
        ],
        compiler_params=pltpu.CompilerParams(vmem_limit_bytes=60 * 1024 * 1024),
        cost_estimate=work(80),
    )(home, begins, parts, pre, gate, cols, *[first] * per_step)


def scan_backward_kernel(
    heads, p, home_ref, begins_ref, parts_ref, values_ref, joined_ref, scanned_ref, gate_ref, grad_a_ref,
    grad_b_ref, pre_ref, first_a_ref, first_b_ref, cols_ref, state_ref, mats_ref, *rest,
):
    steps = pl.num_programs(0)
    step = steps - 1 - pl.program_id(0)
    grads_ref, first_grad_ref, col_grad_ref, state, buffer, sems = rest
    turn = pl.program_id(0)
    slot = turn % 2
    width = heads * HEAD
    n = heads * SPAN

    def first_copy(where, b, stored):
        return pltpu.make_async_copy(buffer.at[where, b], first_grad_ref.at[stored], sems.at[where, b])

    def first_done(where):
        for b in range(2):
            first_copy(where, b, 0).wait()

    @pl.when(turn >= 2)
    def _():
        first_done(slot)

    @pl.when(pl.program_id(0) == 0)
    def _():
        state[...] = jnp.zeros_like(state)
        col_grad_ref[...] = jnp.zeros_like(col_grad_ref)

    begins = [begins_ref[i] for i in range(begins_ref.shape[0])]
    masks = head_masks(heads)
    ones = head_ones(width)
    tri_r = lax.broadcasted_iota(jnp.int32, (SPAN, SPAN), 0)
    tri_c = lax.broadcasted_iota(jnp.int32, (SPAN, SPAN), 1)
    later = (tri_c >= tri_r).astype(LOW)
    after = (tri_c > tri_r).astype(LOW)
    sums = [jnp.zeros((1, width), F32) for _ in range(8)]

    def add(slot, value):
        sums[slot] = sums[slot] + jnp.sum(value, 0, keepdims=True)

    c13, c14 = cols_ref[0:1], cols_ref[1:2]
    grads = jnp.concatenate([grad_a_ref[0], grad_b_ref[0]], 0).astype(F32)
    firsts = jnp.concatenate([first_a_ref[0], first_b_ref[0]], 0).astype(F32)
    ready = []
    for c in range(BACKWARD_CHUNKS):
        rows = pl.ds(c * SPAN, SPAN)
        r, lw, k, kn, a = [parts_ref[i, rows] for i in range(5)]
        v = values_ref[rows]
        q = Chunk(r, lw, k, kn, a, begins, (step * BACKWARD_CHUNKS + c) * SPAN, heads)
        r, k, v = r.astype(F32), k.astype(F32), v.astype(F32)
        unit, scale = group_norm_parts(scanned_ref[rows], ones)
        grad_out = grads[c * SPAN : (c + 1) * SPAN]
        grad_joined = (grad_out * gate_ref[rows]).astype(LOW).astype(F32)
        grad_gate = (grad_out * joined_ref[rows].astype(F32)).astype(LOW)
        add(6, grad_joined * unit)
        add(7, grad_joined)
        grad_unit = grad_joined * c14
        grad_scan = scale * (
            grad_unit
            - head_sum(grad_unit, ones) * (1.0 / HEAD)
            - unit * (head_sum(grad_unit * unit, ones) * (1.0 / HEAD))
        )
        bonus = head_sum(r * k * c13, ones)
        grad_bonus = head_sum(grad_joined * v, ones)
        add(5, grad_bonus * r * k)
        own_r = grad_bonus * k * c13
        own_k = grad_bonus * r * c13
        own_v = grad_joined * bonus
        d_out = stacked(grad_scan, masks)
        flow = product(d_out, mats_ref[c, 7], TN, p["val"])
        ready.append((q, d_out, flow, own_r, own_k, own_v, grad_gate))
    now = state[...]
    ended = [None] * BACKWARD_CHUNKS
    for c in reversed(range(BACKWARD_CHUNKS)):
        ended[c] = now
        now = product(now, mats_ref[c, 6], NT, p["chain"]) + ready[c][2]
    state[...] = now
    span = range(BACKWARD_CHUNKS)
    mats = [[mats_ref[c, i] for i in range(6)] for c in span]
    begin = [state_ref[c] for c in span]
    chunks = [ready[c][0] for c in span]
    d_outs = [ready[c][1] for c in span]
    v_st = [stacked(values_ref[pl.ds(c * SPAN, SPAN)].astype(F32), masks) for c in span]
    update = [mats[c][5] + product(mats[c][4], begin[c], NT, p["val"]) for c in span]
    through = [product(mats[c][2], d_outs[c], TN, p["val"]) for c in span]
    through = [
        through[c] + product(chunks[c].b_end, ended[c], NT, p["val"]) for c in span
    ]
    back = [product(mats[c][0], through[c], TN, p["val"]) for c in span]
    left = [jnp.concatenate([back[c], d_outs[c]], 0) for c in span]
    right = [jnp.concatenate([update[c], v_st[c]], 0) for c in span]
    d_hats = [product(left[c], begin[c], NN, p["val"]) for c in span]
    pair_grads = [product(left[c], right[c], NT, p["bpair"]) for c in span]
    for c in span:
        strict, upto = chunks[c].strict.astype(F32), chunks[c].upto.astype(F32)
        mask = jnp.concatenate(
            [jnp.concatenate([strict, strict], 1), jnp.concatenate([upto, upto], 1)], 0
        )
        pair_grads[c] = pair_grads[c] * mask
    all_asks = []
    for c in span:
        q = chunks[c]
        keys = jnp.concatenate([q.b_hat, q.k_hat], 0)
        carried = jnp.concatenate([q.carried, q.carried], 0)
        all_asks.append(d_hats[c] * carried + product(pair_grads[c], keys, NN, p["bpair"]))
    all_keys = [
        product(
            pair_grads[c], jnp.concatenate([chunks[c].a_hat, chunks[c].r_hat], 0), TN, p["bpair"]
        )
        for c in span
    ]
    all_ends = [product(right[c], ended[c], NN, p["val"]) for c in span]
    all_vals = [
        product(jnp.concatenate([mats[c][1], mats[c][3]], 0), left[c], TN, p["val"]) for c in span
    ]
    all_vals = [
        all_vals[c] + product(chunks[c].k_end, ended[c], NT, p["val"]) for c in span
    ]
    for c in span:
        rows = pl.ds(c * SPAN, SPAN)
        q, _, _, own_r, own_k, own_v, grad_gate = ready[c]
        end_grad, begin_now = ended[c], begin[c]
        r, lw, k, kn, a = [parts_ref[i, rows].astype(F32) for i in range(5)]
        v = values_ref[rows].astype(F32)
        d_asks, d_keys, d_val = all_asks[c], all_keys[c], all_vals[c]
        d_ends = all_ends[c] * jnp.concatenate([q.final, q.final], 0)
        d_a, d_r = unstacked(d_asks[:n], heads) * q.before, unstacked(d_asks[n:], heads) * q.decay
        d_b = unstacked(d_keys[:n], heads) * q.inverse
        d_k = unstacked(d_keys[n:], heads) * q.inverse
        e_b = unstacked(d_ends[:n], heads) * q.to_end
        e_k = unstacked(d_ends[n:], heads) * q.to_end
        d_v = unstacked(d_val, heads) + own_v
        beta = kn * a
        end_part = e_b * beta + e_k * k
        here = d_r * r - d_b * beta - d_k * k - end_part
        ahead = -d_a * kn
        at_end = jnp.sum(end_part, 0, keepdims=True) + q.whole * q.end * jnp.sum(
            begin_now * end_grad, 0, keepdims=True
        )
        high, low = halves(here)
        high2, low2 = halves(ahead)
        d_lw = at_end + dot(
            jnp.concatenate([later, later, after, after], 1),
            jnp.concatenate([high, low, high2, low2], 0),
            NN,
        )
        d_b = d_b + e_b
        d_k = d_k + e_k + own_k
        d_r = d_r + own_r
        d_kn = d_b * a - d_a
        d_rate = d_b * kn
        g_r, g_lw, g_k, g_kn, g_a, g_v = [
            x.astype(LOW).astype(F32) for x in (d_r, d_lw, d_k, d_kn, d_rate, d_v)
        ]
        key_pre, value_pre, decay_up, rate_up, value_up = [pre_ref[i, rows] for i in range(5)]
        first = firsts[c * SPAN : (c + 1) * SPAN]
        c8, c9, c10, c11, c12 = [cols_ref[i : i + 1] for i in range(3, 8)]
        sig = jax.nn.sigmoid(c8 + decay_up)
        log_decay = -0.6065306597126334 * sig
        g_decay = g_lw * log_decay * (1.0 - sig)
        add(0, g_decay)
        rate = jax.nn.sigmoid(c9 + rate_up)
        g_rate = (g_a + g_k * key_pre * c12) * rate * (1.0 - rate)
        add(1, g_rate)
        g_key = g_k * (1.0 + (rate - 1.0) * c12)
        add(4, g_k * key_pre * (rate - 1.0))
        scaled = key_pre * c11
        norm = lax.rsqrt(head_sum(scaled * scaled, ones) + 1e-06)
        unit = scaled * norm
        g_scaled = norm * (g_kn - unit * head_sum(g_kn * unit, ones))
        g_key = g_key + g_scaled * c11
        add(3, g_scaled * key_pre)
        mix = jax.nn.sigmoid(c10 + value_up)
        g_value = g_v * (1.0 - mix)
        inside = c * SPAN % BLOCK
        buffer[slot, c * SPAN // BLOCK, inside : inside + SPAN] = (g_v * mix).astype(LOW)
        g_vup = g_v * (first - value_pre) * mix * (1.0 - mix)
        add(2, g_vup)
        for i, x in enumerate((g_r, g_key, g_value, g_decay, g_rate, g_vup)):
            grads_ref[i, rows] = x.astype(LOW)
        grads_ref[6, rows] = grad_gate
    col_grad_ref[...] += jnp.concatenate(sums, 0)
    for b in range(2):
        first_copy(slot, b, home_ref[2 * step + b]).start()

    @pl.when(step == 0)
    def _():
        first_done(slot)

        @pl.when(turn > 0)
        def _():
            first_done(1 - slot)


def scan_backward(parts, values, joined, scanned, gate, grad, pre, first, cols, states, mats, home, begins, p):
    _, total, width = parts.shape
    heads = width // HEAD
    rows = BACKWARD_CHUNKS * SPAN
    n = heads * SPAN
    steps = total // rows
    row_spec = pl.BlockSpec((rows, width), lambda i, *_: (steps - 1 - i, 0))
    assert rows == 2 * BLOCK

    def stored(which):
        return pl.BlockSpec(
            (1, BLOCK, width), lambda i, home, b: (home[2 * (steps - 1 - i) + which], 0, 0)
        )

    return pl.pallas_call(
        functools.partial(scan_backward_kernel, heads, p),
        grid_spec=pltpu.PrefetchScalarGridSpec(
            num_scalar_prefetch=2,
            grid=(steps,),
            in_specs=[
                pl.BlockSpec((5, rows, width), lambda i, *_: (0, steps - 1 - i, 0)),
                row_spec,
                row_spec,
                row_spec,
                row_spec,
                stored(0),
                stored(1),
                pl.BlockSpec((5, rows, width), lambda i, *_: (0, steps - 1 - i, 0)),
                stored(0),
                stored(1),
                pl.BlockSpec(cols.shape, lambda i, *_: (0, 0)),
                pl.BlockSpec((BACKWARD_CHUNKS, width, width), lambda i, *_: (steps - 1 - i, 0, 0)),
                pl.BlockSpec((BACKWARD_CHUNKS, 8, n, width), lambda i, *_: (steps - 1 - i, 0, 0, 0)),
            ],
            out_specs=[
                pl.BlockSpec((7, rows, width), lambda i, *_: (0, steps - 1 - i, 0)),
                pl.BlockSpec(memory_space=pl.ANY),
                pl.BlockSpec((8, width), lambda i, *_: (0, 0)),
            ],
            scratch_shapes=[
                pltpu.VMEM((width, width), F32),
                pltpu.VMEM((2, 2, BLOCK, width), LOW),
                pltpu.SemaphoreType.DMA((2, 2)),
            ],
        ),
        out_shape=[
            jax.ShapeDtypeStruct((7, total, width), LOW),
            jax.ShapeDtypeStruct((total // BLOCK, BLOCK, width), LOW),
            jax.ShapeDtypeStruct((8, width), F32),
        ],
        compiler_params=pltpu.CompilerParams(vmem_limit_bytes=60 * 1024 * 1024),
        cost_estimate=work(60),
    )(home, begins, parts, values, joined, scanned, gate, grad, grad, pre, first, first, cols, states, mats)


def norm_rows(x):
    center = x - jnp.mean(x, -1, keepdims=True)
    scale = lax.rsqrt(jnp.mean(center * center, -1, keepdims=True) + 1e-05)
    return center * scale, scale


def keep_rows(rows, first, begins):
    position = first + lax.broadcasted_iota(jnp.int32, (rows, 1), 0)
    hit = position == begins[0]
    for b in begins[1:]:
        hit = hit | (position == b)
    return 1.0 - hit.astype(F32)


def rows_down(x, edge):
    row = lax.broadcasted_iota(jnp.int32, (x.shape[0], 1), 0)
    return jnp.where(row == 0, edge, pltpu.roll(x, 1, 0))


def rows_up(x, edge):
    row = lax.broadcasted_iota(jnp.int32, (x.shape[0], 1), 0)
    return jnp.where(row == x.shape[0] - 1, edge, pltpu.roll(x, x.shape[0] - 1, 0))


def lane_below(limit):
    return lax.broadcasted_iota(jnp.int32, (1, 128), 1) < limit


def kept(x, mask):
    return jnp.where(mask, x, jnp.zeros_like(x))


class SmallWeights:
    def __init__(self, small, up):
        self.pair, self.gate, self.value = small[:, :128], small[:, 128:256], small[:, 256:384]
        self.up_pair, self.up_gate = up[:, 384:512], up[:, 512:640]
        self.up_value = jnp.concatenate([up[:, 320:352], jnp.zeros((up.shape[0], 96), LOW)], 1)


PROJECT_BLOCKS = 4
BACK_BLOCKS = 4


def project_kernel(place_ref, begins_ref, *refs):
    x_refs, refs = refs[:PROJECT_BLOCKS], refs[PROJECT_BLOCKS:]
    cols_ref, own_ref, columns_ref, small_ref, up_ref, ends_ref, stats_ref, parts_ref, gate_ref = refs[:9]
    pre_ref, pair_ref, vm_ref, gs_ref, edge = refs[9:]
    step = pl.program_id(0)

    @pl.when(step == 0)
    def _():
        edge[...] = jnp.zeros_like(edge)

    begins = [begins_ref[i] for i in range(begins_ref.shape[0])]
    for i, ref in enumerate(x_refs):
        ends_ref[i] = jnp.concatenate([ref[0, :16], ref[0, BLOCK - 16 :]], 0)
    x = jnp.concatenate([ref[0] for ref in x_refs], 0).astype(F32)
    rows = x.shape[0]
    mean = jnp.mean(x, -1, keepdims=True)
    center = x - mean
    scale = lax.rsqrt(jnp.mean(center * center, -1, keepdims=True) + 1e-05)
    unit = center * scale
    stats_ref[...] = jnp.concatenate([mean, scale], 1)
    normed = unit * cols_ref[0:1] + cols_ref[1:2]
    moved = rows_down(normed, edge[0:1]) * keep_rows(rows, step * rows, begins)
    edge[0:1] = normed[rows - 1 : rows]
    diff = moved - normed
    mixed = [(normed + diff * cols_ref[i : i + 1]).astype(LOW) for i in range(2, 8)]
    in_r, in_d, in_k, in_v, in_a, in_g = mixed
    low = SmallWeights(small_ref[...], up_ref[...])
    width = own_ref.shape[1]
    recept = dot(in_r, columns_ref[:, :width], NN)
    key_pre = dot(in_k, columns_ref[:, width : 2 * width], NN)
    values = dot(in_v, jnp.concatenate([columns_ref[:, 2 * width :], low.value], 1), NN)
    value_pre = values[:, :width]
    value_mid = kept(values[:, width:], lane_below(DV)).astype(LOW)
    decay, rate = dot(in_d, low.pair, NN), dot(in_a, low.pair, NN)
    pair = jnp.where(lane_below(DECAY_RANK), jnp.tanh(decay), rate)
    pair_low = pair.astype(LOW)
    gate_sig = jax.nn.sigmoid(dot(in_g, low.gate, NN))
    decay_up = dot(kept(pair_low, lane_below(DECAY_RANK)), low.up_pair, NT)
    rate_up = dot(kept(pair_low, ~lane_below(DECAY_RANK)), low.up_pair, NT)
    value_up = dot(value_mid, low.up_value, NT)
    gate_ref[...] = dot(gate_sig.astype(LOW), low.up_gate, NT)
    pair_ref[...] = pair
    vm_ref[...] = value_mid
    gs_ref[...] = gate_sig
    for i, value in enumerate((key_pre, value_pre, decay_up, rate_up, value_up)):
        pre_ref[i] = value
    c8, c9, _, c11, c12 = [own_ref[i : i + 1] for i in range(3, 8)]
    ones = head_ones(recept.shape[1])
    log_decay = -jnp.exp(-jax.nn.softplus(-(c8 + decay_up)) - 0.5)
    rate = jax.nn.sigmoid(c9 + rate_up)
    scaled = key_pre * c11
    key_norm = scaled * lax.rsqrt(head_sum(scaled * scaled, ones) + 1e-06)
    key_main = key_pre * (1.0 + (rate - 1.0) * c12)
    for i, value in enumerate((recept, log_decay, key_main, key_norm, rate)):
        parts_ref[i] = value.astype(LOW)


def block_spec(per, which, rows, width, blocks, back, each, lanes=0):
    def index(i, *tables):
        step = blocks // each - 1 - i if back else i
        stored = tables[0][jnp.maximum(each * step + which, 0)]
        return (stored // per, (stored % per) * (BLOCK // rows) + BLOCK // rows - 1, lanes)

    return pl.BlockSpec((1, rows, width), index)


def whole_spec(array):
    return pl.BlockSpec(array.shape, lambda i, *_: (0,) * array.ndim)


def project(x, cols, own, weights, place, begins, per):
    blocks = place.shape[0]
    total = blocks * BLOCK
    rows = PROJECT_BLOCKS * BLOCK
    width = own.shape[1]
    span = lambda w: pl.BlockSpec((rows, w), lambda i, *_: (i, 0))
    deep = lambda n: pl.BlockSpec((n, rows, width), lambda i, *_: (0, i, 0))
    shape = jax.ShapeDtypeStruct
    return pl.pallas_call(
        project_kernel,
        grid_spec=pltpu.PrefetchScalarGridSpec(
            num_scalar_prefetch=2,
            grid=(blocks // PROJECT_BLOCKS,),
            in_specs=[
                block_spec(per, b, BLOCK, x.shape[2], blocks, False, PROJECT_BLOCKS)
                for b in range(PROJECT_BLOCKS)
            ]
            + [whole_spec(cols), whole_spec(own)]
            + [whole_spec(w) for w in weights],
            out_specs=[
                pl.BlockSpec((PROJECT_BLOCKS, 32, x.shape[2]), lambda i, *_: (i, 0, 0)),
                span(2), deep(5), span(width), deep(5), span(128), span(128), span(128),
            ],
            scratch_shapes=[pltpu.VMEM((8, x.shape[2]), F32)],
        ),
        out_shape=[
            shape((blocks, 32, x.shape[2]), LOW),
            shape((total, 2), F32),
            shape((5, total, width), LOW),
            shape((total, width), F32),
            shape((5, total, width), F32),
            shape((total, 128), F32),
            shape((total, 128), LOW),
            shape((total, 128), F32),
        ],
        compiler_params=pltpu.CompilerParams(vmem_limit_bytes=56 * 1024 * 1024),
        cost_estimate=work(20),
    )(place, begins, *[x] * PROJECT_BLOCKS, cols, own, *weights)


def project_back_kernel(
    part, parts, place_ref, turn_ref, row_ref, begins_ref, head_ref, *refs,
):
    x_refs, refs = refs[:BACK_BLOCKS], refs[BACK_BLOCKS:]
    xp_ref, stats_ref, prior_stats_ref, grads_ref, pair_ref, vm_ref, gs_ref, scan_ref, ffn_ref = refs[:9]
    cols_ref, columns_ref, small_ref, up_ref, *rest = refs[9:]
    sizes_x = len(rest) - 6 - (2 if part == 0 else 1)
    back_refs, rest = rest[:sizes_x], rest[sizes_x:]
    if part == 0:
        low_sum_ref, up_sum_ref, edge, sum_ref, columns_t, small_t, buffer, sems = rest
    else:
        low_sum_ref, edge, sum_ref, columns_t, small_t, buffer, sems = rest
    turn = pl.program_id(0)
    step = pl.num_programs(0) - 1 - turn
    wide = columns_ref.shape[0]

    @pl.when(turn == 0)
    def _():
        for ref in (edge, sum_ref) + ((up_sum_ref,) if part == 0 else ()):
            ref[...] = jnp.zeros_like(ref)
        columns_t[...] = columns_ref[...].T
        small_t[...] = small_ref[:, :384].T

    begins = [begins_ref[i] for i in range(begins_ref.shape[0])]

    x = jnp.concatenate([ref[0] for ref in x_refs], 0).astype(F32)
    unit = (x - stats_ref[:, 0:1]) * stats_ref[:, 1:2]
    rows = unit.shape[0]
    normed = unit * cols_ref[0:1] + cols_ref[1:2]
    last = xp_ref[0].astype(F32)[8:]
    prior = (last - prior_stats_ref[:, 0:1]) * prior_stats_ref[:, 1:2] * cols_ref[0:1] + cols_ref[1:2]
    keep = keep_rows(rows, step * rows, begins)
    diff = rows_down(normed, prior[prior.shape[0] - 1 :]) * keep - normed
    up = up_ref[...]
    up_pair, up_gate = up[:, 384:512], up[:, 512:640]
    up_value = jnp.concatenate([up[:, 320:352], jnp.zeros((up.shape[0], 96), LOW)], 1)
    width = grads_ref.shape[2]
    g_r, g_k, g_v, g_decay, g_rate, g_vup, g_gate = [grads_ref[i] for i in range(7)]
    pair, sig = pair_ref[...], gs_ref[...]
    is_decay = lane_below(DECAY_RANK)
    m_pair = jnp.where(
        is_decay, dot(g_decay, up_pair, NN) * (1.0 - pair * pair), dot(g_rate, up_pair, NN)
    ).astype(LOW)
    m_v = kept(dot(g_vup, up_value, NN), lane_below(DV)).astype(LOW)
    m_g = (dot(g_gate, up_gate, NN) * sig * (1.0 - sig)).astype(LOW)
    near = jnp.zeros_like(unit)
    far = jnp.zeros_like(unit)
    value_weights = jnp.concatenate([columns_t[2 * width :], small_t[256:384]], 0)
    pair_weights = small_t[:128]
    cut = DECAY_RANK + DA + 3 * width
    grads = (
        (2, g_r, columns_t[:width], ((0, g_r),)),
        (3, kept(m_pair, is_decay), pair_weights, ((3 * width, m_pair[:, :DECAY_RANK]),)),
        (4, g_k, columns_t[width : 2 * width], ((width, g_k),)),
        (5, jnp.concatenate([g_v, m_v], 1), value_weights, ((2 * width, g_v), (cut, m_v[:, :DV]))),
        (6, kept(m_pair, ~is_decay), pair_weights, ((3 * width + DECAY_RANK, m_pair[:, DECAY_RANK:]),)),
        (7, m_g, small_t[128:256], ((cut + DV, m_g),)),
    )
    col_sums = []
    for slot, grad, weight, pieces in grads:
        mix = cols_ref[slot : slot + 1]
        mixed = (normed + diff * mix).astype(LOW)
        total = dot(grad, weight, NN)
        for start, piece in pieces:
            sum_ref[start : start + piece.shape[1]] += dot(piece, mixed, TN)
        near = near + total
        far = far + total * mix
        col_sums.append(jnp.sum(total * diff, 0, keepdims=True))
    if part == 0:
        start = 0
        pair_low = pair.astype(LOW)
        for mid, grad in (
            (pair_low[:, :DECAY_RANK], g_decay),
            (pair_low[:, DECAY_RANK:], g_rate),
            (vm_ref[:, :DV], g_vup),
            (sig.astype(LOW), g_gate),
        ):
            up_sum_ref[start : start + mid.shape[1]] += dot(mid, grad, TN)
            start += mid.shape[1]
    moved = far * keep
    back = near - far + rows_up(moved, edge[0:1])
    edge[0:1] = moved[0:1]
    first = [jnp.sum(back * unit, 0, keepdims=True), jnp.sum(back, 0, keepdims=True)]
    sum_ref[sum_ref.shape[0] - 8 :] += jnp.concatenate(first + col_sums, 0)

    slot = turn % 2

    def leave(where):
        for which in range(BACK_BLOCKS):
            pltpu.make_async_copy(
                buffer.at[where, which], back_refs[0].at[0], sems.at[where, which]
            ).wait()

    @pl.when(turn >= 2)
    def _():
        leave(slot)

    buffer[slot] = back.astype(LOW).reshape(BACK_BLOCKS, BLOCK, wide)
    for which in range(BACK_BLOCKS):
        block = BACK_BLOCKS * step + which
        for x, ref in enumerate(back_refs):

            @pl.when(turn_ref[block] == x)
            def _():
                pltpu.make_async_copy(
                    buffer.at[slot, which], ref.at[row_ref[block]], sems.at[slot, which]
                ).start()

    @pl.when(step == 0)
    def _():
        lane = lax.broadcasted_iota(jnp.int32, (1, wide), 1) + part * wide
        spread = jnp.concatenate([scan_ref[...]] * (wide // width), 1)
        spread = jnp.where(lane // width == head_ref[0], spread, 0.0)
        rest_rows = low_sum_ref.shape[0] - sum_ref.shape[0] - 16
        low_sum_ref[...] = jnp.concatenate(
            [sum_ref[...], spread, ffn_ref[...], jnp.zeros((rest_rows, wide), F32)], 0
        ).astype(LOW)
        leave(1 - slot)
        leave(slot)


def project_back(
    part, parts, x, stats, grads, mids, extra_cols, cols, weights, place, turn, row, begins, head, per, sizes
):
    blocks = place.shape[0]
    rows = BACK_BLOCKS * BLOCK
    steps = blocks // BACK_BLOCKS
    wide = x.shape[2] // parts
    width = grads.shape[2]
    size_z, size_x = sizes
    low_rank = DECAY_RANK + DA + DV + 128
    span = lambda w: pl.BlockSpec((rows, w), lambda i, *_: (steps - 1 - i, 0))
    shape = jax.ShapeDtypeStruct
    held = 3 * width + low_rank + 8
    sums = [shape((held + 16 + -(held + 16) % 16, wide), LOW)]
    if part == 0:
        sums.append(shape((low_rank, width), F32))
    columns, small, up = weights
    assert steps > 1
    return pl.pallas_call(
        functools.partial(project_back_kernel, part, parts),
        grid_spec=pltpu.PrefetchScalarGridSpec(
            num_scalar_prefetch=5,
            grid=(steps,),
            in_specs=[
                *[
                    block_spec(per, b, BLOCK, wide, blocks, True, BACK_BLOCKS, part)
                    for b in range(BACK_BLOCKS)
                ],
                block_spec(per, -1, 16, wide, blocks, True, BACK_BLOCKS, part),
                span(2),
                pl.BlockSpec(
                    (8, 2), lambda i, *_: (jnp.maximum((steps - 1 - i) * (rows // 8) - 1, 0), 0)
                ),
                pl.BlockSpec((7, rows, width), lambda i, *_: (0, steps - 1 - i, 0)),
            ]
            + [span(m.shape[1]) for m in mids]
            + [
                whole_spec(extra_cols[0]),
                pl.BlockSpec((8, wide), lambda i, *_: (0, part)),
                pl.BlockSpec((cols.shape[0], wide), lambda i, *_: (0, part)),
                pl.BlockSpec((wide, columns.shape[1]), lambda i, *_: (part, 0)),
                pl.BlockSpec((wide, small.shape[1]), lambda i, *_: (part, 0)),
                whole_spec(up),
            ],
            out_specs=[pl.BlockSpec(memory_space=pl.ANY)] * size_x + [whole_spec(s) for s in sums],
            scratch_shapes=[
                pltpu.VMEM((8, wide), F32),
                pltpu.VMEM((held, wide), F32),
                pltpu.VMEM((columns.shape[1], wide), LOW),
                pltpu.VMEM((384, wide), LOW),
                pltpu.VMEM((2, BACK_BLOCKS, BLOCK, wide), LOW),
                pltpu.SemaphoreType.DMA((2, BACK_BLOCKS)),
            ],
        ),
        out_shape=[shape((size_z * per, BLOCK, wide), LOW)] * size_x + sums,
        compiler_params=pltpu.CompilerParams(vmem_limit_bytes=56 * 1024 * 1024),
        cost_estimate=work(17000),
    )(
        place, turn, row, begins, head, *[x] * (BACK_BLOCKS + 1), stats, stats, grads, *mids, *extra_cols, cols, columns, small, up
    )


TALL = BLOCK + 16


def block_keeps(local_ref, begins_ref, j):
    begins = [begins_ref[i] for i in range(begins_ref.shape[0])]
    first = local_ref[j] * BLOCK
    after = jnp.float32(1.0)
    for b in begins:
        after = jnp.where(first + BLOCK == b, 0.0, after)
    return keep_rows(BLOCK, first, begins), after


def middle_kernel(
    per, local_ref, begins_ref, table_ref, out_ref, tokens_ref, cols_ref, near_ref, far_ref, middle_ref, ffn_ref,
    rows_ref, weight_ref,
):
    count, height, _ = near_ref.shape
    for i in range(2 * count):
        slot = table_ref[i]
        other = lax.rem(slot, count)
        weight_ref[i * height : (i + 1) * height] = jnp.where(slot < count, near_ref[other], far_ref[other])
    heads = out_ref.shape[0]
    rows = [jnp.concatenate([out_ref[h, j] for h in range(heads)], 1) for j in range(per)]
    rows = jnp.concatenate(rows, 0)
    rows_ref[...] = rows
    middle = tokens_ref[...].astype(F32) + dot(rows, weight_ref[...], NN)
    middle_ref[...] = middle
    unit, _ = norm_rows(middle)
    normed = unit * cols_ref[16:17] + cols_ref[17:18]
    c18 = cols_ref[18:19]
    extra_row = lax.broadcasted_iota(jnp.int32, (TALL - BLOCK, 1), 0)
    for j in range(per):
        main = normed[j * TALL : j * TALL + BLOCK]
        extra = normed[j * TALL + BLOCK : (j + 1) * TALL]
        keep, keep_after = block_keeps(local_ref, begins_ref, j)
        moved = rows_down(main, extra[0:1]) * keep
        ffn_ref[j * TALL : j * TALL + BLOCK] = (main + (moved - main) * c18).astype(LOW)
        after = extra + (main[BLOCK - 1 :] * keep_after - extra) * c18
        ffn_ref[j * TALL + BLOCK : (j + 1) * TALL] = jnp.where(extra_row == 1, after, 0.0).astype(LOW)


def middle_rows(out, tokens_ext, near, far, table, cols, local, begins):
    _, per, _, _ = out.shape
    wide = near.shape[2]
    shape = jax.ShapeDtypeStruct
    weight = shape((wide, wide), LOW)
    return pl.pallas_call(
        functools.partial(middle_kernel, per),
        grid_spec=pltpu.PrefetchScalarGridSpec(
            num_scalar_prefetch=3,
            grid=(1,),
            in_specs=[whole_spec(x) for x in (out, tokens_ext, cols, near, far)],
            out_specs=[whole_spec(tokens_ext)] * 3 + [whole_spec(weight)],
        ),
        out_shape=[
            shape((per * TALL, wide), F32),
            shape((per * TALL, wide), LOW),
            shape((per * TALL, wide), LOW),
            weight,
        ],
        compiler_params=pltpu.CompilerParams(vmem_limit_bytes=48 * 1024 * 1024),
        cost_estimate=work(6),
    )(local, begins, table, out, tokens_ext, cols, near, far)


def with_extra(main, extra):
    per = main.shape[0] // BLOCK
    pieces = []
    for j in range(per):
        pieces += [main[j * BLOCK : (j + 1) * BLOCK], extra[j * 16 : (j + 1) * 16]]
    return pieces


def weight_rows_of(ref):
    heads, _, seqs, _, _ = ref.shape
    return jnp.concatenate([ref[h, 0, s] for s in range(seqs) for h in range(heads)], 0)


def channel_kernel(
    xa_ref, xb_ref, ga_ref, gb_ref, ea_ref, eb_ref, key_ref, value_ref, hidden_ref, pre_ref, a_ref, b_ref
):
    rows = xa_ref.shape[0]
    x = jnp.concatenate([xa_ref[...], xb_ref[...]], 0)
    g = jnp.concatenate(with_extra(ga_ref, ea_ref) + with_extra(gb_ref, eb_ref), 0)
    key, value = weight_rows_of(key_ref), weight_rows_of(value_ref)
    active = jnp.maximum(dot(x, key, NN), 0.0)
    hidden_ref[...] = (active * active).astype(LOW)
    grad = (dot(g, value, NN) * 2.0 * active).astype(LOW)
    pre_ref[...] = grad
    back = dot(grad, key, NT)

    @pl.when(pl.program_id(0) == 0)
    def _():
        a_ref[...] = back[:rows]
        b_ref[...] = back[rows:]

    @pl.when(pl.program_id(0) > 0)
    def _():
        a_ref[...] += back[:rows]
        b_ref[...] += back[rows:]


def channel_mix(x, g, extra, weights):
    rows, wide = x[0].shape
    heads, _, seqs, weight_rows, columns = weights.shape
    part = columns // 4

    def weight(which):
        return pl.BlockSpec(
            (heads, 1, seqs, weight_rows, part), lambda i: (0, which, 0, 0, i)
        )

    piece = pl.BlockSpec((2 * rows, part), lambda i: (0, i))
    shape = jax.ShapeDtypeStruct
    return pl.pallas_call(
        channel_kernel,
        grid=(4,),
        in_specs=[whole_spec(a) for a in (*x, *g, *extra)]
        + [weight(0), weight(1)],
        out_specs=[piece, piece, whole_spec(x[0]), whole_spec(x[0])],
        out_shape=[
            shape((2 * rows, columns), LOW),
            shape((2 * rows, columns), LOW),
            shape((rows, wide), F32),
            shape((rows, wide), F32),
        ],
        compiler_params=pltpu.CompilerParams(vmem_limit_bytes=48 * 1024 * 1024),
        cost_estimate=work(8),
    )(*x, *g, *extra, weights, weights)


def main_rows(refs):
    pieces = []
    for ref in refs:
        for start in range(0, ref.shape[0], TALL):
            pieces.append(ref[start : start + BLOCK])
    return jnp.concatenate(pieces, 0)


def channel_grad_kernel(count, *refs):
    og, x = jnp.concatenate([r[...] for r in refs[:count]], 0), main_rows(refs[count : 2 * count])
    hidden, pre = main_rows(refs[2 * count : 2 * count + 2]), main_rows(refs[2 * count + 2 : 2 * count + 4])
    out = refs[2 * count + 4]
    columns = hidden.shape[1]
    out[:, :columns] = dot(og, hidden, TN).astype(LOW)
    out[:, columns : 2 * columns] = dot(x, pre, TN).astype(LOW)


def channel_grads(og, x, hidden, pre, extra):
    wide = og[0].shape[1]
    part = 256
    columns = hidden[0].shape[1]
    return pl.pallas_call(
        functools.partial(channel_grad_kernel, len(og)),
        grid=(wide // part,),
        in_specs=[pl.BlockSpec((a.shape[0], part), lambda i: (0, i)) for a in (*og, *x)]
        + [whole_spec(h) for h in (*hidden, *pre)],
        out_specs=pl.BlockSpec((part, 2 * columns + extra), lambda i: (i, 0)),
        out_shape=jax.ShapeDtypeStruct((wide, 2 * columns + extra), LOW),
        compiler_params=pltpu.CompilerParams(vmem_limit_bytes=48 * 1024 * 1024),
        cost_estimate=work(9),
    )(*og, *x, *hidden, *pre)


def output_grad_kernel(count, *refs):
    rows, grads, out = refs[:count], refs[count : 2 * count], refs[-1]
    left = jnp.concatenate([r[...] for r in rows], 0)
    right = jnp.concatenate([r[...] for r in grads], 0)
    out[...] = dot(left, right, TN).astype(LOW)


def output_grads(rows, grads, room):
    tall, wide = rows[0].shape
    part = grads[0].shape[1]
    last = room.shape[1] // part - 1
    return pl.pallas_call(
        functools.partial(output_grad_kernel, len(rows)),
        grid=(wide // part,),
        in_specs=[pl.BlockSpec((tall, part), lambda i: (0, i))] * len(rows)
        + [whole_spec(g) for g in grads]
        + [pl.BlockSpec(memory_space=pl.ANY)],
        out_specs=pl.BlockSpec((part, part), lambda i: (i, last)),
        out_shape=jax.ShapeDtypeStruct(room.shape, LOW),
        input_output_aliases={2 * len(rows): 0},
        compiler_params=pltpu.CompilerParams(vmem_limit_bytes=48 * 1024 * 1024),
        cost_estimate=work(2),
    )(*rows, *grads, room)


def middle_back_kernel(
    per, local_ref, begins_ref, near_ref, core_ref, far_ref, middle_ref, og_ref, weight_ref, cols_ref,
    grad_ref, low_ref, heads_ref, sums_ref,
):
    c16, c17, c18 = [cols_ref[i : i + 1] for i in (16, 17, 18)]
    grad_in = near_ref[...] + core_ref[...] + far_ref[...].astype(F32)
    sums = [jnp.zeros((1, c16.shape[1]), F32) for _ in range(3)]
    lows = []
    for j in range(per):
        start = j * TALL
        grad, after = grad_in[start : start + BLOCK], grad_in[start + BLOCK + 1 : start + BLOCK + 2]
        keep, keep_after = block_keeps(local_ref, begins_ref, j)
        ahead = rows_up(grad * keep, after * keep_after)
        grad_normed = grad + (ahead - grad) * c18
        unit, scale = norm_rows(middle_ref[start : start + BLOCK])
        prior, _ = norm_rows(middle_ref[start + BLOCK : start + TALL])
        normed = unit * c16 + c17
        diff = rows_down(normed, prior[0:1] * c16 + c17) * keep - normed
        for i, value in enumerate((grad_normed * unit, grad_normed, grad * diff)):
            sums[i] = sums[i] + jnp.sum(value, 0, keepdims=True)
        og = og_ref[j * BLOCK : (j + 1) * BLOCK].astype(F32)
        total = og + norm_back(grad_normed, unit, scale, c16)
        grad_ref[j * BLOCK : (j + 1) * BLOCK] = total
        lows.append(total.astype(LOW))
        quarter = low_ref.shape[2]
        for s in range(low_ref.shape[0]):
            low_ref[s, start : start + BLOCK] = lows[-1][:, s * quarter : (s + 1) * quarter]
            low_ref[s, start + BLOCK : start + TALL] = jnp.zeros((TALL - BLOCK, quarter), LOW)
    sums_ref[...] = jnp.concatenate(sums + [jnp.zeros((5, c16.shape[1]), F32)], 0)
    out = dot(jnp.concatenate(lows, 0), weight_ref[...], NT).astype(LOW)
    width = heads_ref.shape[2]
    for h in range(heads_ref.shape[0]):
        heads_ref[h] = out[:, h * width : (h + 1) * width]


def norm_back(grad, unit, scale, gain):
    grad = grad * gain
    return scale * (
        grad - jnp.mean(grad, -1, keepdims=True) - unit * jnp.mean(grad * unit, -1, keepdims=True)
    )


def middle_back(near, core, far, middle, og, weight, cols, local, begins, heads, seqs):
    tall, wide = near.shape
    per = tall // TALL
    shape = jax.ShapeDtypeStruct
    outs = [
        shape((per * BLOCK, wide), F32),
        shape((seqs, tall, wide // seqs), LOW),
        shape((heads, per * BLOCK, wide // heads), LOW),
        shape((8, wide), F32),
    ]
    operands = (near, core, far, middle, og, weight, cols)
    return pl.pallas_call(
        functools.partial(middle_back_kernel, per),
        grid_spec=pltpu.PrefetchScalarGridSpec(
            num_scalar_prefetch=2,
            grid=(1,),
            in_specs=[whole_spec(x) for x in operands],
            out_specs=[whole_spec(x) for x in outs],
        ),
        out_shape=outs,
        compiler_params=pltpu.CompilerParams(vmem_limit_bytes=48 * 1024 * 1024),
        cost_estimate=work(8),
    )(local, begins, *operands)


HEAD_AXES = ("hz", "hx")


def all_gather(x, axes):
    return lax.all_gather(x, axes, axis=0, tiled=True)


def steps_along(x, axis):
    size = lax.axis_size(axis)
    return [lax.ppermute(x, axis, [(i, i ^ k) for i in range(size)]) for k in range(1, size)]


def grown(x, axis):
    return jnp.concatenate([x] + steps_along(x, axis), 0)


def order_table(axes):
    strides, stride = {}, 1
    for axis in axes:
        strides[axis] = stride
        stride *= lax.axis_size(axis)
    index = jnp.arange(stride, dtype=jnp.int32)
    place, below = jnp.zeros((), jnp.int32), stride
    for axis in ("ys", "core") + HEAD_AXES:
        if axis in axes:
            below //= lax.axis_size(axis)
            there = (index // below) % lax.axis_size(axis)
            place = place + (there ^ lax.axis_index(axis)) * strides[axis]
    return place


def in_order(x, axes):
    x = taken_blocks(x, order_table(axes))
    return x.reshape((x.shape[0] * x.shape[1],) + x.shape[2:])


def swap(x, axis):
    return lax.ppermute(x, axis, [(0, 1), (1, 0)])


def seq_gather(x):
    if lax.axis_size("ys") != 2:
        return list(lax.all_gather(x, ("ys", "core"), axis=0))
    far = swap(x, "ys")
    return [x, swap(x, "core"), far, swap(far, "core")]


def seq_return(near, core, far, diagonal):
    return swap(core, "core"), swap((far + swap(diagonal, "core")).astype(LOW), "ys")


def seq_step(x, axis):
    if lax.axis_size("ys") != 2:
        if axis == "ys":
            return x
        return lax.psum_scatter(x, ("ys", "core"), scatter_dimension=0, tiled=True)[0].astype(F32)
    if axis == "ys":
        x = x.reshape((2, 2) + x.shape[1:])
    index = lax.axis_index(axis)
    sent = swap(lax.dynamic_index_in_dim(x, 1 - index, 0, keepdims=False).astype(LOW), axis)
    return lax.dynamic_index_in_dim(x, index, 0, keepdims=False).astype(F32) + sent.astype(F32)


def taken_blocks(x, table):
    return x.at[table].get(mode="promise_in_bounds")


def start_flags(positions, begins):
    return jnp.any(positions[..., None] == begins, -1).astype(F32)


def body(
    tokens,
    leading_layer_value,
    output_gradient,
    lengths,
    sequence_block_of,
    stored_block_of,
    channel_settings,
    receptance_matrix,
    key_matrix,
    value_matrix,
    output_matrix,
    branch_down_weight,
    branch_up_weight,
    channel_key_weight,
    channel_value_weight,
):
    rows_here, wide = tokens.shape
    per = rows_here // BLOCK
    ys, heads_axis = lax.axis_size("ys"), lax.axis_size("hz") * lax.axis_size("hx")
    seqs = 2 * ys
    head = lax.axis_index(HEAD_AXES)
    core = lax.axis_index("core")
    width = wide // heads_axis
    weight_rows = receptance_matrix.shape[0]
    low_rank = branch_down_weight.shape[1]
    order, home = sequence_block_of[0], stored_block_of[0]
    blocks = order.shape[0]
    begins = (jnp.cumsum(lengths[0]) - lengths[0]).astype(jnp.int32)
    splits = (DECAY_RANK, DECAY_RANK + DA, DECAY_RANK + DA + DV)

    og_first = output_gradient.reshape(per, BLOCK, wide)[:, 0]
    place = home
    out_table = order_table(HEAD_AXES + ("ys", "core"))
    size_z, size_x = lax.axis_size("hz"), lax.axis_size("hx")
    apart = (home // per) ^ head
    turn_x, turn_row = apart % size_x, (apart // size_x) * per + home % per
    local = lax.dynamic_slice_in_dim(order, head * per, per)
    group = all_gather(tokens[None], HEAD_AXES)
    og_rows = in_order(grown(grown(og_first[None], "hz"), "hx"), HEAD_AXES)
    og_parts = seq_gather(output_gradient)

    quarter = channel_key_weight.shape[1] // seqs
    pair = jnp.stack([channel_key_weight, channel_value_weight], 0).reshape(2, weight_rows, seqs, quarter)
    pair = lax.all_to_all(
        pair.transpose(2, 0, 1, 3), ("ys", "core"), split_axis=0, concat_axis=0, tiled=True
    )
    columns = (
        jnp.stack([receptance_matrix, key_matrix, value_matrix], 1)
        .reshape(weight_rows * 3, heads_axis, width)
        .transpose(1, 0, 2)
    )
    columns = lax.all_to_all(columns, HEAD_AXES, split_axis=0, concat_axis=0, tiled=True)
    def rank_columns(weight):
        return jnp.split(weight, (DECAY_RANK + DA, DECAY_RANK + DA + DV), 1)

    (down_pair, down_value, down_gate), (up_pair, up_value, up_gate) = [
        rank_columns(w) for w in (branch_down_weight, branch_up_weight)
    ]
    count = channel_settings.shape[1]
    blank = [jnp.zeros((weight_rows, n), LOW) for n in (32 - count, 32)]
    small = jnp.concatenate(
        [
            down_pair, down_gate, down_value, channel_settings, blank[0], up_value, blank[1],
            up_pair, up_gate,
        ],
        1,
    )[None]
    for axis in HEAD_AXES + ("ys", "core"):
        small = grown(small, axis)
    small = in_order(small, HEAD_AXES + ("ys", "core"))
    columns = columns.reshape(1, heads_axis * weight_rows, 3 * width)
    columns = in_order(grown(grown(columns, "ys"), "core"), ("ys", "core"))
    settings = small[:, 256 + DV : 256 + DV + count].astype(F32).T
    up = lax.dynamic_slice_in_dim(small, head * width, width, 0)
    own = lax.dynamic_slice_in_dim(settings, head * width, width, 1)
    own = jnp.concatenate([own[13:16], own[8:13]], 0)
    out_shards = grown(grown(output_matrix[None], "hz"), "hx")
    columns, small, settings, up, own, og_parts, pair, first_sent, out_shards = (
        lax.optimization_barrier(
            (
                columns, small, settings, up, own, og_parts, pair, leading_layer_value, out_shards,
            )
        )
    )
    first_group = lax.all_to_all(
        first_sent.reshape(rows_here, heads_axis, width).transpose(1, 0, 2),
        HEAD_AXES, split_axis=0, concat_axis=0, tiled=True,
    ).reshape(blocks, BLOCK, width)
    weights = [columns, small, up]

    out_shards = grown(out_shards, "ys")

    def gathered(half):
        return all_gather(half[None], HEAD_AXES).transpose(1, 0, 2, 3)

    whole_quarter = quarter == wide
    if whole_quarter:
        every = all_gather(pair.transpose(1, 0, 2, 3).reshape(1, -1, weight_rows, wide), HEAD_AXES)
    else:
        every = (gathered(pair[:, 0]), gathered(pair[:, 1]))

    ends, stats, parts, gate, pre, *mids = project(group, settings, own, weights, place, begins, per)
    parts, out_shards = lax.optimization_barrier((parts, out_shards))
    far_shards = swap(out_shards, "core")
    values, out_in, joined, scanned, states, mats = scan_forward(
        parts, pre, first_group, gate, own, home, begins, PASSES
    )

    before, follow = jnp.maximum(order - 1, 0), jnp.minimum(order + 1, blocks - 1)
    in_blocks = out_in.reshape(blocks, BLOCK, width)
    extended = jnp.concatenate(
        [
            taken_blocks(in_blocks, order),
            taken_blocks(in_blocks[:, BLOCK - 1], before)[:, None],
            taken_blocks(in_blocks[:, 0], follow)[:, None],
            jnp.zeros((blocks, 14, width), LOW),
        ],
        1,
    )
    extended, far_shards, ends, og_rows = lax.optimization_barrier((extended, far_shards, ends, og_rows))
    out_ext = lax.all_to_all(
        extended.reshape(heads_axis, per, TALL, width), HEAD_AXES, split_axis=0, concat_axis=0, tiled=True
    )
    local = lax.dynamic_slice_in_dim(order, head * per, per)
    after_seq = local + 1
    after_live = (after_seq < blocks).astype(LOW)[:, None]
    after = jnp.minimum(after_seq, blocks - 1)
    row_before = taken_blocks(ends, jnp.maximum(local - 1, 0))[:, 31]
    row_after = taken_blocks(ends, after)[:, 0]
    og_after = taken_blocks(og_rows, taken_blocks(home, after)) * after_live
    none = jnp.zeros((per, 14, wide), LOW)
    extra_parts = seq_gather(jnp.concatenate([none[:, :1], og_after[:, None], none], 1).reshape(-1, wide))
    tokens_b = tokens.reshape(per, BLOCK, wide)
    tokens_ext = jnp.concatenate([tokens_b, row_before[:, None], row_after[:, None], none], 1)
    if weight_rows % 16:
        ordered = in_order(jnp.concatenate([out_shards, far_shards], 0), HEAD_AXES + ("ys", "core"))
        out_shards, far_shards = ordered.reshape(2, -1, 32, wide)
        out_table = jnp.arange(2 * out_shards.shape[0], dtype=jnp.int32)
    middle, ffn_in, out_rows, out_weight = middle_rows(
        out_ext, tokens_ext.reshape(-1, wide), out_shards, far_shards, out_table, settings, local, begins
    )
    ffn_in, every = lax.optimization_barrier((ffn_in, every))
    if whole_quarter:
        every = every.reshape(heads_axis, 2, seqs, weight_rows, wide)
        value_part = every[:, 1].transpose(1, 0, 2, 3).reshape(wide, wide)
        ffn_parts = [ffn_in, swap(ffn_in, "core"), swap(ffn_in, "ys")]
        *near, own_part, core_part = channel_mix(ffn_parts[:2], og_parts[:2], extra_parts[:2], every)
        ffn_parts[2], near, own_part, core_part, out_rows = lax.optimization_barrier(
            (ffn_parts[2], near, own_part, core_part, out_rows)
        )
        ffn_parts.append(swap(ffn_parts[2], "core"))
        *far, far_part, diagonal = channel_mix(ffn_parts[2:], og_parts[2:], extra_parts[2:], every)
        came_core, came_far = seq_return(own_part, core_part, far_part, diagonal)
        grads_here = channel_grads(
            og_parts, ffn_parts, (near[0], far[0]), (near[1], far[1]), wide // seqs
        )
        came_far, grads_here = lax.optimization_barrier((came_far, grads_here))
        hidden = [near[0], far[0]]
    else:
        key_part, value_part = [x.reshape(wide, quarter) for x in every]
        ffn_parts = seq_gather(ffn_in)
        rows = jnp.concatenate(ffn_parts, 0)
        og_rows = jnp.concatenate(
            [
                jnp.concatenate([g.reshape(per, BLOCK, wide), x.reshape(per, 16, wide)], 1).reshape(-1, wide)
                for g, x in zip(og_parts, extra_parts)
            ],
            0,
        )
        active = jax.nn.relu(dot(rows, key_part, NN))
        hidden = [(active * active).astype(LOW)]
        grad_pre = (dot(og_rows, value_part, NN) * 2.0 * active).astype(LOW)
        own_part = dot(grad_pre, key_part, NT).reshape(seqs, per * TALL, wide)
        own_part = lax.psum_scatter(own_part, ("ys", "core"), scatter_dimension=0, tiled=True)[0]
        came_core, came_far = jnp.zeros_like(own_part), jnp.zeros_like(ffn_in)
        is_main = (jnp.arange(rows.shape[0]) % TALL < BLOCK).astype(LOW)[:, None]
        grads_here = [dot(og_rows * is_main, hidden[0], TN), dot(rows * is_main, grad_pre, TN)]
    grad_middle, middle_low, grad_out, cols_ffn = middle_back(
        own_part, came_core, came_far, middle, output_gradient, out_weight, settings, local, begins, heads_axis,
        seqs,
    )
    grad_heads = lax.all_to_all(grad_out, HEAD_AXES, split_axis=0, concat_axis=0, tiled=True)
    out_parts = seq_gather(out_rows)
    which = lax.axis_index(("ys", "core"))
    if whole_quarter:

        def quarter_from(k):
            sent = lax.dynamic_index_in_dim(middle_low, which ^ k, 0, keepdims=False)
            return lax.ppermute(sent, ("ys", "core"), [(i, i ^ k) for i in range(seqs)])

        low_parts = [lax.dynamic_index_in_dim(middle_low, which, 0, keepdims=False)]
        low_parts += [quarter_from(k) for k in (1, 2, 3)]
        grads_here = output_grads(out_parts, low_parts, grads_here)
    else:
        right = lax.all_to_all(middle_low, ("ys", "core"), split_axis=0, concat_axis=0, tiled=True)
        grads_here.append(dot(jnp.concatenate(out_parts, 0), right.reshape(-1, right.shape[2]), TN))
        grads_here = jnp.concatenate(grads_here, 1).astype(LOW)
    grad_heads, grads_here = lax.optimization_barrier((grad_heads, grads_here))
    grads_here = lax.psum_scatter(grads_here, HEAD_AXES, scatter_dimension=0, tiled=True)

    scan_grads, first_grad, cols_scan = scan_backward(
        parts, values, joined, scanned, gate, grad_heads.reshape(blocks, BLOCK, width), pre, first_group,
        own, states, mats, home, begins, PASSES,
    )
    first_came = lax.all_to_all(
        first_grad.reshape(heads_axis, rows_here, width), HEAD_AXES, split_axis=0, concat_axis=0, tiled=True
    )

    share = wide // seqs
    thin = low_rank // seqs
    fold = heads_axis // seqs

    cut = 3 * width
    end = cut + low_rank

    def over_ys(left, right, up_sums):
        up_sums = up_sums.astype(LOW).reshape(seqs, thin, width)
        if ys != 2:
            rows_out = jnp.concatenate([left, right], 1)
            by_feature = jnp.concatenate([rows_out[:cut], rows_out[end:]], 0)
            by_feature = by_feature.reshape(-1, seqs, share).transpose(1, 0, 2)
            return by_feature, rows_out[cut:end].reshape(seqs, thin, wide), up_sums
        index = lax.axis_index("ys")

        def part_of(which):
            half = jnp.where(which == 0, left, right)
            rank = [lax.dynamic_slice_in_dim(x, cut + which * 2 * thin, 2 * thin, 0) for x in (left, right)]
            return jnp.concatenate([half[:cut], half[end:]] + rank, 0)

        total = part_of(index).astype(F32) + swap(part_of(1 - index), "ys").astype(F32)
        features = total.shape[0] - 4 * thin
        by_rank = total[features:].reshape(2, 2, thin, -1).transpose(1, 2, 0, 3)
        return total[:features].reshape(-1, 2, share), by_rank, seq_step(up_sums, "ys")

    def over_core(by_feature, by_rank, up_sums):
        if ys != 2:
            return [
                lax.psum_scatter(x, ("ys", "core"), scatter_dimension=0, tiled=True)[0].astype(F32)
                for x in (by_feature, by_rank, up_sums)
            ]

        def step(x, dim):
            sent = lax.dynamic_index_in_dim(x, 1 - core, dim, keepdims=False).astype(LOW)
            return lax.dynamic_index_in_dim(x, core, dim, keepdims=False) + swap(sent, "core").astype(F32)

        return step(by_feature, 1), step(by_rank, 0).reshape(thin, wide), step(up_sums, 0)

    def to_owners(by_feature, by_rank):
        rows_low = by_feature.astype(LOW)
        squares = rows_low[:cut].reshape(cut, fold, width)
        mixed = by_rank.astype(LOW).reshape(thin, heads_axis, width).transpose(1, 0, 2)
        cols_part = rows_low[cut:][:count].reshape(count, heads_axis, -1)
        cols_part = jnp.pad(
            cols_part.transpose(1, 0, 2), ((0, 0), (0, -count % 8), (0, width - cols_part.shape[2]))
        )
        mixed = lax.all_to_all(
            jnp.concatenate([mixed, cols_part], 1), HEAD_AXES, split_axis=0, concat_axis=0, tiled=True
        )
        came = []
        for k in range(fold):
            sent = lax.dynamic_index_in_dim(squares, (head + k) % fold, 1, keepdims=False)
            came.append(
                lax.ppermute(
                    sent, every_axis, [(q * heads_axis + h, owner(q, h, (h + k) % fold)) for q, h in pairs]
                )
            )
        return mixed, came

    every_axis = ("ys", "core") + HEAD_AXES
    pairs = [(q, h) for q in range(seqs) for h in range(heads_axis)]

    def owner(q, h, j):
        return (h // fold) * heads_axis + q * fold + j

    sizes = (size_z, size_x)

    def others_x(blocks_back):
        return [
            lax.ppermute(blocks_back[k], "hx", [(i, i ^ k) for i in range(size_x)])
            for k in range(1, size_x)
        ]

    def after_x(kept_blocks, came):
        total = kept_blocks.astype(F32)
        for x in came:
            total = total + x.astype(F32)
        total = total.reshape(size_z, rows_here, -1)
        return total[0], [total[k].astype(LOW) for k in range(1, size_z)]

    def others_z(sent):
        return [
            lax.ppermute(x, "hz", [(i, i ^ k) for i in range(size_z)]) for k, x in enumerate(sent, 1)
        ]

    def half_back(part, grads):
        outs = project_back(
            part, 2, group, stats, grads, mids, (cols_scan, cols_ffn), settings, weights, place, turn_x, turn_row,
            begins, head[None], per, sizes,
        )
        return outs[:size_x], outs[size_x:]

    left_blocks, (left_sum, up_sums) = half_back(0, scan_grads)
    left_came = others_x(left_blocks)
    scan_grads, left_sum, first_came = lax.optimization_barrier((scan_grads, left_sum, first_came))
    right_blocks, (right_sum,) = half_back(1, scan_grads)
    right_blocks, left_came = lax.optimization_barrier((right_blocks, left_came))
    right_came = others_x(right_blocks)
    left_own, left_sent = after_x(left_blocks[0], left_came)
    left_sent, right_sum, hidden = lax.optimization_barrier((left_sent, right_sum, hidden))
    left_z = others_z(left_sent)
    sums = over_ys(left_sum, right_sum, up_sums)
    outs = [dot(h, value_part, NT) for h in hidden]
    right_came, outs, grads_here = lax.optimization_barrier((right_came, outs, grads_here))
    right_own, right_sent = after_x(right_blocks[0], right_came)
    right_sent, left_z, sums, outs = lax.optimization_barrier((right_sent, left_z, sums, outs))
    right_z = others_z(right_sent)
    by_feature, by_rank, up_sums = over_core(*sums)
    right_z[0], by_feature, by_rank = lax.optimization_barrier((right_z[0], by_feature, by_rank))
    mixed, came = to_owners(by_feature, by_rank)
    if whole_quarter:
        came_core, came_far = seq_return(*[x for out in outs for x in jnp.split(out, 2, 0)])
        right_z, came_core, came_far = lax.optimization_barrier((right_z, came_core, came_far))
    right_z[0], first_came = lax.optimization_barrier((right_z[0], first_came))
    first_value_grad = first_came.transpose(1, 0, 2).reshape(rows_here, wide).astype(F32)
    right_z, up_sums, mixed, came = lax.optimization_barrier((right_z, up_sums, mixed, came))
    back = jnp.concatenate(
        [own + sum(x.astype(F32) for x in z) for own, z in ((left_own, left_z), (right_own, right_z))], 1
    )
    value_sum, key_sum, out_sum = jnp.split(grads_here.astype(F32), (quarter, 2 * quarter), 1)

    unit, scale = norm_rows(tokens.astype(F32))
    tokens_grad = grad_middle + norm_back(back, unit, scale, settings[0])
    mixed = jnp.sum(mixed.astype(F32), 0)
    channel_grad = mixed[thin : thin + count, :weight_rows].T
    down_grad = mixed[:thin].T

    def main_of(x):
        return x.reshape(-1, per, TALL, wide)[:, :, :BLOCK].reshape(-1, rows_here, wide)

    layer_out = main_of(middle)[0]
    if whole_quarter:
        own_out = jnp.split(outs[0], 2, 0)[0]
        layer_out = layer_out + main_of(own_out)[0] + main_of(came_core)[0] + main_of(came_far)[0].astype(F32)
    else:
        layer_out = layer_out + lax.psum_scatter(
            main_of(outs[0]), ("ys", "core"), scatter_dimension=0, tiled=True
        )[0]
    came = jnp.stack(came, 0)
    came = taken_blocks(came, (head - jnp.arange(fold, dtype=jnp.int32)) % fold)
    came = came.reshape(fold, 3, width, width).transpose(1, 3, 0, 2).reshape(3, width, share)
    recept_grad, key_grad, value_grad = [came[i].astype(F32) for i in range(3)]
    up_grad = up_sums.T
    return (
        layer_out.astype(LOW),
        tokens_grad,
        first_value_grad,
        channel_grad,
        recept_grad,
        key_grad,
        value_grad,
        out_sum,
        down_grad,
        up_grad,
        key_sum,
        value_sum,
    )


def solution(mesh):
    seqs, heads = mesh.devices.shape
    split = Mesh(mesh.devices.reshape(seqs // 2, 2, 4, heads // 4), ("ys", "core") + HEAD_AXES)
    rows = P(("ys", "core") + HEAD_AXES, None)
    table = P(("ys", "core"), None)
    square = P(HEAD_AXES, ("ys", "core"))
    return jax.shard_map(
        body,
        mesh=split,
        in_specs=(rows,) * 3 + (table,) * 3 + (rows,) * 9,
        out_specs=(rows,) * 4 + (square,) * 8,
        check_vma=False,
    )
```
